32 devices in a mesh: grp: 4 (over y, core), cache: 8 (over z, x).
Axes of the slice: x: 2, y: 2, z: 4, core: 2. Of those that a mesh axis runs over, the one named last changes fastest.
Arguments:
- queries: bfloat16 [128, 4, 8192], P(('grp', 'cache')), may hold values from -6 to 6
- new_kv: bfloat16 [128, 4, 2048], P(('grp', 'cache')), may hold values from -6 to 6
- kv_cache: bfloat16 [512, 128, 2048], P(('grp', 'cache')), may hold values from -6 to 6
- page_owner: int32 [128, 4], P(('grp', 'cache')), may hold values from 0 to 7, all different within a row; in each aligned block of 4 rows (0 to 3, 4 to 7, ...) at most 4 rows name the same one
- page_index: int32 [128, 4, 1], P(('grp', 'cache')), may hold values from 0 to 15
- lengths: int32 [128], P(('grp', 'cache')), may hold values from 1 to 512, as said below
Outputs:
- attention_out: bfloat16 [128, 4, 8192], P(('grp', 'cache'))
The draws below stay inside these ranges and needn't reach their ends.
Inputs may be any that keep to these rules, and one draw needn't show every extreme that they name: `page_owner`: each row names 4 different owners; among the 4 rows held by one device no owner is named by more than 4 rows, and in every draw some owner is named by exactly 4 rows of some device. `lengths`: some request has exactly 512 valid tokens in every draw.
All inputs are finite; a program needn't handle non-finite values.
Results may differ from the reference program's by a relative error of at most 0.0051.
Values may be sent and summed in bfloat16 or wider, within the bound.
No kernel may reach another device: no remote copies, remote signals or barrier semaphores. Data moves between devices by JAX's collectives and lax.ppermute only.
A program may use at most 192 MiB of HBM per device.

```python
import math
import jax
import jax.numpy as jnp
import numpy as np
from jax import lax

H = 64
KVH = 8
HD = 128
GQ = 8
STEPS = 4
PAGE = 128
SEL = 4
PPO = 1
RG = 1
P_DEV = 16
R_DEV = 4
REQS = 128
CACHE_PAGES = 512
CAP = 4
MAXLEN = 512
N_GRP = 4
N_CACHE = 8


def draw_queries(key, part):
    key = jax.random.fold_in(key, 11)
    entries = 2.0 * jax.random.truncated_normal(key, -3.0, 3.0, (REQS, STEPS, H, HD), jnp.float32)
    return entries.reshape(REQS, STEPS, H * HD).astype(jnp.bfloat16)


def draw_new_kv(key, part):
    key = jax.random.fold_in(key, 23)
    entries = jax.random.truncated_normal(key, -6.0, 6.0, (REQS, STEPS, 2, KVH, HD), jnp.float32)
    return entries.reshape(REQS, STEPS, 2 * KVH * HD).astype(jnp.bfloat16)


def draw_kv_cache(key, part):
    key = jax.random.fold_in(key, 41)
    entries = jax.random.truncated_normal(key, -6.0, 6.0, (CACHE_PAGES, PAGE, 2, KVH, HD), jnp.float32)
    return entries.reshape(CACHE_PAGES, PAGE, 2 * KVH * HD).astype(jnp.bfloat16)


def draw_lengths(key, part):
    key = jax.random.fold_in(key, 37)
    drawn = jax.random.randint(key, (REQS,), 1, MAXLEN + 1, dtype=jnp.int32)
    return drawn.at[0].set(MAXLEN)


def place_ends(values, rng, smallest, high):
    extent = values.shape
    place = [jax.random.randint(jax.random.fold_in(rng, axis), (), 0, extent[axis]) for axis in range(len(extent))]
    values = values.at[tuple(place)].set(smallest)
    longest = extent.index(max(extent))
    place[longest] = (place[longest] + 1) % extent[longest]
    return values.at[tuple(place)].set(high)


def deal_out(own_key, own, number, rows, count, top, most, slope):
    order = jax.random.permutation(own_key, count)
    crowded, common = load_shares(count, rows * top, most, slope, True), load_shares(count, rows * top, most, slope, False)
    places = jnp.arange(count)

    def named(tallies, rotation):
        used = int((tallies > 0).sum())
        fixed = max(1, used // 4)
        moved = fixed + (places - fixed + rotation * (used - fixed)) % max(1, count - fixed)
        return jnp.zeros((count,), jnp.int32).at[order[jnp.where(places < fixed, places, moved)]].set(jnp.asarray(tallies, jnp.int32))

    tallies = jnp.where(number % 4 == 0, named(crowded, number // 4), named(common, number - number // 4 - 1))
    mixed = jax.random.permutation(jax.random.fold_in(own, 3), count)
    donor, taker = mixed[0:count // 2 * 2:2], mixed[1:count // 2 * 2:2]
    slack = jnp.minimum(tallies[donor] - 1, most - tallies[taker]) // 2
    slack = jnp.where((donor == order[0]) | (taker == order[0]) | (tallies[taker] == 0), 0, jnp.maximum(slack, 0))
    moved = jax.random.randint(jax.random.fold_in(own, 4), (count // 2,), 0, 1 << 20) % (slack + 1)
    tallies = tallies.at[donor].add(-moved).at[taker].add(moved)
    items = jnp.searchsorted(jnp.cumsum(tallies), jnp.arange(rows * top), side="right").astype(jnp.int32)
    grid = items.reshape(top, rows).T
    grid = grid[jax.random.permutation(jax.random.fold_in(own, 1), rows)]
    rotation = jax.random.randint(jax.random.fold_in(own, 2), (rows, 1), 0, top)
    return jnp.take_along_axis(grid, (jnp.arange(top)[None, :] + rotation) % top, axis=1)


def load_shares(number_of, total, most, lean, full):
    weights = [(1 << 20) // math.isqrt(standing ** lean) + 1 for standing in range(1, number_of + 1)]
    largest = most if full else min(most, max(-(-total // number_of), total * weights[0] // sum(weights)))
    least = 1 if total - largest >= number_of - 1 else 0
    holding, surplus = [largest] + [least] * (number_of - 1), total - largest - least * (number_of - 1)
    while surplus > 0:
        movable = [i for i in range(1, number_of) if holding[i] < largest] or [i for i in range(1, number_of) if holding[i] < most]
        mass, budget = sum([weights[i] for i in movable]), surplus
        for i in movable:
            addition = min(most - holding[i], max(1, budget * weights[i] // mass), surplus)
            holding[i] = holding[i] + addition
            surplus = surplus - addition
    return np.array(holding)


def setup_inputs(seed: int = 0) -> dict:
    streams_of = jax.random.split(jax.random.key(seed), 7)
    queries = draw_queries(jax.random.fold_in(streams_of[6], 71), 0)
    new_kv = draw_new_kv(jax.random.fold_in(streams_of[6], 71), 0)
    kv_cache = draw_kv_cache(jax.random.fold_in(streams_of[6], 71), 0)
    page_owner_keys = jax.random.split(jax.random.fold_in(streams_of[3], 1), REQS // R_DEV)
    page_owner_turns = jax.random.permutation(jax.random.fold_in(streams_of[3], 3), REQS // R_DEV)
    page_owner = jax.vmap(lambda own, number: deal_out(jax.random.fold_in(streams_of[3], 2), own, number, R_DEV, N_CACHE, SEL, CAP, 2))(page_owner_keys, page_owner_turns).reshape((REQS, SEL))
    page_index = place_ends(jax.random.randint(streams_of[4], (REQS, SEL, PPO), 0, P_DEV), jax.random.fold_in(streams_of[4], 1), 0, P_DEV - 1).astype(jnp.int32)
    lengths = draw_lengths(jax.random.fold_in(streams_of[6], 71), 0)
    return dict(queries=queries, new_kv=new_kv, kv_cache=kv_cache, page_owner=page_owner, page_index=page_index, lengths=lengths)


neg_fill = -1e+30

def item_partial(query_row, panel_rows, valid_count):
    token_count = panel_rows.shape[0]
    query_heads = query_row.reshape(STEPS, KVH, GQ, HD).astype(jnp.float32)
    key_rows = panel_rows[:, :KVH * HD].reshape(token_count, KVH, HD).astype(jnp.float32)
    value_rows = panel_rows[:, KVH * HD:].reshape(token_count, KVH, HD).astype(jnp.float32)
    scores = jnp.einsum('tkgd,ukd->tkgu', query_heads, key_rows) * (1.0 / math.sqrt(HD))
    usable = jnp.arange(token_count, dtype=jnp.int32) < valid_count
    scores = jnp.where(usable, scores, neg_fill)
    highest = lax.optimization_barrier(jnp.max(scores, axis=-1))
    weights = jnp.where(usable, jnp.exp(scores - highest[..., None]), 0.0)
    weight_sum = lax.optimization_barrier(jnp.sum(weights, axis=-1))
    rounded = lax.optimization_barrier(weights.astype(jnp.bfloat16)).astype(jnp.float32)
    mixture = jnp.einsum('tkgu,ukd->tkgd', rounded, value_rows)
    normed = (mixture / jnp.maximum(weight_sum, 1.0)[..., None]).astype(jnp.bfloat16)
    return (normed.reshape(STEPS, KVH * GQ * HD), highest.reshape(STEPS, KVH * GQ), weight_sum.reshape(STEPS, KVH * GQ))

def new_partial(query_row, new_row):
    query_heads = query_row.reshape(STEPS, KVH, GQ, HD).astype(jnp.float32)
    key_rows = new_row[:, :KVH * HD].reshape(STEPS, KVH, HD).astype(jnp.float32)
    value_rows = new_row[:, KVH * HD:].reshape(STEPS, KVH, HD).astype(jnp.float32)
    scores = jnp.einsum('tkgd,ukd->tkgu', query_heads, key_rows) * (1.0 / math.sqrt(HD))
    causal = (jnp.arange(STEPS)[:, None] >= jnp.arange(STEPS)[None, :])[:, None, None, :]
    scores = jnp.where(causal, scores, neg_fill)
    highest = lax.optimization_barrier(jnp.max(scores, axis=-1))
    weights = jnp.where(causal, jnp.exp(scores - highest[..., None]), 0.0)
    weight_sum = lax.optimization_barrier(jnp.sum(weights, axis=-1))
    rounded = lax.optimization_barrier(weights.astype(jnp.bfloat16)).astype(jnp.float32)
    mixture = jnp.einsum('tkgu,ukd->tkgd', rounded, value_rows)
    return (mixture.reshape(STEPS, KVH * GQ, HD), highest.reshape(STEPS, KVH * GQ), weight_sum.reshape(STEPS, KVH * GQ))

def merge_parts(item_out, item_top, item_sum, new_mix, new_top, new_sum):
    peak_score = jnp.maximum(new_top, lax.optimization_barrier(jnp.max(item_top, axis=0)))
    item_weight = jnp.exp(item_top - peak_score[None]) * item_sum
    new_weight = jnp.exp(new_top - peak_score)
    item_values = lax.optimization_barrier(item_out).astype(jnp.float32).reshape(SEL, STEPS, KVH * GQ, HD)
    numerator = lax.optimization_barrier(jnp.sum(item_weight[..., None] * item_values, axis=0)) + new_weight[..., None] * new_mix
    denominator = lax.optimization_barrier(jnp.sum(item_weight, axis=0)) + new_weight * new_sum
    return (numerator / denominator[..., None]).astype(jnp.bfloat16).reshape(STEPS, KVH * GQ * HD)

def reference(queries, new_kv, kv_cache, page_owner, page_index, lengths):

    def home_order(table):
        trailing = table.shape[1:]
        grid_view = table.reshape((N_GRP, N_CACHE, N_GRP, RG) + trailing)
        return jnp.swapaxes(grid_view, 0, 2).reshape((REQS,) + trailing)
    owners = home_order(page_owner)
    page_ids = home_order(page_index)
    valid_len = home_order(lengths)
    group_ids = jnp.arange(REQS, dtype=jnp.int32) // RG % N_GRP
    page_rows = ((group_ids[:, None] * N_CACHE + owners)[:, :, None] * P_DEV + page_ids).astype(jnp.int32)
    item_span = PPO * PAGE
    starts = jnp.arange(SEL, dtype=jnp.int32) * item_span
    valid_counts = jnp.clip(valid_len[:, None] - starts[None, :], 0, item_span).astype(jnp.int32)

    def one_request(query_row, new_row, row_ids, counts):
        panel_rows = kv_cache[row_ids.reshape(-1)].reshape(SEL, item_span, kv_cache.shape[2])
        item_out, item_top, item_sum = jax.vmap(item_partial, in_axes=(None, 0, 0))(query_row, panel_rows, counts)
        new_mix, new_top, new_sum = new_partial(query_row, new_row)
        return merge_parts(item_out, item_top, item_sum, new_mix, new_top, new_sum)

    def one_block(packed):
        block_queries, block_new, block_rows, block_counts = packed
        return jax.vmap(one_request)(block_queries, block_new, block_rows, block_counts)
    block_count = REQS // N_GRP
    packed = (queries.reshape(block_count, N_GRP, STEPS, -1), new_kv.reshape(block_count, N_GRP, STEPS, -1), page_rows.reshape(block_count, N_GRP, SEL, PPO), valid_counts.reshape(block_count, N_GRP, SEL))
    outputs = lax.map(one_block, packed)
    return outputs.reshape(REQS, STEPS, -1)
```

```python
import functools
import math

import jax
import jax.numpy as jnp
from jax import lax
from jax.experimental import pallas as pl
from jax.experimental.pallas import tpu as pltpu
from jax.sharding import PartitionSpec as P

KVH = 8
HD = 128
GQ = 8
STEPS = 4
PAGE = 128
SEL = 4

LANES = 128
ROWS = GQ * STEPS
HALF = 16
BODY = KVH * ROWS
FULL = BODY + HALF
PIECE = 32
COLS = KVH * ROWS // HALF
EMPTY = -1e30
SCALE = math.log2(math.e) / math.sqrt(HD)
VMEM_BYTES = 24 * 1024 * 1024


def params():
    return pltpu.CompilerParams(vmem_limit_bytes=VMEM_BYTES)


def cost(flops, moved):
    return pl.CostEstimate(flops=flops, bytes_accessed=moved, transcendentals=0)


def lane_ids():
    return lax.broadcasted_iota(jnp.int32, (HALF, LANES), 1)


def pack_stats(stats):
    stats = jnp.where(lane_ids() < COLS, stats, 0.0)
    high = stats.astype(jnp.bfloat16).astype(jnp.float32)
    rest = stats - high
    middle = rest.astype(jnp.bfloat16).astype(jnp.float32)
    low = rest - middle
    tile = high + pltpu.roll(middle, PIECE, 1) + pltpu.roll(low, 2 * PIECE, 1)
    return tile.astype(jnp.bfloat16)


def unpack_stats(tile):
    tile = tile.astype(jnp.float32)
    return tile + pltpu.roll(tile, LANES - PIECE, 1) + pltpu.roll(tile, LANES - 2 * PIECE, 1)


def column(stats, index):
    return stats[:, index : index + 1]


def tile_rows(index):
    half, head = divmod(index, KVH)
    start = head * ROWS + half * HALF
    return slice(start, start + HALF)


def relayout_kernel(place_ref, queries_ref, *refs):
    outs, scratch = refs[:-1], refs[-1]
    per = outs[0].shape[0]
    for d, out in enumerate(outs):
        for k in range(per):
            row = (place_ref[0] ^ d) * per + k
            values = queries_ref[row].astype(jnp.float32)
            for head in range(KVH * GQ):
                scratch[head * STEPS : (head + 1) * STEPS, :] = values[:, head * HD : (head + 1) * HD]
            out[k] = scratch[...].astype(jnp.bfloat16)


def relayout(place, queries, groups):
    per = queries.shape[0] // groups
    whole = pl.BlockSpec(memory_space=pltpu.VMEM)
    return pl.pallas_call(
        relayout_kernel,
        out_shape=[jax.ShapeDtypeStruct((per, BODY, HD), jnp.bfloat16)] * groups,
        in_specs=[pl.BlockSpec(memory_space=pltpu.SMEM), whole],
        out_specs=[whole] * groups,
        scratch_shapes=[pltpu.VMEM((BODY, HD), jnp.float32)],
        compiler_params=params(),
        cost_estimate=cost(0, 2 * queries.size * 2),
    )(place, queries)


def new_kernel(groups, place_ref, *refs):
    queries, (new_ref, out_ref, stats_ref) = refs[:groups], refs[groups:]
    per = queries[0].shape[0]
    for d in range(groups):
        for k in range(per):
            row = (place_ref[0] ^ d) * per + k
            new = new_ref[row].astype(jnp.float32)
            step = lax.broadcasted_iota(jnp.int32, (ROWS, STEPS), 0) % STEPS
            usable = lax.broadcasted_iota(jnp.int32, (ROWS, STEPS), 1) <= step
            stats = jnp.full((HALF, LANES), EMPTY, jnp.float32)
            lanes = lane_ids()
            for head in range(KVH):
                rows = slice(head * ROWS, (head + 1) * ROWS)
                keys = new[:, head * HD : (head + 1) * HD].astype(jnp.bfloat16)
                values = new[:, (KVH + head) * HD : (KVH + head + 1) * HD].astype(jnp.bfloat16)
                scores = lax.dot_general(
                    queries[d][k, rows, :], keys, (((1,), (1,)), ((), ())), preferred_element_type=jnp.float32
                )
                scores = jnp.where(usable, scores * SCALE, EMPTY)
                top = jnp.max(scores, axis=1, keepdims=True)
                weights = jnp.exp2(scores - top)
                total = jnp.sum(weights, axis=1, keepdims=True)
                mixed = lax.dot_general(
                    weights.astype(jnp.bfloat16), values, (((1,), (0,)), ((), ())), preferred_element_type=jnp.float32
                )
                out_ref[d * per + k, rows, :] = mixed / total
                level = jnp.broadcast_to(top + jnp.log2(total), (ROWS, LANES))
                for half in range(ROWS // HALF):
                    part = level[half * HALF : (half + 1) * HALF, :]
                    stats = jnp.where(lanes == half * KVH + head, part, stats)
            stats_ref[d * per + k] = stats


def new_tokens(place, queries, new_kv):
    groups = len(queries)
    requests = new_kv.shape[0]
    whole = pl.BlockSpec(memory_space=pltpu.VMEM)
    return pl.pallas_call(
        functools.partial(new_kernel, groups),
        out_shape=[
            jax.ShapeDtypeStruct((requests, BODY, HD), jnp.float32),
            jax.ShapeDtypeStruct((requests, HALF, LANES), jnp.float32),
        ],
        in_specs=[pl.BlockSpec(memory_space=pltpu.SMEM)] + [whole] * (groups + 1),
        out_specs=[whole, whole],
        compiler_params=params(),
        cost_estimate=cost(requests * KVH * 4 * ROWS * HD * HD, requests * BODY * HD * 6),
    )(place, *queries, new_kv)


def item_kernel(sides, slots, entries, meta_ref, *refs):
    queries = refs[:sides]
    pages = refs[sides : sides + len(entries)]
    outs = refs[sides + len(entries) :]
    lanes = lane_ids()
    tokens = lax.broadcasted_iota(jnp.int32, (ROWS, PAGE), 1)
    for number, (side, slot, entry) in enumerate(entries):
        count = meta_ref[2 * entry]
        query, page, out = queries[side], pages[number], outs[side]

        @pl.when(count > 0)
        def _():
            stats = jnp.full((HALF, LANES), EMPTY, jnp.float32)
            for head in range(KVH):
                rows = slice(head * ROWS, (head + 1) * ROWS)
                scores = lax.dot_general(
                    query[slot, rows, :],
                    page[0, :, head * HD : (head + 1) * HD],
                    (((1,), (1,)), ((), ())),
                    preferred_element_type=jnp.float32,
                )
                scores = jnp.where(tokens < count, scores * SCALE, EMPTY)
                top = jnp.max(scores, axis=1, keepdims=True)
                weights = jnp.exp2(scores - top)
                total = jnp.sum(weights, axis=1, keepdims=True)
                mixed = lax.dot_general(
                    weights.astype(jnp.bfloat16),
                    page[0, :, (KVH + head) * HD : (KVH + head + 1) * HD],
                    (((1,), (0,)), ((), ())),
                    preferred_element_type=jnp.float32,
                )
                out[slot, rows, :] = (mixed / total).astype(jnp.bfloat16)
                level = jnp.broadcast_to(top + jnp.log2(total), (ROWS, LANES))
                for half in range(ROWS // HALF):
                    part = level[half * HALF : (half + 1) * HALF, :]
                    stats = jnp.where(lanes == half * KVH + head, part, stats)
            out[slot, BODY:FULL, :] = pack_stats(stats)

        @pl.when(count <= 0)
        def _():
            out[slot, :BODY, :] = jnp.zeros((BODY, HD), jnp.bfloat16)
            out[slot, BODY:FULL, :] = pack_stats(jnp.full((HALF, LANES), EMPTY, jnp.float32))


def page_map(entry):
    return lambda i, meta: (meta[2 * entry + 1], 0, 0)


def items(meta, queries, entries_of, kv_cache):
    entries = [(side, slot, e) for side, row in enumerate(entries_of) for slot, e in enumerate(row)]
    slots = [q.shape[0] for q in queries]

    def whole(count, rows):
        return pl.BlockSpec((count, rows, HD), lambda i, meta: (0, 0, 0))

    page_spec = [pl.BlockSpec((1, PAGE, kv_cache.shape[2]), page_map(e)) for _, _, e in entries]
    return pl.pallas_call(
        functools.partial(item_kernel, len(queries), slots, entries),
        out_shape=[jax.ShapeDtypeStruct((n, FULL, HD), jnp.bfloat16) for n in slots],
        grid_spec=pltpu.PrefetchScalarGridSpec(
            num_scalar_prefetch=1,
            grid=(1,),
            in_specs=[whole(n, BODY) for n in slots] + page_spec,
            out_specs=[whole(n, FULL) for n in slots],
        ),
        compiler_params=params(),
        cost_estimate=cost(len(entries) * KVH * 4 * ROWS * HD * PAGE, len(entries) * PAGE * kv_cache.shape[2] * 2),
    )(meta, *queries, *([kv_cache] * len(entries)))


def blend(sources, out, slot_out):
    levels = [unpack_stats(ref[slot, BODY:FULL, :]) for ref, slot in sources]
    peak = functools.reduce(jnp.maximum, levels)
    shares = [jnp.exp2(level - peak) for level in levels]
    total = functools.reduce(jnp.add, shares)
    shares = [share / total for share in shares]
    out[slot_out, BODY:FULL, :] = pack_stats(peak + jnp.log2(total))
    for index in range(COLS):
        rows = tile_rows(index)
        parts = [
            column(share, index) * ref[slot, rows, :].astype(jnp.float32)
            for share, (ref, slot) in zip(shares, sources)
        ]
        out[slot_out, rows, :] = functools.reduce(jnp.add, parts).astype(jnp.bfloat16)


def merge_kernel(plans, inputs, *refs):
    ins, outs = refs[:inputs], refs[inputs:]
    for out, plan in zip(outs, plans):
        for slot_out, sources in enumerate(plan):
            if len(sources) == 1:
                number, slot = sources[0]
                out[slot_out] = ins[number][slot]
            else:
                blend([(ins[number], slot) for number, slot in sources], out, slot_out)


def merge(arrays, plans):
    whole = pl.BlockSpec(memory_space=pltpu.VMEM)
    count = sum(len(plan) for plan in plans)
    return pl.pallas_call(
        functools.partial(merge_kernel, plans, len(arrays)),
        out_shape=[jax.ShapeDtypeStruct((len(plan), FULL, HD), jnp.bfloat16) for plan in plans],
        in_specs=[whole] * len(arrays),
        out_specs=[whole] * len(plans),
        compiler_params=params(),
        cost_estimate=cost(0, count * FULL * HD * 6),
    )(*arrays)


def final_kernel(groups, place_ref, *refs):
    parts, (new_ref, level_ref, out_ref, scratch) = refs[:groups], refs[groups:]
    per = parts[0].shape[0]
    for d in range(groups):
        for k in range(per):
            row = (place_ref[0] ^ d) * per + k
            cached = unpack_stats(parts[d][k, BODY:FULL, :])
            fresh = level_ref[d * per + k]
            peak = jnp.maximum(cached, fresh)
            share, share_new = jnp.exp2(cached - peak), jnp.exp2(fresh - peak)
            total = share + share_new
            share, share_new = share / total, share_new / total
            for index in range(COLS):
                rows = tile_rows(index)
                scratch[rows, :] = (
                    column(share, index) * parts[d][k, rows, :].astype(jnp.float32)
                    + column(share_new, index) * new_ref[d * per + k, rows, :]
                )
            for head in range(KVH * GQ):
                out_ref[row, :, head * HD : (head + 1) * HD] = scratch[
                    head * STEPS : (head + 1) * STEPS, :
                ].astype(jnp.bfloat16)


def final(place, parts, new_out, new_level):
    groups = len(parts)
    requests = new_out.shape[0]
    whole = pl.BlockSpec(memory_space=pltpu.VMEM)
    return pl.pallas_call(
        functools.partial(final_kernel, groups),
        out_shape=jax.ShapeDtypeStruct((requests, STEPS, KVH * GQ * HD), jnp.bfloat16),
        in_specs=[pl.BlockSpec(memory_space=pltpu.SMEM)] + [whole] * (groups + 2),
        out_specs=whole,
        scratch_shapes=[pltpu.VMEM((BODY, HD), jnp.float32)],
        compiler_params=params(),
        cost_estimate=cost(0, requests * BODY * HD * 8),
    )(place, *parts, new_out, new_level)


def ring_order(owners):
    return list(range(0, owners, 2)) + list(range(owners - 1, 0, -2))


def per_device(queries, new_kv, kv_cache, page_owner, page_index, lengths):
    groups = lax.axis_size("grp")
    owners = lax.axis_size("cache")
    requests = queries.shape[0]
    per = requests // groups
    reach = owners // 2
    order = ring_order(owners)
    here = [0] * owners
    for position, owner in enumerate(order):
        here[owner] = position
    forward = [(order[i], order[(i + 1) % owners]) for i in range(owners)]
    backward = [(b, a) for a, b in forward]

    group = lax.axis_index("grp")
    position = jnp.asarray(here, jnp.int32)[lax.axis_index("cache")]
    place = jnp.reshape(group, (1,)).astype(jnp.int32)

    visitor = (group ^ jnp.arange(groups, dtype=jnp.int32))[:, None] * per + jnp.arange(per, dtype=jnp.int32)
    visitor = visitor.reshape(-1)
    counts = jnp.clip(lengths[:, None] - jnp.arange(SEL, dtype=jnp.int32) * PAGE, 0, PAGE)
    named = (page_owner[None] == jnp.arange(owners, dtype=jnp.int32)[:, None, None]).astype(jnp.int32)
    sent = jnp.stack([jnp.sum(named * counts[None], -1), jnp.sum(named * page_index[None, :, :, 0], -1)], -1)
    sent = sent[:, visitor]
    got = lax.all_to_all(sent, "cache", split_axis=0, concat_axis=0, tiled=True)
    ring = jnp.asarray(order, jnp.int32)[(position + jnp.arange(owners, dtype=jnp.int32)) % owners]
    meta = got[ring].reshape(-1)

    rows = relayout(place, queries, groups)
    visits = [rows[0]]
    for d in range(1, groups):
        swap = [(g, g ^ d) for g in range(groups)]
        visits.append(lax.ppermute(rows[d], "grp", swap))
    new_out, new_level = new_tokens(place, rows, new_kv)

    chunks = [list(range(0, groups // 2)), list(range(groups // 2, groups))]
    returned = [None] * groups
    states = []
    for chunk in chunks:
        block = jnp.concatenate([visits[d] for d in chunk], axis=0)
        slots = [d * per + k for d in chunk for k in range(per)]
        cut = (len(slots) + 1) // 2
        ahead = behind = block
        parts = {}
        parts[0] = items(meta, [block], [[s for s in slots]], kv_cache)[0]
        for step in range(1, reach + 1):
            if step == reach:
                ahead, behind = ahead[:cut], behind[cut:]
            ahead = lax.ppermute(ahead, "cache", forward)
            behind = lax.ppermute(behind, "cache", backward)
            below = (owners - step) * requests
            above = step * requests
            if step < reach:
                entries = [[below + s for s in slots], [above + s for s in slots]]
            else:
                entries = [[below + s for s in slots[:cut]], [above + s for s in slots[cut:]]]
            from_below, from_above = items(meta, [ahead, behind], entries, kv_cache)
            parts[-step], parts[step] = from_below, from_above
        states.append((chunk, slots, cut, parts))

    for chunk, slots, cut, parts in reversed(states):
        count = len(slots)
        ahead, behind = parts[-reach], parts[reach]
        for step in range(reach - 1, -1, -1):
            ahead = lax.ppermute(ahead, "cache", forward)
            behind = lax.ppermute(behind, "cache", backward)
            first = step == reach - 1
            if step > 0:
                up, down = [], []
                for s in range(count):
                    low, high = first and s >= cut, first and s < cut
                    up.append([(1, s)] if low else [(0, s), (1, s)])
                    down.append([(3, s)] if high else [(2, s - cut if first else s), (3, s)])
                ahead, behind = merge([ahead, parts[step], behind, parts[-step]], [up, down])
            else:
                plans = []
                for number in range(len(chunk)):
                    plan = []
                    for k in range(per):
                        s = number * per + k
                        sources = [(2, s)]
                        if not (first and s >= cut):
                            sources.append((0, s))
                        if not (first and s < cut):
                            sources.append((1, s - cut if first else s))
                        plan.append(sources)
                    plans.append(plan)
                merged = merge([ahead, behind, parts[0]], plans)
                for d, part in zip(chunk, merged):
                    returned[d] = part

    home = [returned[0]]
    for d in range(1, groups):
        swap = [(g, g ^ d) for g in range(groups)]
        home.append(lax.ppermute(returned[d], "grp", swap))
    return final(place, home, new_out, new_level)


def solution(mesh):
    in_specs = (
        P(("grp", "cache"), None, None),
        P(("grp", "cache"), None, None),
        P(("grp", "cache"), None, None),
        P(("grp", "cache"), None),
        P(("grp", "cache"), None, None),
        P(("grp", "cache")),
    )
    out_specs = P(("grp", "cache"), None, None)
    return jax.shard_map(
        per_device, mesh=mesh, in_specs=in_specs, out_specs=out_specs, check_vma=False
    )
```

```python
import functools
import math

import jax
import jax.numpy as jnp
from jax import lax
from jax.experimental import pallas as pl
from jax.experimental.pallas import tpu as pltpu
from jax.sharding import PartitionSpec as P

KVH = 8
HD = 128
GQ = 8
STEPS = 4
PAGE = 128
SEL = 4

LANES = 128
ROWS = GQ * STEPS
HALF = 16
BODY = KVH * ROWS
COLS = BODY // HALF
SECOND = 3 * COLS
PAIR = 2 * BODY + HALF
LONE = BODY + HALF
EMPTY = -1e30
SCALE = math.log2(math.e) / math.sqrt(HD)
VMEM_BYTES = 24 * 1024 * 1024
BF16 = jnp.bfloat16
F32 = jnp.float32
IN_VMEM = pl.BlockSpec(memory_space=pltpu.VMEM)
IN_SMEM = pl.BlockSpec(memory_space=pltpu.SMEM)


def params():
    return pltpu.CompilerParams(vmem_limit_bytes=VMEM_BYTES)


def cost(flops, moved):
    return pl.CostEstimate(flops=flops, bytes_accessed=moved, transcendentals=0)


def list_rows(requests):
    return -(-2 * requests // HALF) * HALF


def lane_ids(rows=HALF):
    return lax.broadcasted_iota(jnp.int32, (rows, LANES), 1)


def pack_stats(stats):
    lanes = lane_ids()
    used = (lanes < COLS) | ((lanes >= SECOND) & (lanes < SECOND + COLS))
    stats = jnp.where(used, stats, 0.0)
    high = stats.astype(BF16).astype(F32)
    rest = stats - high
    middle = rest.astype(BF16).astype(F32)
    low = rest - middle
    return (high + pltpu.roll(middle, COLS, 1) + pltpu.roll(low, 2 * COLS, 1)).astype(BF16)


def unpack_stats(tile):
    tile = tile.astype(F32)
    return tile + pltpu.roll(tile, LANES - COLS, 1) + pltpu.roll(tile, LANES - 2 * COLS, 1)


def tile_start(index):
    half, head = divmod(index, KVH)
    return head * ROWS + half * HALF


def by_lane(columns):
    lanes = lane_ids()
    tile = jnp.zeros((HALF, LANES), F32)
    for head, values in enumerate(columns):
        for half in range(ROWS // HALF):
            part = values[half * HALF : (half + 1) * HALF, :]
            tile = jnp.where(lanes == half * KVH + head, part, tile)
    return tile


def attend(queries, keys, values, usable):
    across = (((1,), (1,)), ((), ()))
    along = (((1,), (0,)), ((), ()))
    scores = [lax.dot_general(q, k, across, preferred_element_type=F32) for q, k in zip(queries, keys)]
    scores = [jnp.where(usable, s * SCALE, EMPTY) for s in scores]
    tops = [jnp.max(s, axis=1, keepdims=True) for s in scores]
    weights = [jnp.exp2(s - t) for s, t in zip(scores, tops)]
    totals = [jnp.sum(w, axis=1, keepdims=True) for w in weights]
    mixed = [lax.dot_general(w.astype(BF16), v, along, preferred_element_type=F32) for w, v in zip(weights, values)]
    level = by_lane(tops) + jnp.log2(jnp.maximum(by_lane(totals), 1.0))
    return [m / t for m, t in zip(mixed, totals)], level


def relayout_kernel(place_ref, queries_ref, *outs):
    for d, out in enumerate(outs):
        values = queries_ref[place_ref[0] ^ d].astype(F32)
        for head in range(KVH):
            first = head * GQ
            parts = [values[:, (first + g) * HD : (first + g + 1) * HD] for g in range(GQ)]
            out[head * ROWS : (head + 1) * ROWS, :] = jnp.concatenate(parts, axis=0).astype(BF16)


def relayout(place, queries):
    groups = queries.shape[0]
    return pl.pallas_call(
        relayout_kernel,
        out_shape=[jax.ShapeDtypeStruct((BODY, HD), BF16)] * groups,
        in_specs=[IN_SMEM, IN_VMEM],
        out_specs=[IN_VMEM] * groups,
        compiler_params=params(),
        cost_estimate=cost(0, 4 * queries.size),
    )(place, queries)


def new_kernel(place_ref, *refs):
    queries, (new_ref, out_ref, level_ref) = refs[:-3], refs[-3:]
    step = lax.broadcasted_iota(jnp.int32, (ROWS, STEPS), 0) % STEPS
    usable = lax.broadcasted_iota(jnp.int32, (ROWS, STEPS), 1) <= step
    for d, query in enumerate(queries):
        new = new_ref[place_ref[0] ^ d]
        heads = [new[:, head * HD : (head + 1) * HD] for head in range(2 * KVH)]
        rows = [query[head * ROWS : (head + 1) * ROWS, :] for head in range(KVH)]
        mixed, level = attend(rows, heads[:KVH], heads[KVH:], usable)
        for head, values in enumerate(mixed):
            out_ref[d, head * ROWS : (head + 1) * ROWS, :] = values
        level_ref[d] = level


def new_tokens(place, queries, new_kv):
    groups = len(queries)
    return pl.pallas_call(
        new_kernel,
        out_shape=[
            jax.ShapeDtypeStruct((groups, BODY, HD), F32),
            jax.ShapeDtypeStruct((groups, HALF, LANES), F32),
        ],
        in_specs=[IN_SMEM] + [IN_VMEM] * (groups + 1),
        out_specs=[IN_VMEM, IN_VMEM],
        compiler_params=params(),
        cost_estimate=cost(groups * KVH * 4 * ROWS * HD * HD, groups * BODY * HD * 6),
    )(place, *queries, new_kv)


def payload_kernel(place_ref, owner_ref, index_ref, length_ref, *refs):
    visits, out = refs[:-1], refs[-1]
    cut = len(visits) // 2
    lists = list_rows(len(visits))
    rows = lax.broadcasted_iota(jnp.int32, (lists, LANES), 0)
    lanes = lane_ids(lists)
    tile = jnp.zeros((lists, LANES), F32)
    for d, visit in enumerate(visits):
        start = d * BODY + (lists if d >= cut else 0)
        out[start : start + BODY, :] = visit[...]
        row = place_ref[0] ^ d
        for s in range(SEL):
            count = jnp.clip(length_ref[row] - s * PAGE, 0, PAGE).astype(F32)
            mine = lanes == owner_ref[row, s]
            tile = jnp.where(mine & (rows == 2 * d), count, tile)
            tile = jnp.where(mine & (rows == 2 * d + 1), index_ref[row, s].astype(F32), tile)
    out[cut * BODY : cut * BODY + lists, :] = tile.astype(BF16)


def payload(place, page_owner, page_index, lengths, visits):
    groups = len(visits)
    rows = groups * BODY + list_rows(groups)
    return pl.pallas_call(
        payload_kernel,
        out_shape=jax.ShapeDtypeStruct((rows, HD), BF16),
        in_specs=[IN_SMEM] * 4 + [IN_VMEM] * groups,
        out_specs=IN_VMEM,
        compiler_params=params(),
        cost_estimate=cost(0, 4 * rows * HD),
    )(place, page_owner, page_index, lengths, *visits)


def item_kernel(slots, list_start, first, gap_at, lists, place_ref, query_ref, cache_ref, out_ref, level_ref, code_ref):
    owner = place_ref[1]
    table = query_ref[list_start : list_start + lists, :].astype(F32)
    rows = lax.broadcasted_iota(jnp.int32, (lists, LANES), 0)
    table = jnp.where(lane_ids(lists) == owner, table, 0.0)
    for entry, slot in enumerate(slots):
        code = jnp.where(rows == 2 * slot, table, jnp.where(rows == 2 * slot + 1, table * 256.0, 0.0))
        code_ref[entry] = jnp.sum(code).astype(jnp.int32)
    tokens = lax.broadcasted_iota(jnp.int32, (ROWS, PAGE), 1)

    @pl.loop(0, len(slots))
    def _(entry):
        code = code_ref[entry]
        count, page = code & 255, code >> 8
        start = first + entry * BODY + jnp.where(entry >= gap_at, lists, 0)
        out = (entry // 2) * PAIR + (entry % 2) * BODY

        @pl.when(count > 0)
        def _():
            queries = [query_ref[pl.ds(pl.multiple_of(start + h * ROWS, HALF), ROWS), :] for h in range(KVH)]
            keys = [cache_ref[page, :, h * HD : (h + 1) * HD] for h in range(KVH)]
            values = [cache_ref[page, :, (KVH + h) * HD : (KVH + h + 1) * HD] for h in range(KVH)]
            mixed, level = attend(queries, keys, values, tokens < count)
            for head, part in enumerate(mixed):
                out_ref[pl.ds(pl.multiple_of(out + head * ROWS, HALF), ROWS), :] = part.astype(BF16)
            level_ref[entry] = level

        @pl.when(count <= 0)
        def _():
            out_ref[pl.ds(pl.multiple_of(out, HALF), BODY), :] = jnp.zeros((BODY, HD), BF16)
            level_ref[entry] = jnp.full((HALF, LANES), EMPTY, F32)

    lanes = lane_ids()
    for pair in range(len(slots) // 2):
        level = jnp.where(lanes < COLS, level_ref[2 * pair], pltpu.roll(level_ref[2 * pair + 1], SECOND, 1))
        start = pair * PAIR + 2 * BODY
        out_ref[start : start + HALF, :] = pack_stats(level)


def items(place, queries, kv_cache, requests, slots):
    lists = list_rows(requests)
    cut = requests // 2
    if len(slots) == requests:
        list_start, first, gap_at = cut * BODY, 0, cut
    elif slots[0] == 0:
        list_start, first, gap_at = cut * BODY, 0, requests
    else:
        list_start, first, gap_at = 0, lists, requests
    count = len(slots)
    out_rows = count // 2 * PAIR
    return pl.pallas_call(
        functools.partial(item_kernel, slots, list_start, first, gap_at, lists),
        out_shape=jax.ShapeDtypeStruct((out_rows, HD), BF16),
        in_specs=[IN_SMEM, IN_VMEM, IN_VMEM],
        out_specs=IN_VMEM,
        scratch_shapes=[pltpu.VMEM((count, HALF, LANES), F32), pltpu.SMEM((count,), jnp.int32)],
        compiler_params=params(),
        cost_estimate=cost(count * KVH * 4 * ROWS * HD * PAGE, count * PAGE * kv_cache.shape[2] * 2),
    )(place, queries, kv_cache)


def blend(levels):
    peak = functools.reduce(jnp.maximum, levels)
    shares = [jnp.exp2(level - peak) for level in levels]
    total = functools.reduce(jnp.add, shares)
    return [share / total for share in shares], peak + jnp.log2(total)


def mix(shares, refs, start, first_lane):
    values = []
    for index in range(COLS):
        row, lane = start + tile_start(index), first_lane + index
        parts = [share[:, lane : lane + 1] * ref[row : row + HALF, :].astype(F32) for share, ref in zip(shares, refs)]
        values.append(functools.reduce(jnp.add, parts))
    return values


def merge_kernel(base, arrived_ref, own_ref, out_ref):
    pairs = out_ref.shape[0] // PAIR
    arrived_pairs = arrived_ref.shape[0] // PAIR
    for pair in range(pairs):
        start = pair * PAIR
        if not base <= pair < base + arrived_pairs:
            out_ref[start : start + PAIR, :] = own_ref[start : start + PAIR, :]
            continue
        arrived = arrived_ref.at[(pair - base) * PAIR : (pair - base + 1) * PAIR]
        own = own_ref.at[start : start + PAIR]
        out = out_ref.at[start : start + PAIR]
        levels = [unpack_stats(ref[2 * BODY : PAIR, :]) for ref in (arrived, own)]
        shares, level = blend(levels)
        values = [mix(shares, (arrived, own), second * BODY, second * SECOND) for second in range(2)]
        for second in range(2):
            for index in range(COLS):
                row = second * BODY + tile_start(index)
                out[row : row + HALF, :] = values[second][index].astype(BF16)
        out[2 * BODY : PAIR, :] = pack_stats(level)


def merge(arrived, own, base):
    return pl.pallas_call(
        functools.partial(merge_kernel, base),
        out_shape=jax.ShapeDtypeStruct(own.shape, BF16),
        in_specs=[IN_VMEM, IN_VMEM],
        out_specs=IN_VMEM,
        compiler_params=params(),
        cost_estimate=cost(0, 6 * own.size),
    )(arrived, own)


def gather_kernel(ahead_base, behind_base, ahead_ref, behind_ref, own_ref, *outs):
    for pair in range(len(outs) // 2):
        sources = [own_ref.at[pair * PAIR : (pair + 1) * PAIR]]
        for ref, base in ((ahead_ref, ahead_base), (behind_ref, behind_base)):
            if base <= pair < base + ref.shape[0] // PAIR:
                sources.append(ref.at[(pair - base) * PAIR : (pair - base + 1) * PAIR])
        shares, level = blend([unpack_stats(ref[2 * BODY : PAIR, :]) for ref in sources])
        for second in range(2):
            out = outs[2 * pair + second]
            for index, values in enumerate(mix(shares, sources, second * BODY, second * SECOND)):
                row = tile_start(index)
                out[row : row + HALF, :] = values.astype(BF16)
            here = pltpu.roll(level, LANES - SECOND, 1) if second else level
            out[BODY:LONE, :] = pack_stats(here)


def gather(ahead, behind, own, requests, ahead_base, behind_base):
    return pl.pallas_call(
        functools.partial(gather_kernel, ahead_base, behind_base),
        out_shape=[jax.ShapeDtypeStruct((LONE, HD), BF16)] * requests,
        in_specs=[IN_VMEM] * 3,
        out_specs=[IN_VMEM] * requests,
        compiler_params=params(),
        cost_estimate=cost(0, 8 * own.size),
    )(ahead, behind, own)


def final_kernel(place_ref, *refs):
    parts, (new_ref, level_ref, out_ref) = refs[:-3], refs[-3:]
    for d, part in enumerate(parts):
        row = place_ref[0] ^ d
        shares, _ = blend([unpack_stats(part[BODY:LONE, :]), level_ref[d]])
        values = mix(shares, (part, new_ref.at[d]), 0, 0)
        for index, tile in enumerate(values):
            first = tile_start(index) // STEPS
            for g in range(HALF // STEPS):
                head = first + g
                out_ref[row, :, head * HD : (head + 1) * HD] = tile[g * STEPS : (g + 1) * STEPS, :].astype(BF16)


def final(place, parts, new_out, new_level):
    groups = len(parts)
    return pl.pallas_call(
        final_kernel,
        out_shape=jax.ShapeDtypeStruct((groups, STEPS, KVH * GQ * HD), BF16),
        in_specs=[IN_SMEM] + [IN_VMEM] * (groups + 2),
        out_specs=IN_VMEM,
        compiler_params=params(),
        cost_estimate=cost(0, groups * BODY * HD * 8),
    )(place, *parts, new_out, new_level)


def ring_order(owners):
    return list(range(0, owners, 2)) + list(range(owners - 1, 0, -2))


def per_device(queries, new_kv, kv_cache, page_owner, page_index, lengths):
    groups = lax.axis_size("grp")
    owners = lax.axis_size("cache")
    requests = queries.shape[0]
    assert requests == groups and requests % 4 == 0 and owners <= LANES
    reach = owners // 2
    order = ring_order(owners)
    forward = [(order[i], order[(i + 1) % owners]) for i in range(owners)]
    backward = [(b, a) for a, b in forward]
    place = jnp.stack([lax.axis_index("grp"), lax.axis_index("cache")]).astype(jnp.int32)

    def swap(array, d):
        return lax.ppermute(array, "grp", [(g, g ^ d) for g in range(groups)]) if d else array

    rows = relayout(place, queries)
    visits = [swap(rows[d], d) for d in range(groups)]
    new_out, new_level = new_tokens(place, rows, new_kv)
    block = payload(place, page_owner, page_index[:, :, 0], lengths, visits)

    slots = list(range(requests))
    cut = requests // 2
    lists = list_rows(requests)
    ahead = behind = block
    parts = {0: items(place, block, kv_cache, requests, slots)}
    for step in range(1, reach + 1):
        if step == reach:
            ahead, behind = ahead[: cut * BODY + lists], behind[cut * BODY :]
        ahead = lax.ppermute(ahead, "cache", forward)
        behind = lax.ppermute(behind, "cache", backward)
        parts[-step] = items(place, ahead, kv_cache, requests, slots if step < reach else slots[:cut])
        parts[step] = items(place, behind, kv_cache, requests, slots if step < reach else slots[cut:])

    ahead, behind = parts[-reach], parts[reach]
    for step in range(reach - 1, -1, -1):
        ahead = lax.ppermute(ahead, "cache", forward)
        behind = lax.ppermute(behind, "cache", backward)
        base = cut // 2 if step == reach - 1 else 0
        if step > 0:
            ahead, behind = merge(ahead, parts[step], 0), merge(behind, parts[-step], base)
        else:
            returned = gather(ahead, behind, parts[0], requests, 0, base)
    home = [swap(returned[d], d) for d in range(groups)]
    return final(place, home, new_out, new_level)


def solution(mesh):
    in_specs = (
        P(("grp", "cache"), None, None),
        P(("grp", "cache"), None, None),
        P(("grp", "cache"), None, None),
        P(("grp", "cache"), None),
        P(("grp", "cache"), None, None),
        P(("grp", "cache")),
    )
    out_specs = P(("grp", "cache"), None, None)
    return jax.shard_map(
        per_device, mesh=mesh, in_specs=in_specs, out_specs=out_specs, check_vma=False
    )
```

```python
import functools
import math

import jax
import jax.numpy as jnp
from jax import lax
from jax.experimental import pallas as pl
from jax.experimental.pallas import tpu as pltpu
from jax.sharding import PartitionSpec as P

KVH = 8
HD = 128
GQ = 8
STEPS = 4
PAGE = 128
SEL = 4

LANES = 128
ROWS = GQ * STEPS
HALF = 16
BODY = KVH * ROWS
COLS = BODY // HALF
SECOND = 3 * COLS
PAIR = 2 * BODY + HALF
LONE = BODY + HALF
EMPTY = -1e30
SCALE = math.log2(math.e) / math.sqrt(HD)
VMEM_BYTES = 24 * 1024 * 1024
BF16 = jnp.bfloat16
F32 = jnp.float32
IN_VMEM = pl.BlockSpec(memory_space=pltpu.VMEM)
IN_SMEM = pl.BlockSpec(memory_space=pltpu.SMEM)


def params():
    return pltpu.CompilerParams(vmem_limit_bytes=VMEM_BYTES)


def cost(flops, moved):
    return pl.CostEstimate(flops=flops, bytes_accessed=moved, transcendentals=0)


def list_rows(requests):
    return -(-2 * requests // HALF) * HALF


def lane_ids(rows=HALF):
    return lax.broadcasted_iota(jnp.int32, (rows, LANES), 1)


def pack_stats(stats):
    lanes = lane_ids()
    used = (lanes < COLS) | ((lanes >= SECOND) & (lanes < SECOND + COLS))
    stats = jnp.where(used, stats, 0.0)
    high = stats.astype(BF16).astype(F32)
    rest = stats - high
    middle = rest.astype(BF16).astype(F32)
    low = rest - middle
    return (high + pltpu.roll(middle, COLS, 1) + pltpu.roll(low, 2 * COLS, 1)).astype(BF16)


def unpack_stats(tile):
    tile = tile.astype(F32)
    return tile + pltpu.roll(tile, LANES - COLS, 1) + pltpu.roll(tile, LANES - 2 * COLS, 1)


def tile_start(index):
    half, head = divmod(index, KVH)
    return head * ROWS + half * HALF


def by_lane(columns):
    lanes = lane_ids()
    tile = jnp.zeros((HALF, LANES), F32)
    for head, values in enumerate(columns):
        for half in range(ROWS // HALF):
            part = values[half * HALF : (half + 1) * HALF, :]
            tile = jnp.where(lanes == half * KVH + head, part, tile)
    return tile


def attend(queries, keys, values, usable):
    across = (((1,), (1,)), ((), ()))
    along = (((1,), (0,)), ((), ()))
    scores = [lax.dot_general(q, k, across, preferred_element_type=F32) for q, k in zip(queries, keys)]
    scores = [jnp.where(usable, s * SCALE, EMPTY) for s in scores]
    tops = [jnp.max(s, axis=1, keepdims=True) for s in scores]
    weights = [jnp.exp2(s - t) for s, t in zip(scores, tops)]
    totals = [jnp.sum(w, axis=1, keepdims=True) for w in weights]
    mixed = [lax.dot_general(w.astype(BF16), v, along, preferred_element_type=F32) for w, v in zip(weights, values)]
    level = by_lane(tops) + jnp.log2(jnp.maximum(by_lane(totals), 1.0))
    return [m / t for m, t in zip(mixed, totals)], level


def relayout_kernel(place_ref, queries_ref, *outs):
    for d, out in enumerate(outs):
        values = queries_ref[place_ref[0] ^ d].astype(F32)
        for head in range(KVH):
            first = head * GQ
            parts = [values[:, (first + g) * HD : (first + g + 1) * HD] for g in range(GQ)]
            out[head * ROWS : (head + 1) * ROWS, :] = jnp.concatenate(parts, axis=0).astype(BF16)


def relayout(place, queries):
    groups = queries.shape[0]
    return pl.pallas_call(
        relayout_kernel,
        out_shape=[jax.ShapeDtypeStruct((BODY, HD), BF16)] * groups,
        in_specs=[IN_SMEM, IN_VMEM],
        out_specs=[IN_VMEM] * groups,
        compiler_params=params(),
        cost_estimate=cost(0, 4 * queries.size),
    )(place, queries)


def new_kernel(place_ref, *refs):
    queries, (new_ref, out_ref, level_ref) = refs[:-3], refs[-3:]
    step = lax.broadcasted_iota(jnp.int32, (ROWS, STEPS), 0) % STEPS
    usable = lax.broadcasted_iota(jnp.int32, (ROWS, STEPS), 1) <= step
    for d, query in enumerate(queries):
        new = new_ref[place_ref[0] ^ d]
        heads = [new[:, head * HD : (head + 1) * HD] for head in range(2 * KVH)]
        rows = [query[head * ROWS : (head + 1) * ROWS, :] for head in range(KVH)]
        mixed, level = attend(rows, heads[:KVH], heads[KVH:], usable)
        for head, values in enumerate(mixed):
            out_ref[d, head * ROWS : (head + 1) * ROWS, :] = values
        level_ref[d] = level


def new_tokens(place, queries, new_kv):
    groups = len(queries)
    return pl.pallas_call(
        new_kernel,
        out_shape=[
            jax.ShapeDtypeStruct((groups, BODY, HD), F32),
            jax.ShapeDtypeStruct((groups, HALF, LANES), F32),
        ],
        in_specs=[IN_SMEM] + [IN_VMEM] * (groups + 1),
        out_specs=[IN_VMEM, IN_VMEM],
        compiler_params=params(),
        cost_estimate=cost(groups * KVH * 4 * ROWS * HD * HD, groups * BODY * HD * 6),
    )(place, *queries, new_kv)


def list_kernel(place_ref, owner_ref, index_ref, length_ref, out):
    requests = owner_ref.shape[0]
    lists = list_rows(requests)
    rows = lax.broadcasted_iota(jnp.int32, (lists, LANES), 0)
    lanes = lane_ids(lists)
    tile = jnp.zeros((lists, LANES), F32)
    for d in range(requests):
        row = place_ref[0] ^ d
        for s in range(SEL):
            count = jnp.clip(length_ref[row] - s * PAGE, 0, PAGE).astype(F32)
            mine = lanes == owner_ref[row, s]
            tile = jnp.where(mine & (rows == 2 * d), count, tile)
            tile = jnp.where(mine & (rows == 2 * d + 1), index_ref[row, s].astype(F32), tile)
    out[...] = tile.astype(BF16)


def page_lists(place, page_owner, page_index, lengths):
    lists = list_rows(page_owner.shape[0])
    return pl.pallas_call(
        list_kernel,
        out_shape=jax.ShapeDtypeStruct((lists, LANES), BF16),
        in_specs=[IN_SMEM] * 4,
        out_specs=IN_VMEM,
        compiler_params=params(),
        cost_estimate=cost(0, 4 * lists * HD),
    )(place, page_owner, page_index, lengths)


def payload_kernel(after, *refs):
    lists_ref, visits, out = refs[0], refs[1 : len(refs) - 1 - after], refs[-1]
    cut = len(visits) // 2
    lists = lists_ref.shape[0]
    for d, visit in enumerate(visits):
        start = d * BODY + (lists if d >= cut else 0)
        out[start : start + BODY, :] = visit[...]
    out[cut * BODY : cut * BODY + lists, :] = lists_ref[...]


def payload(lists, visits, after):
    rows = len(visits) * BODY + lists.shape[0]
    return pl.pallas_call(
        functools.partial(payload_kernel, len(after)),
        out_shape=jax.ShapeDtypeStruct((rows, HD), BF16),
        in_specs=[IN_VMEM] * (1 + len(visits) + len(after)),
        out_specs=IN_VMEM,
        compiler_params=params(),
        cost_estimate=cost(0, 4 * rows * HD),
    )(lists, *visits, *after)


def item_kernel(slots, list_start, first, gap_at, lists, outs, place_ref, query_ref, cache_ref, *refs):
    out_refs, (level_ref, code_ref) = refs[-2 - outs : -2], refs[-2:]
    owner = place_ref[1]
    table = query_ref[list_start : list_start + lists, :].astype(F32)
    rows = lax.broadcasted_iota(jnp.int32, (lists, LANES), 0)
    table = jnp.where(lane_ids(lists) == owner, table, 0.0)
    for entry, slot in enumerate(slots):
        code = jnp.where(rows == 2 * slot, table, jnp.where(rows == 2 * slot + 1, table * 256.0, 0.0))
        code_ref[entry] = jnp.sum(code).astype(jnp.int32)
    tokens = lax.broadcasted_iota(jnp.int32, (ROWS, PAGE), 1)
    each = len(slots) // outs

    def one(entry, out_ref, inner):
        code = code_ref[entry]
        count, page = code & 255, code >> 8
        start = first + entry * BODY + jnp.where(entry >= gap_at, lists, 0)
        out = (inner // 2) * PAIR + (inner % 2) * BODY

        @pl.when(count > 0)
        def _():
            queries = [query_ref[pl.ds(pl.multiple_of(start + h * ROWS, HALF), ROWS), :] for h in range(KVH)]
            keys = [cache_ref[page, :, h * HD : (h + 1) * HD] for h in range(KVH)]
            values = [cache_ref[page, :, (KVH + h) * HD : (KVH + h + 1) * HD] for h in range(KVH)]
            mixed, level = attend(queries, keys, values, tokens < count)
            for head, part in enumerate(mixed):
                out_ref[pl.ds(pl.multiple_of(out + head * ROWS, HALF), ROWS), :] = part.astype(BF16)
            level_ref[entry] = level

        @pl.when(count <= 0)
        def _():
            out_ref[pl.ds(pl.multiple_of(out, HALF), BODY), :] = jnp.zeros((BODY, HD), BF16)
            level_ref[entry] = jnp.full((HALF, LANES), EMPTY, F32)

    lanes = lane_ids()
    for number, out_ref in enumerate(out_refs):

        @pl.loop(0, each)
        def _(inner):
            one(number * each + inner, out_ref, inner)

        for pair in range(each // 2):
            entry = number * each + 2 * pair
            level = jnp.where(lanes < COLS, level_ref[entry], pltpu.roll(level_ref[entry + 1], SECOND, 1))
            start = pair * PAIR + 2 * BODY
            out_ref[start : start + HALF, :] = pack_stats(level)


def items(place, queries, pages, requests, slots, after=()):
    lists = list_rows(requests)
    cut = requests // 2
    if len(slots) == requests:
        list_start, first, gap_at = cut * BODY, 0, cut
    elif slots[0] == 0:
        list_start, first, gap_at = cut * BODY, 0, requests
    else:
        list_start, first, gap_at = 0, lists, requests
    count = len(slots)
    outs = count // cut
    return pl.pallas_call(
        functools.partial(item_kernel, slots, list_start, first, gap_at, lists, outs),
        out_shape=[jax.ShapeDtypeStruct((cut // 2 * PAIR, HD), BF16)] * outs,
        in_specs=[IN_SMEM] + [IN_VMEM] * (2 + len(after)),
        out_specs=[IN_VMEM] * outs,
        scratch_shapes=[pltpu.VMEM((count, HALF, LANES), F32), pltpu.SMEM((count,), jnp.int32)],
        compiler_params=params(),
        cost_estimate=cost(count * KVH * 4 * ROWS * HD * PAGE, count * PAGE * pages.shape[2] * 2),
    )(place, queries, pages, *after)


def blend(levels):
    peak = functools.reduce(jnp.maximum, levels)
    shares = [jnp.exp2(level - peak) for level in levels]
    total = functools.reduce(jnp.add, shares)
    return [share / total for share in shares], peak + jnp.log2(total)


def mix(shares, refs, start, first_lane):
    values = []
    for index in range(COLS):
        row, lane = start + tile_start(index), first_lane + index
        tiles = [ref[row : row + HALF, :].astype(F32) for ref in refs]
        total = tiles[0]
        for share, tile in zip(shares[1:], tiles[1:]):
            total = total + share[:, lane : lane + 1] * (tile - tiles[0])
        values.append(total)
    return values


def merge_kernel(arrived_ref, own_ref, out_ref):
    for pair in range(out_ref.shape[0] // PAIR):
        part = slice(pair * PAIR, (pair + 1) * PAIR)
        arrived, own, out = arrived_ref.at[part], own_ref.at[part], out_ref.at[part]
        shares, level = blend([unpack_stats(ref[2 * BODY : PAIR, :]) for ref in (arrived, own)])
        values = [mix(shares, (arrived, own), second * BODY, second * SECOND) for second in range(2)]
        for second in range(2):
            for index in range(COLS):
                row = second * BODY + tile_start(index)
                out[row : row + HALF, :] = values[second][index].astype(BF16)
        out[2 * BODY : PAIR, :] = pack_stats(level)


def merge(arrived, own):
    return pl.pallas_call(
        merge_kernel,
        out_shape=jax.ShapeDtypeStruct(own.shape, BF16),
        in_specs=[IN_VMEM, IN_VMEM],
        out_specs=IN_VMEM,
        compiler_params=params(),
        cost_estimate=cost(0, 6 * own.size),
    )(arrived, own)


def gather_kernel(ahead_ref, behind_ref, own_ref, *outs):
    for pair in range(len(outs) // 2):
        part = slice(pair * PAIR, (pair + 1) * PAIR)
        sources = [ref.at[part] for ref in (own_ref, ahead_ref, behind_ref)]
        shares, level = blend([unpack_stats(ref[2 * BODY : PAIR, :]) for ref in sources])
        values = [mix(shares, sources, second * BODY, second * SECOND) for second in range(2)]
        for second in range(2):
            out = outs[2 * pair + second]
            for index in range(COLS):
                row = tile_start(index)
                out[row : row + HALF, :] = values[second][index].astype(BF16)
            here = pltpu.roll(level, LANES - SECOND, 1) if second else level
            out[BODY:LONE, :] = pack_stats(here)


def gather(ahead, behind, own):
    requests = own.shape[0] // PAIR * 2
    return pl.pallas_call(
        gather_kernel,
        out_shape=[jax.ShapeDtypeStruct((LONE, HD), BF16)] * requests,
        in_specs=[IN_VMEM] * 3,
        out_specs=[IN_VMEM] * requests,
        compiler_params=params(),
        cost_estimate=cost(0, 8 * own.size),
    )(ahead, behind, own)


def final_kernel(place_ref, *refs):
    parts, (new_ref, level_ref, out_ref, rows_ref) = refs[:-4], refs[-4:]
    for d, part in enumerate(parts):
        shares, _ = blend([unpack_stats(part[BODY:LONE, :]), level_ref[d]])
        for index, tile in enumerate(mix(shares, (part, new_ref.at[d]), 0, 0)):
            row = tile_start(index)
            rows_ref[d, row : row + HALF, :] = tile
    for d in range(len(parts)):
        row = place_ref[0] ^ d
        for head in range(KVH * GQ):
            tile = rows_ref[d, head * STEPS : (head + 1) * STEPS, :]
            out_ref[row, :, head * HD : (head + 1) * HD] = tile.astype(BF16)


def final(place, parts, new_out, new_level):
    groups = len(parts)
    return pl.pallas_call(
        final_kernel,
        out_shape=jax.ShapeDtypeStruct((groups, STEPS, KVH * GQ * HD), BF16),
        in_specs=[IN_SMEM] + [IN_VMEM] * (groups + 2),
        out_specs=IN_VMEM,
        scratch_shapes=[pltpu.VMEM((groups, BODY, HD), F32)],
        compiler_params=params(),
        cost_estimate=cost(0, groups * BODY * HD * 8),
    )(place, *parts, new_out, new_level)


def ring_order(owners):
    return list(range(0, owners, 2)) + list(range(owners - 1, 0, -2))


def per_device(queries, new_kv, kv_cache, page_owner, page_index, lengths):
    groups = lax.axis_size("grp")
    owners = lax.axis_size("cache")
    requests = queries.shape[0]
    assert requests == groups and requests % 4 == 0 and owners <= LANES
    reach = owners // 2
    order = ring_order(owners)
    forward = [(order[i], order[(i + 1) % owners]) for i in range(owners)]
    backward = [(b, a) for a, b in forward]
    place = jnp.stack([lax.axis_index("grp"), lax.axis_index("cache")]).astype(jnp.int32)

    def swap(array, d):
        return lax.ppermute(array, "grp", [(g, g ^ d) for g in range(groups)]) if d else array

    rows = relayout(place, queries)
    visits = [rows[0]] + [None] * (groups - 1)
    for d in range(groups - 1, 0, -1):
        visits[d] = swap(rows[d], d)
    new_out, new_level = new_tokens(place, rows, new_kv)
    lists = page_lists(place, page_owner, page_index[:, :, 0], lengths)
    block = payload(lists, visits, (new_level,))

    slots = list(range(requests))
    cut = requests // 2
    middle = cut * BODY
    below = above = block
    parts = {0: items(place, block, kv_cache, requests, slots)}
    for step in range(1, reach + 1):
        if step == reach:
            below, above = below[: middle + lists.shape[0]], above[middle:]
        below = lax.ppermute(below, "cache", forward)
        above = lax.ppermute(above, "cache", backward)
        if step < reach:
            done = parts[0] if step == 1 else parts[1 - step] + parts[step - 1]
            below, above = lax.optimization_barrier((below, done))[0], lax.optimization_barrier((above, done))[0]
            parts[-step] = items(place, below, kv_cache, requests, slots)
            parts[step] = items(place, above, kv_cache, requests, slots)
    far_ahead = items(place, below, kv_cache, requests, slots[:cut])
    far_behind = items(place, above, kv_cache, requests, slots[cut:])

    arrived = []
    for half in range(2):
        for ring, sign in ((forward, 1), (backward, -1)):
            if half == 0 and sign == 1:
                chain, steps = far_ahead[0], range(reach - 1, -1, -1)
            elif half == 1 and sign == -1:
                chain, steps = far_behind[0], range(reach - 1, -1, -1)
            else:
                chain, steps = parts[sign * (reach - 1)][half], range(reach - 2, -1, -1)
            for step in steps:
                chain = lax.ppermute(chain, "cache", ring)
                if step > 0:
                    chain = merge(chain, parts[sign * step][half])
            arrived.append(chain)
    back = gather(arrived[2], arrived[3], parts[0][1])
    front = gather(arrived[0], arrived[1], parts[0][0])
    returned = list(front) + list(back)
    home = [returned[0]] + [None] * (groups - 1)
    for d in range(groups - 1, 0, -1):
        home[d] = swap(returned[d], d)
    return final(place, home, new_out, new_level)


def solution(mesh):
    in_specs = (
        P(("grp", "cache"), None, None),
        P(("grp", "cache"), None, None),
        P(("grp", "cache"), None, None),
        P(("grp", "cache"), None),
        P(("grp", "cache"), None, None),
        P(("grp", "cache")),
    )
    out_specs = P(("grp", "cache"), None, None)
    return jax.shard_map(
        per_device, mesh=mesh, in_specs=in_specs, out_specs=out_specs, check_vma=False
    )
```

```python
import functools
import math

import jax
import jax.numpy as jnp
from jax import lax
from jax.experimental import pallas as pl
from jax.experimental.pallas import tpu as pltpu
from jax.sharding import PartitionSpec as P

KVH = 8
HD = 128
GQ = 8
STEPS = 4
PAGE = 128
SEL = 4

LANES = 128
ROWS = GQ * STEPS
HALF = 16
BODY = KVH * ROWS
COLS = BODY // HALF
SECOND = 3 * COLS
PAIR = 2 * BODY + HALF
LONE = BODY + HALF
EMPTY = -1e30
SCALE = math.log2(math.e) / math.sqrt(HD)
VMEM_BYTES = 24 * 1024 * 1024
BF16 = jnp.bfloat16
F32 = jnp.float32
IN_VMEM = pl.BlockSpec(memory_space=pltpu.VMEM)
IN_SMEM = pl.BlockSpec(memory_space=pltpu.SMEM)


def params():
    return pltpu.CompilerParams(vmem_limit_bytes=VMEM_BYTES)


def cost(flops, moved):
    return pl.CostEstimate(flops=flops, bytes_accessed=moved, transcendentals=0)


def list_rows(requests):
    return -(-2 * requests // HALF) * HALF


def lane_ids(rows=HALF):
    return lax.broadcasted_iota(jnp.int32, (rows, LANES), 1)


def pack_stats(stats):
    lanes = lane_ids()
    used = (lanes < COLS) | ((lanes >= SECOND) & (lanes < SECOND + COLS))
    stats = jnp.where(used, stats, 0.0)
    high = stats.astype(BF16).astype(F32)
    rest = stats - high
    middle = rest.astype(BF16).astype(F32)
    low = rest - middle
    return (high + pltpu.roll(middle, COLS, 1) + pltpu.roll(low, 2 * COLS, 1)).astype(BF16)


def unpack_stats(tile):
    tile = tile.astype(F32)
    return tile + pltpu.roll(tile, LANES - COLS, 1) + pltpu.roll(tile, LANES - 2 * COLS, 1)


def tile_start(index):
    half, head = divmod(index, KVH)
    return head * ROWS + half * HALF


def by_lane(columns):
    lanes = lane_ids()
    tile = jnp.zeros((HALF, LANES), F32)
    for head, values in enumerate(columns):
        for half in range(ROWS // HALF):
            part = values[half * HALF : (half + 1) * HALF, :]
            tile = jnp.where(lanes == half * KVH + head, part, tile)
    return tile


def attend(queries, keys, values, usable):
    across = (((1,), (1,)), ((), ()))
    along = (((1,), (0,)), ((), ()))
    ones = jnp.ones(values[0].shape, BF16)
    scores = [lax.dot_general(q, k, across, preferred_element_type=F32) for q, k in zip(queries, keys)]
    scores = [jnp.where(usable, s * SCALE, EMPTY) for s in scores]
    tops = [jnp.max(s, axis=1, keepdims=True) for s in scores]
    weights = [jnp.exp2(s - t).astype(BF16) for s, t in zip(scores, tops)]
    both = [
        lax.dot_general(w, jnp.concatenate([v, ones], axis=1), along, preferred_element_type=F32)
        for w, v in zip(weights, values)
    ]
    mixed, totals = [b[:, :HD] for b in both], [b[:, HD:] for b in both]
    level = by_lane(tops) + jnp.log2(jnp.maximum(by_lane(totals), 1.0))
    return [m / t for m, t in zip(mixed, totals)], level


def relayout_kernel(place_ref, queries_ref, *outs):
    for d, out in enumerate(outs):
        values = queries_ref[place_ref[0] ^ d].astype(F32)
        for head in range(KVH):
            first = head * GQ
            parts = [values[:, (first + g) * HD : (first + g + 1) * HD] for g in range(GQ)]
            out[head * ROWS : (head + 1) * ROWS, :] = jnp.concatenate(parts, axis=0).astype(BF16)


def relayout(place, queries):
    groups = queries.shape[0]
    return pl.pallas_call(
        relayout_kernel,
        out_shape=[jax.ShapeDtypeStruct((BODY, HD), BF16)] * groups,
        in_specs=[IN_SMEM, IN_VMEM],
        out_specs=[IN_VMEM] * groups,
        compiler_params=params(),
        cost_estimate=cost(0, 4 * queries.size),
    )(place, queries)


def new_kernel(place_ref, *refs):
    queries, (new_ref, out_ref, level_ref) = refs[:-3], refs[-3:]
    step = lax.broadcasted_iota(jnp.int32, (ROWS, STEPS), 0) % STEPS
    usable = lax.broadcasted_iota(jnp.int32, (ROWS, STEPS), 1) <= step
    for d, query in enumerate(queries):
        new = new_ref[place_ref[0] ^ d]
        heads = [new[:, head * HD : (head + 1) * HD] for head in range(2 * KVH)]
        rows = [query[head * ROWS : (head + 1) * ROWS, :] for head in range(KVH)]
        mixed, level = attend(rows, heads[:KVH], heads[KVH:], usable)
        for head, values in enumerate(mixed):
            out_ref[d, head * ROWS : (head + 1) * ROWS, :] = values
        level_ref[d] = level


def new_tokens(place, queries, new_kv):
    groups = len(queries)
    return pl.pallas_call(
        new_kernel,
        out_shape=[
            jax.ShapeDtypeStruct((groups, BODY, HD), F32),
            jax.ShapeDtypeStruct((groups, HALF, LANES), F32),
        ],
        in_specs=[IN_SMEM] + [IN_VMEM] * (groups + 1),
        out_specs=[IN_VMEM, IN_VMEM],
        compiler_params=params(),
        cost_estimate=cost(groups * KVH * 4 * ROWS * HD * HD, groups * BODY * HD * 6),
    )(place, *queries, new_kv)


def page_lists(page_owner, page_index, lengths):
    visitors = page_owner.shape[0]
    lanes = jnp.arange(LANES, dtype=jnp.int32)[None, None, :]
    first = jnp.arange(2, dtype=jnp.int32)[None, :, None] == 0
    table = jnp.zeros((visitors, 2, LANES), jnp.int32)
    for s in range(SEL):
        count = jnp.clip(lengths - s * PAGE, 0, PAGE)[:, None, None]
        value = jnp.where(first, count, page_index[:, s, 0][:, None, None])
        table = table + jnp.where(page_owner[:, s][:, None, None] == lanes, value, 0)
    table = table.reshape(2 * visitors, LANES).astype(BF16)
    return jnp.pad(table, ((0, list_rows(visitors) - 2 * visitors), (0, 0)))


def payload_kernel(lists_ref, *refs):
    visits, out = refs[:-1], refs[-1]
    for number, visit in enumerate(visits):
        out[number * BODY : (number + 1) * BODY, :] = visit[...]
    out[len(visits) * BODY :, :] = lists_ref[...]


def payload(lists, visits):
    rows = len(visits) * BODY + lists.shape[0]
    return pl.pallas_call(
        payload_kernel,
        out_shape=jax.ShapeDtypeStruct((rows, HD), BF16),
        in_specs=[IN_VMEM] * (1 + len(visits)),
        out_specs=IN_VMEM,
        compiler_params=params(),
        cost_estimate=cost(0, 4 * rows * HD),
    )(lists, *visits)


def item_kernel(slots, place_ref, cache_ref, *refs):
    sides = len(slots)
    query_refs, out_refs, (level_ref, code_ref) = refs[:sides], refs[sides : 2 * sides], refs[2 * sides :]
    each = len(slots[0])
    for side, query_ref in enumerate(query_refs):
        lists = query_ref.shape[0] - each * BODY
        rows = lax.broadcasted_iota(jnp.int32, (lists, LANES), 0)
        table = query_ref[each * BODY :, :].astype(F32)
        table = jnp.where(lane_ids(lists) == place_ref[1], table, 0.0)
        table = jnp.where((rows & 1) == 0, table, table * 256.0)
        for number, slot in enumerate(slots[side]):
            code = jnp.where(rows >> 1 == (place_ref[0] ^ slot), table, 0.0)
            code_ref[side * each + number] = jnp.sum(code).astype(jnp.int32)
    tokens = lax.broadcasted_iota(jnp.int32, (ROWS, PAGE), 1)

    def one(side, number):
        entry = side * each + number
        query_ref, out_ref = query_refs[side], out_refs[side]
        code = code_ref[entry]
        count, page = code & 255, code >> 8
        start = number * BODY
        out = (number // 2) * PAIR + (number % 2) * BODY

        @pl.when(count > 0)
        def _():
            queries = [query_ref[pl.ds(pl.multiple_of(start + h * ROWS, HALF), ROWS), :] for h in range(KVH)]
            keys = [cache_ref[page, :, h * HD : (h + 1) * HD] for h in range(KVH)]
            values = [cache_ref[page, :, (KVH + h) * HD : (KVH + h + 1) * HD] for h in range(KVH)]
            mixed, level = attend(queries, keys, values, tokens < count)
            for head, part in enumerate(mixed):
                out_ref[pl.ds(pl.multiple_of(out + head * ROWS, HALF), ROWS), :] = part.astype(BF16)
            level_ref[entry] = level

        @pl.when(count <= 0)
        def _():
            out_ref[pl.ds(pl.multiple_of(out, HALF), BODY), :] = jnp.zeros((BODY, HD), BF16)
            level_ref[entry] = jnp.full((HALF, LANES), EMPTY, F32)

    lanes = lane_ids()
    for side, out_ref in enumerate(out_refs):

        @pl.loop(0, each)
        def _(number):
            one(side, number)

    for side, out_ref in enumerate(out_refs):
        for pair in range(each // 2):
            entry = side * each + 2 * pair
            level = jnp.where(lanes < COLS, level_ref[entry], pltpu.roll(level_ref[entry + 1], SECOND, 1))
            start = pair * PAIR + 2 * BODY
            out_ref[start : start + HALF, :] = pack_stats(level)


def items(place, kv_cache, payloads, slots):
    count = sum(len(row) for row in slots)
    rows = len(slots[0]) // 2 * PAIR
    return pl.pallas_call(
        functools.partial(item_kernel, slots),
        out_shape=[jax.ShapeDtypeStruct((rows, HD), BF16)] * len(slots),
        in_specs=[IN_SMEM] + [IN_VMEM] * (1 + len(slots)),
        out_specs=[IN_VMEM] * len(slots),
        scratch_shapes=[pltpu.VMEM((count, HALF, LANES), F32), pltpu.SMEM((count,), jnp.int32)],
        compiler_params=params(),
        cost_estimate=cost(count * KVH * 4 * ROWS * HD * PAGE, count * PAGE * kv_cache.shape[2] * 2),
    )(place, kv_cache, *payloads)


def blend(levels):
    peak = functools.reduce(jnp.maximum, levels)
    shares = [jnp.exp2(level - peak) for level in levels]
    total = functools.reduce(jnp.add, shares)
    return [share / total for share in shares], peak + jnp.log2(total)


def mix(shares, refs, start, first_lane):
    values = []
    for index in range(COLS):
        row, lane = start + tile_start(index), first_lane + index
        tiles = [ref[row : row + HALF, :].astype(F32) for ref in refs]
        total = tiles[0]
        for share, tile in zip(shares[1:], tiles[1:]):
            total = total + share[:, lane : lane + 1] * (tile - tiles[0])
        values.append(total)
    return values


def merge_kernel(arrived_ref, own_ref, out_ref):
    for pair in range(out_ref.shape[0] // PAIR):
        part = slice(pair * PAIR, (pair + 1) * PAIR)
        arrived, own, out = arrived_ref.at[part], own_ref.at[part], out_ref.at[part]
        shares, level = blend([unpack_stats(ref[2 * BODY : PAIR, :]) for ref in (arrived, own)])
        values = [mix(shares, (arrived, own), second * BODY, second * SECOND) for second in range(2)]
        for second in range(2):
            for index in range(COLS):
                row = second * BODY + tile_start(index)
                out[row : row + HALF, :] = values[second][index].astype(BF16)
        out[2 * BODY : PAIR, :] = pack_stats(level)


def merge(arrived, own):
    return pl.pallas_call(
        merge_kernel,
        out_shape=jax.ShapeDtypeStruct(own.shape, BF16),
        in_specs=[IN_VMEM, IN_VMEM],
        out_specs=IN_VMEM,
        compiler_params=params(),
        cost_estimate=cost(0, 6 * own.size),
    )(arrived, own)


def gather_kernel(ahead_ref, behind_ref, own_ref, *outs):
    for pair in range(len(outs) // 2):
        part = slice(pair * PAIR, (pair + 1) * PAIR)
        sources = [ref.at[part] for ref in (own_ref, ahead_ref, behind_ref)]
        shares, level = blend([unpack_stats(ref[2 * BODY : PAIR, :]) for ref in sources])
        values = [mix(shares, sources, second * BODY, second * SECOND) for second in range(2)]
        for second in range(2):
            out = outs[2 * pair + second]
            for index in range(COLS):
                row = tile_start(index)
                out[row : row + HALF, :] = values[second][index].astype(BF16)
            here = pltpu.roll(level, LANES - SECOND, 1) if second else level
            out[BODY:LONE, :] = pack_stats(here)


def gather(ahead, behind, own):
    requests = own.shape[0] // PAIR * 2
    return pl.pallas_call(
        gather_kernel,
        out_shape=[jax.ShapeDtypeStruct((LONE, HD), BF16)] * requests,
        in_specs=[IN_VMEM] * 3,
        out_specs=[IN_VMEM] * requests,
        compiler_params=params(),
        cost_estimate=cost(0, 8 * own.size),
    )(ahead, behind, own)


def final_kernel(place_ref, *refs):
    parts, (new_ref, level_ref, out_ref, rows_ref) = refs[:-4], refs[-4:]
    for d, part in enumerate(parts):
        shares, _ = blend([unpack_stats(part[BODY:LONE, :]), level_ref[d]])
        for index, tile in enumerate(mix(shares, (part, new_ref.at[d]), 0, 0)):
            row = tile_start(index)
            rows_ref[d, row : row + HALF, :] = tile
    for d in range(len(parts)):
        row = place_ref[0] ^ d
        for head in range(KVH * GQ):
            tile = rows_ref[d, head * STEPS : (head + 1) * STEPS, :]
            out_ref[row, :, head * HD : (head + 1) * HD] = tile.astype(BF16)


def final(place, parts, new_out, new_level):
    groups = len(parts)
    return pl.pallas_call(
        final_kernel,
        out_shape=jax.ShapeDtypeStruct((groups, STEPS, KVH * GQ * HD), BF16),
        in_specs=[IN_SMEM] + [IN_VMEM] * (groups + 2),
        out_specs=IN_VMEM,
        scratch_shapes=[pltpu.VMEM((groups, BODY, HD), F32)],
        compiler_params=params(),
        cost_estimate=cost(0, groups * BODY * HD * 8),
    )(place, *parts, new_out, new_level)


def ring_order(owners):
    return list(range(0, owners, 2)) + list(range(owners - 1, 0, -2))


def per_device(queries, new_kv, kv_cache, page_owner, page_index, lengths):
    groups = lax.axis_size("grp")
    owners = lax.axis_size("cache")
    requests = queries.shape[0]
    assert requests == groups and requests % 4 == 0 and owners <= LANES
    reach = owners // 2
    order = ring_order(owners)
    forward = [(order[i], order[(i + 1) % owners]) for i in range(owners)]
    backward = [(b, a) for a, b in forward]
    place = jnp.stack([lax.axis_index("grp"), lax.axis_index("cache")]).astype(jnp.int32)

    def swap(array, d):
        return lax.ppermute(array, "grp", [(g, g ^ d) for g in range(groups)]) if d else array

    rows = relayout(place, queries)
    visits = [rows[0]] + [None] * (groups - 1)
    for d in range(groups - 1, 0, -1):
        visits[d] = swap(rows[d], d)
    new_out, new_level = new_tokens(place, rows, new_kv)
    lists = page_lists(page_owner, page_index, lengths)

    cut = requests // 2
    slots = [list(range(cut)), list(range(cut, requests))]
    blocks = [payload(lists, visits[:cut])]
    blocks.append(payload(lax.optimization_barrier((lists, blocks[0]))[0], visits[cut:]))
    below, above = list(blocks), list(blocks)
    parts = {(half, 0): part for half, part in enumerate(items(place, kv_cache, blocks, slots))}
    far = [None, None]
    for step in range(1, reach + 1):
        for half in range(2):
            if step < reach or half == 0:
                below[half] = lax.ppermute(below[half], "cache", forward)
            if step < reach or half == 1:
                above[half] = lax.ppermute(above[half], "cache", backward)
            if step == reach:
                far[half] = items(place, kv_cache, [(below, above)[half][half]], [slots[half]])[0]
                continue
            done = [parts[half, 0]] if step == 1 else [parts[half, 1 - step], parts[half, step - 1]]
            below[half] = lax.optimization_barrier((below[half], done))[0]
            above[half] = lax.optimization_barrier((above[half], done))[0]
            parts[half, -step], parts[half, step] = items(
                place, kv_cache, [below[half], above[half]], [slots[half]] * 2
            )

    arrived = []
    for half in range(2):
        for ring, sign in ((forward, 1), (backward, -1)):
            if half == (0 if sign == 1 else 1):
                chain, steps = far[half], range(reach - 1, -1, -1)
            else:
                chain, steps = parts[half, sign * (reach - 1)], range(reach - 2, -1, -1)
            for step in steps:
                chain = lax.ppermute(chain, "cache", ring)
                if step > 0:
                    chain = merge(chain, parts[half, sign * step])
            arrived.append(chain)
    back = gather(arrived[2], arrived[3], parts[1, 0])
    front = gather(arrived[0], arrived[1], parts[0, 0])
    returned = list(front) + list(back)
    home = [returned[0]] + [None] * (groups - 1)
    for d in range(groups - 1, 0, -1):
        home[d] = swap(returned[d], d)
    return final(place, home, new_out, new_level)


def solution(mesh):
    in_specs = (
        P(("grp", "cache"), None, None),
        P(("grp", "cache"), None, None),
        P(("grp", "cache"), None, None),
        P(("grp", "cache"), None),
        P(("grp", "cache"), None, None),
        P(("grp", "cache")),
    )
    out_specs = P(("grp", "cache"), None, None)
    return jax.shard_map(
        per_device, mesh=mesh, in_specs=in_specs, out_specs=out_specs, check_vma=False
    )
```

```python
import functools
import math

import jax
import jax.numpy as jnp
from jax import lax
from jax.experimental import pallas as pl
from jax.experimental.pallas import tpu as pltpu
from jax.sharding import PartitionSpec as P

KVH = 8
HD = 128
GQ = 8
STEPS = 4
PAGE = 128
SEL = 4

LANES = 128
ROWS = GQ * STEPS
HALF = 16
BODY = KVH * ROWS
COLS = BODY // HALF
SECOND = 3 * COLS
PAIR = 2 * BODY + HALF
LONE = BODY + HALF
EMPTY = -1e30
SCALE = math.log2(math.e) / math.sqrt(HD)
VMEM_BYTES = 24 * 1024 * 1024
BF16 = jnp.bfloat16
F32 = jnp.float32
IN_VMEM = pl.BlockSpec(memory_space=pltpu.VMEM)
IN_SMEM = pl.BlockSpec(memory_space=pltpu.SMEM)


def params():
    return pltpu.CompilerParams(vmem_limit_bytes=VMEM_BYTES)


def cost(flops, moved):
    return pl.CostEstimate(flops=flops, bytes_accessed=moved, transcendentals=0)


def list_rows(requests):
    return -(-2 * requests // HALF) * HALF


def lane_ids(rows=HALF):
    return lax.broadcasted_iota(jnp.int32, (rows, LANES), 1)


def pack_stats(stats):
    lanes = lane_ids()
    used = (lanes < COLS) | ((lanes >= SECOND) & (lanes < SECOND + COLS))
    stats = jnp.where(used, stats, 0.0)
    high = stats.astype(BF16).astype(F32)
    rest = stats - high
    middle = rest.astype(BF16).astype(F32)
    low = rest - middle
    return (high + pltpu.roll(middle, COLS, 1) + pltpu.roll(low, 2 * COLS, 1)).astype(BF16)


def unpack_stats(tile):
    tile = tile.astype(F32)
    return tile + pltpu.roll(tile, LANES - COLS, 1) + pltpu.roll(tile, LANES - 2 * COLS, 1)


def tile_start(index):
    half, head = divmod(index, KVH)
    return head * ROWS + half * HALF


def by_lane(columns):
    lanes = lane_ids()
    tile = jnp.zeros((HALF, LANES), F32)
    for head, values in enumerate(columns):
        for half in range(ROWS // HALF):
            part = values[half * HALF : (half + 1) * HALF, :]
            tile = jnp.where(lanes == half * KVH + head, part, tile)
    return tile


def attend(queries, keys, values, usable):
    across = (((1,), (1,)), ((), ()))
    along = (((1,), (0,)), ((), ()))
    ones = jnp.ones(values[0].shape, BF16)
    scores = [lax.dot_general(q, k, across, preferred_element_type=F32) for q, k in zip(queries, keys)]
    scores = [jnp.where(usable, s * SCALE, EMPTY) for s in scores]
    tops = [jnp.max(s, axis=1, keepdims=True) for s in scores]
    weights = [jnp.exp2(s - t).astype(BF16) for s, t in zip(scores, tops)]
    both = [
        lax.dot_general(w, jnp.concatenate([v, ones], axis=1), along, preferred_element_type=F32)
        for w, v in zip(weights, values)
    ]
    mixed, totals = [b[:, :HD] for b in both], [b[:, HD:] for b in both]
    level = by_lane(tops) + jnp.log2(jnp.maximum(by_lane(totals), 1.0))
    return [m / t for m, t in zip(mixed, totals)], level


def relayout_kernel(place_ref, queries_ref, *outs):
    for d, out in enumerate(outs):
        values = queries_ref[place_ref[0] ^ d].astype(F32)
        for head in range(KVH):
            first = head * GQ
            parts = [values[:, (first + g) * HD : (first + g + 1) * HD] for g in range(GQ)]
            out[head * ROWS : (head + 1) * ROWS, :] = jnp.concatenate(parts, axis=0).astype(BF16)


def relayout(place, queries):
    groups = queries.shape[0]
    return pl.pallas_call(
        relayout_kernel,
        out_shape=[jax.ShapeDtypeStruct((BODY, HD), BF16)] * groups,
        in_specs=[IN_SMEM, IN_VMEM],
        out_specs=[IN_VMEM] * groups,
        compiler_params=params(),
        cost_estimate=cost(0, 4 * queries.size),
    )(place, queries)


def new_kernel(place_ref, *refs):
    queries, (new_ref, out_ref, level_ref) = refs[:-3], refs[-3:]
    step = lax.broadcasted_iota(jnp.int32, (ROWS, STEPS), 0) % STEPS
    usable = lax.broadcasted_iota(jnp.int32, (ROWS, STEPS), 1) <= step
    for d, query in enumerate(queries):
        new = new_ref[place_ref[0] ^ d]
        heads = [new[:, head * HD : (head + 1) * HD] for head in range(2 * KVH)]
        rows = [query[head * ROWS : (head + 1) * ROWS, :] for head in range(KVH)]
        mixed, level = attend(rows, heads[:KVH], heads[KVH:], usable)
        for head, values in enumerate(mixed):
            out_ref[d, head * ROWS : (head + 1) * ROWS, :] = values
        level_ref[d] = level


def new_tokens(place, queries, new_kv):
    groups = len(queries)
    return pl.pallas_call(
        new_kernel,
        out_shape=[
            jax.ShapeDtypeStruct((groups, BODY, HD), F32),
            jax.ShapeDtypeStruct((groups, HALF, LANES), F32),
        ],
        in_specs=[IN_SMEM] + [IN_VMEM] * (groups + 1),
        out_specs=[IN_VMEM, IN_VMEM],
        compiler_params=params(),
        cost_estimate=cost(groups * KVH * 4 * ROWS * HD * HD, groups * BODY * HD * 6),
    )(place, *queries, new_kv)


def page_lists(page_owner, page_index, lengths):
    lanes = jnp.arange(LANES, dtype=jnp.int32)[None, None, :]
    counts = jnp.clip(lengths[:, None] - jnp.arange(SEL, dtype=jnp.int32)[None, :] * PAGE, 0, PAGE)
    named = page_owner[:, :, None] == lanes
    return (
        jnp.sum(jnp.where(named, counts[:, :, None], 0), axis=1),
        jnp.sum(jnp.where(named, page_index, 0), axis=1),
    )


def payload_kernel(after, counts_ref, pages_ref, *refs):
    visits, out = refs[: len(refs) - 1 - after], refs[-1]
    for number, visit in enumerate(visits):
        out[number * BODY : (number + 1) * BODY, :] = visit[...]
    tables = [counts_ref[...].astype(F32), pages_ref[...].astype(F32)]
    short = out.shape[0] - len(visits) * BODY - 2 * tables[0].shape[0]
    if short:
        tables.append(jnp.zeros((short, LANES), F32))
    out[len(visits) * BODY :, :] = jnp.concatenate(tables, axis=0).astype(BF16)


def payload(lists, visits, after=()):
    rows = len(visits) * BODY + list_rows(lists[0].shape[0])
    return pl.pallas_call(
        functools.partial(payload_kernel, len(after)),
        out_shape=jax.ShapeDtypeStruct((rows, HD), BF16),
        in_specs=[IN_VMEM] * (2 + len(visits) + len(after)),
        out_specs=IN_VMEM,
        compiler_params=params(),
        cost_estimate=cost(0, 4 * rows * HD),
    )(*lists, *visits, *after)


def touch_kernel(after_ref, cache_ref, out_ref):
    out_ref[...] = cache_ref[0, :HALF, :HD]


def touch(kv_cache, after):
    return pl.pallas_call(
        touch_kernel,
        out_shape=jax.ShapeDtypeStruct((HALF, HD), BF16),
        in_specs=[IN_VMEM, IN_VMEM],
        out_specs=IN_VMEM,
        compiler_params=params(),
        cost_estimate=cost(0, 2 * HALF * HD),
    )(after, kv_cache)


def item_kernel(slots, visitors, place_ref, cache_ref, *refs):
    sides = len(slots)
    query_refs, (out_ref, level_ref, code_ref) = refs[:sides], refs[sides:]
    each = len(slots[0])
    for side, query_ref in enumerate(query_refs):
        lists = query_ref.shape[0] - each * BODY
        rows = lax.broadcasted_iota(jnp.int32, (lists, LANES), 0)
        table = query_ref[each * BODY :, :].astype(F32)
        table = jnp.where(lane_ids(lists) == place_ref[1], table, 0.0)
        for number, slot in enumerate(slots[side]):
            row = place_ref[0] ^ slot
            code = jnp.where(rows == row, table, jnp.where(rows == row + visitors, table * 256.0, 0.0))
            code_ref[side * each + number] = jnp.sum(code).astype(jnp.int32)
    tokens = lax.broadcasted_iota(jnp.int32, (ROWS, PAGE), 1)

    def one(side, number):
        entry = side * each + number
        query_ref = query_refs[side]
        code = code_ref[entry]
        count, page = code & 255, code >> 8
        start = number * BODY
        out = (entry // 2) * PAIR + (entry % 2) * BODY

        @pl.when(count > 0)
        def _():
            queries = [query_ref[pl.ds(pl.multiple_of(start + h * ROWS, HALF), ROWS), :] for h in range(KVH)]
            keys = [cache_ref[page, :, h * HD : (h + 1) * HD] for h in range(KVH)]
            values = [cache_ref[page, :, (KVH + h) * HD : (KVH + h + 1) * HD] for h in range(KVH)]
            mixed, level = attend(queries, keys, values, tokens < count)
            for head, part in enumerate(mixed):
                out_ref[pl.ds(pl.multiple_of(out + head * ROWS, HALF), ROWS), :] = part.astype(BF16)
            level_ref[entry] = level

        @pl.when(count <= 0)
        def _():
            out_ref[pl.ds(pl.multiple_of(out, HALF), BODY), :] = jnp.zeros((BODY, HD), BF16)
            level_ref[entry] = jnp.full((HALF, LANES), EMPTY, F32)

    for side in range(sides):

        @pl.loop(0, each)
        def _(number):
            one(side, number)

    lanes = lane_ids()
    for pair in range(sides * each // 2):
        level = jnp.where(lanes < COLS, level_ref[2 * pair], pltpu.roll(level_ref[2 * pair + 1], SECOND, 1))
        start = pair * PAIR + 2 * BODY
        out_ref[start : start + HALF, :] = pack_stats(level)


def items(place, kv_cache, payloads, slots, visitors):
    count = sum(len(row) for row in slots)
    return pl.pallas_call(
        functools.partial(item_kernel, slots, visitors),
        out_shape=jax.ShapeDtypeStruct((count // 2 * PAIR, HD), BF16),
        in_specs=[IN_SMEM] + [IN_VMEM] * (1 + len(slots)),
        out_specs=IN_VMEM,
        scratch_shapes=[pltpu.VMEM((count, HALF, LANES), F32), pltpu.SMEM((count,), jnp.int32)],
        compiler_params=params(),
        cost_estimate=cost(count * KVH * 4 * ROWS * HD * PAGE, count * PAGE * kv_cache.shape[2] * 2),
    )(place, kv_cache, *payloads)


def blend(levels):
    peak = functools.reduce(jnp.maximum, levels)
    shares = [jnp.exp2(level - peak) for level in levels]
    total = functools.reduce(jnp.add, shares)
    return [share / total for share in shares], peak + jnp.log2(total)


def mix(shares, refs, start, first_lane):
    values = []
    for index in range(COLS):
        row, lane = start + tile_start(index), first_lane + index
        tiles = [ref[row : row + HALF, :].astype(F32) for ref in refs]
        total = tiles[0]
        for share, tile in zip(shares[1:], tiles[1:]):
            total = total + share[:, lane : lane + 1] * (tile - tiles[0])
        values.append(total)
    return values


def merge_kernel(base, arrived_ref, own_ref, out_ref):
    arrived_pairs = arrived_ref.shape[0] // PAIR
    for pair in range(out_ref.shape[0] // PAIR):
        part = slice(pair * PAIR, (pair + 1) * PAIR)
        own, out = own_ref.at[part], out_ref.at[part]
        if not base <= pair < base + arrived_pairs:
            out[...] = own[...]
            continue
        arrived = arrived_ref.at[(pair - base) * PAIR : (pair - base + 1) * PAIR]
        shares, level = blend([unpack_stats(ref[2 * BODY : PAIR, :]) for ref in (arrived, own)])
        values = [mix(shares, (arrived, own), second * BODY, second * SECOND) for second in range(2)]
        for second in range(2):
            for index in range(COLS):
                row = second * BODY + tile_start(index)
                out[row : row + HALF, :] = values[second][index].astype(BF16)
        out[2 * BODY : PAIR, :] = pack_stats(level)


def merge(arrived, own, base):
    return pl.pallas_call(
        functools.partial(merge_kernel, base),
        out_shape=jax.ShapeDtypeStruct(own.shape, BF16),
        in_specs=[IN_VMEM, IN_VMEM],
        out_specs=IN_VMEM,
        compiler_params=params(),
        cost_estimate=cost(0, 6 * own.size),
    )(arrived, own)


def gather_kernel(base, ahead_ref, behind_ref, own_ref, *outs):
    for pair in range(len(outs) // 2):
        part = slice((base + pair) * PAIR, (base + pair + 1) * PAIR)
        sources = [ref.at[part] for ref in (own_ref, ahead_ref, behind_ref)]
        shares, level = blend([unpack_stats(ref[2 * BODY : PAIR, :]) for ref in sources])
        values = [mix(shares, sources, second * BODY, second * SECOND) for second in range(2)]
        for second in range(2):
            out = outs[2 * pair + second]
            for index in range(COLS):
                row = tile_start(index)
                out[row : row + HALF, :] = values[second][index].astype(BF16)
            here = pltpu.roll(level, LANES - SECOND, 1) if second else level
            out[BODY:LONE, :] = pack_stats(here)


def gather(ahead, behind, own, base, pairs):
    return pl.pallas_call(
        functools.partial(gather_kernel, base),
        out_shape=[jax.ShapeDtypeStruct((LONE, HD), BF16)] * (2 * pairs),
        in_specs=[IN_VMEM] * 3,
        out_specs=[IN_VMEM] * (2 * pairs),
        compiler_params=params(),
        cost_estimate=cost(0, 8 * pairs * PAIR * HD),
    )(ahead, behind, own)


def final_kernel(first, early, place_ref, *refs):
    earlier, parts = refs[:early], refs[early:-4]
    new_ref, level_ref, out_ref, rows_ref = refs[-4:]
    for number, part in enumerate(parts):
        d = first + number
        shares, _ = blend([unpack_stats(part[BODY:LONE, :]), level_ref[d]])
        for index, tile in enumerate(mix(shares, (part, new_ref.at[d]), 0, 0)):
            row = tile_start(index)
            rows_ref[number, row : row + HALF, :] = tile
    for number in range(len(parts)):
        row = place_ref[0] ^ (first + number) if early else number
        for head in range(KVH * GQ):
            tile = rows_ref[number, head * STEPS : (head + 1) * STEPS, :]
            out_ref[row, :, head * HD : (head + 1) * HD] = tile.astype(BF16)
    for ref in earlier:
        for d in range(ref.shape[0]):
            out_ref[place_ref[0] ^ d] = ref[d]


def final(place, parts, first, new_out, new_level, earlier=()):
    requests = len(parts) + sum(e.shape[0] for e in earlier)
    return pl.pallas_call(
        functools.partial(final_kernel, first, len(earlier)),
        out_shape=jax.ShapeDtypeStruct((requests, STEPS, KVH * GQ * HD), BF16),
        in_specs=[IN_SMEM] + [IN_VMEM] * (len(earlier) + len(parts) + 2),
        out_specs=IN_VMEM,
        scratch_shapes=[pltpu.VMEM((len(parts), BODY, HD), F32)],
        compiler_params=params(),
        cost_estimate=cost(0, len(parts) * BODY * HD * 8),
    )(place, *earlier, *parts, new_out, new_level)


def ring_order(owners):
    return list(range(0, owners, 2)) + list(range(owners - 1, 0, -2))


def per_device(queries, new_kv, kv_cache, page_owner, page_index, lengths):
    groups = lax.axis_size("grp")
    owners = lax.axis_size("cache")
    requests = queries.shape[0]
    assert requests == groups and requests % 4 == 0 and owners <= LANES
    reach = owners // 2
    order = ring_order(owners)
    forward = [(order[i], order[(i + 1) % owners]) for i in range(owners)]
    backward = [(b, a) for a, b in forward]
    place = jnp.stack([lax.axis_index("grp"), lax.axis_index("cache")]).astype(jnp.int32)

    def swap(array, d):
        return lax.ppermute(array, "grp", [(g, g ^ d) for g in range(groups)]) if d else array

    rows = relayout(place, queries)
    visits = [rows[0]] + [None] * (groups - 1)
    for d in range(groups - 1, 0, -1):
        visits[d] = swap(rows[d], d)
    new_out, new_level = new_tokens(place, rows, new_kv)
    lists = page_lists(page_owner, page_index, lengths)

    cut = requests // 2
    slots = [list(range(cut)), list(range(cut, requests))]
    owned = functools.partial(items, place, kv_cache, visitors=requests)

    def exchange(both, half, last=False):
        below = lax.ppermute(both[0], "cache", forward) if half == 0 or not last else None
        above = lax.ppermute(both[1], "cache", backward) if half == 1 or not last else None
        return (below, above) if last else lax.optimization_barrier((below, above))

    first = payload(lists, visits[:cut])
    halves = [exchange((first, first), 0)]
    second = payload(lists, visits[cut:], [touch(kv_cache, first), *halves[0]])
    halves.append(exchange((second, second), 1))
    parts = {0: owned([first, second], slots)}
    for step in range(1, reach):
        parts[-step] = owned([halves[0][0], halves[1][0]], slots)
        parts[step] = owned([halves[0][1], halves[1][1]], slots)
        halves = [exchange(halves[half], half, step == reach - 1) for half in range(2)]

    ahead, behind = owned([halves[0][0]], slots[:1]), owned([halves[1][1]], slots[1:])
    for step in range(reach - 1, -1, -1):
        ahead = lax.ppermute(ahead, "cache", forward)
        behind = lax.ppermute(behind, "cache", backward)
        if step > 0:
            base = cut // 2 if step == reach - 1 else 0
            ahead, behind = merge(ahead, parts[step], 0), merge(behind, parts[-step], base)
    back = gather(ahead, behind, parts[0], cut // 2, cut // 2)
    front = gather(ahead, behind, parts[0], 0, cut // 2)
    home = [swap(part, d) for d, part in enumerate(list(front) + list(back))]
    early = final(place, home[:cut], 0, new_out, new_level)
    return final(place, home[cut:], cut, new_out, new_level, [early])


def solution(mesh):
    in_specs = (
        P(("grp", "cache"), None, None),
        P(("grp", "cache"), None, None),
        P(("grp", "cache"), None, None),
        P(("grp", "cache"), None),
        P(("grp", "cache"), None, None),
        P(("grp", "cache")),
    )
    out_specs = P(("grp", "cache"), None, None)
    return jax.shard_map(
        per_device, mesh=mesh, in_specs=in_specs, out_specs=out_specs, check_vma=False
    )
```

```python
import functools
import math

import jax
import jax.numpy as jnp
from jax import lax
from jax.experimental import pallas as pl
from jax.experimental.pallas import tpu as pltpu
from jax.sharding import PartitionSpec as P

KVH = 8
HD = 128
GQ = 8
STEPS = 4
PAGE = 128
SEL = 4

LANES = 128
ROWS = GQ * STEPS
HALF = 16
BODY = KVH * ROWS
COLS = BODY // HALF
SECOND = 3 * COLS
PAIR = 2 * BODY + HALF
LONE = BODY + HALF
EMPTY = -1e30
SCALE = math.log2(math.e) / math.sqrt(HD)
VMEM_BYTES = 24 * 1024 * 1024
BF16 = jnp.bfloat16
F32 = jnp.float32
IN_VMEM = pl.BlockSpec(memory_space=pltpu.VMEM)
IN_SMEM = pl.BlockSpec(memory_space=pltpu.SMEM)


def params():
    return pltpu.CompilerParams(vmem_limit_bytes=VMEM_BYTES)


def cost(flops, moved):
    return pl.CostEstimate(flops=flops, bytes_accessed=moved, transcendentals=0)


def list_rows(requests):
    return -(-2 * requests // HALF) * HALF


def lane_ids(rows=HALF):
    return lax.broadcasted_iota(jnp.int32, (rows, LANES), 1)


def pack_stats(stats):
    lanes = lane_ids()
    used = (lanes < COLS) | ((lanes >= SECOND) & (lanes < SECOND + COLS))
    stats = jnp.where(used, stats, 0.0)
    high = stats.astype(BF16).astype(F32)
    rest = stats - high
    middle = rest.astype(BF16).astype(F32)
    low = rest - middle
    return (high + pltpu.roll(middle, COLS, 1) + pltpu.roll(low, 2 * COLS, 1)).astype(BF16)


def unpack_stats(tile):
    tile = tile.astype(F32)
    return tile + pltpu.roll(tile, LANES - COLS, 1) + pltpu.roll(tile, LANES - 2 * COLS, 1)


def tile_start(index):
    half, head = divmod(index, KVH)
    return head * ROWS + half * HALF


def by_lane(columns):
    lanes = lane_ids()
    tile = jnp.zeros((HALF, LANES), F32)
    for head, values in enumerate(columns):
        for half in range(ROWS // HALF):
            part = values[half * HALF : (half + 1) * HALF, :]
            tile = jnp.where(lanes == half * KVH + head, part, tile)
    return tile


def attend(queries, keys, values, usable):
    across = (((1,), (1,)), ((), ()))
    along = (((1,), (0,)), ((), ()))
    ones = jnp.ones(values[0].shape, BF16)
    scores = [lax.dot_general(q, k, across, preferred_element_type=F32) for q, k in zip(queries, keys)]
    scores = [jnp.where(usable, s * SCALE, EMPTY) for s in scores]
    tops = [jnp.max(s, axis=1, keepdims=True) for s in scores]
    weights = [jnp.exp2(s - t).astype(BF16) for s, t in zip(scores, tops)]
    both = [
        lax.dot_general(w, jnp.concatenate([v, ones], axis=1), along, preferred_element_type=F32)
        for w, v in zip(weights, values)
    ]
    mixed, totals = [b[:, :HD] for b in both], [b[:, HD:] for b in both]
    level = by_lane(tops) + jnp.log2(jnp.maximum(by_lane(totals), 1.0))
    return [m / t for m, t in zip(mixed, totals)], level


def relayout_kernel(place_ref, queries_ref, *outs):
    for d, out in enumerate(outs):
        values = queries_ref[place_ref[0] ^ d].astype(F32)
        for head in range(KVH):
            first = head * GQ
            parts = [values[:, (first + g) * HD : (first + g + 1) * HD] for g in range(GQ)]
            out[head * ROWS : (head + 1) * ROWS, :] = jnp.concatenate(parts, axis=0).astype(BF16)


def relayout(place, queries):
    groups = queries.shape[0]
    return pl.pallas_call(
        relayout_kernel,
        out_shape=[jax.ShapeDtypeStruct((BODY, HD), BF16)] * groups,
        in_specs=[IN_SMEM, IN_VMEM],
        out_specs=[IN_VMEM] * groups,
        compiler_params=params(),
        cost_estimate=cost(0, 4 * queries.size),
    )(place, queries)


def new_kernel(place_ref, *refs):
    queries, (new_ref, out_ref, level_ref) = refs[:-3], refs[-3:]
    step = lax.broadcasted_iota(jnp.int32, (ROWS, STEPS), 0) % STEPS
    usable = lax.broadcasted_iota(jnp.int32, (ROWS, STEPS), 1) <= step
    for d, query in enumerate(queries):
        new = new_ref[place_ref[0] ^ d]
        heads = [new[:, head * HD : (head + 1) * HD] for head in range(2 * KVH)]
        rows = [query[head * ROWS : (head + 1) * ROWS, :] for head in range(KVH)]
        mixed, level = attend(rows, heads[:KVH], heads[KVH:], usable)
        for head, values in enumerate(mixed):
            out_ref[d, head * ROWS : (head + 1) * ROWS, :] = values
        level_ref[d] = level


def new_tokens(place, queries, new_kv):
    groups = len(queries)
    return pl.pallas_call(
        new_kernel,
        out_shape=[
            jax.ShapeDtypeStruct((groups, BODY, HD), F32),
            jax.ShapeDtypeStruct((groups, HALF, LANES), F32),
        ],
        in_specs=[IN_SMEM] + [IN_VMEM] * (groups + 1),
        out_specs=[IN_VMEM, IN_VMEM],
        compiler_params=params(),
        cost_estimate=cost(groups * KVH * 4 * ROWS * HD * HD, groups * BODY * HD * 6),
    )(place, *queries, new_kv)


def page_lists(page_owner, page_index, lengths):
    lanes = jnp.arange(LANES, dtype=jnp.int32)[None, None, :]
    counts = jnp.clip(lengths[:, None] - jnp.arange(SEL, dtype=jnp.int32)[None, :] * PAGE, 0, PAGE)
    named = page_owner[:, :, None] == lanes
    return (
        jnp.sum(jnp.where(named, counts[:, :, None], 0), axis=1),
        jnp.sum(jnp.where(named, page_index, 0), axis=1),
    )


def payload_kernel(counts_ref, pages_ref, *refs):
    visits, out = refs[:-1], refs[-1]
    for number, visit in enumerate(visits):
        out[number * BODY : (number + 1) * BODY, :] = visit[...]
    tables = [counts_ref[...].astype(F32), pages_ref[...].astype(F32)]
    short = out.shape[0] - len(visits) * BODY - 2 * tables[0].shape[0]
    if short:
        tables.append(jnp.zeros((short, LANES), F32))
    out[len(visits) * BODY :, :] = jnp.concatenate(tables, axis=0).astype(BF16)


def payload(lists, visits):
    rows = len(visits) * BODY + list_rows(lists[0].shape[0])
    return pl.pallas_call(
        payload_kernel,
        out_shape=jax.ShapeDtypeStruct((rows, HD), BF16),
        in_specs=[IN_VMEM] * (2 + len(visits)),
        out_specs=IN_VMEM,
        compiler_params=params(),
        cost_estimate=cost(0, 4 * rows * HD),
    )(*lists, *visits)


def join_kernel(count, *refs):
    out, start = refs[-1], 0
    for ref in refs[:count]:
        out[start : start + ref.shape[0], :] = ref[...]
        start += ref.shape[0]


def join(arrays, after):
    rows = sum(array.shape[0] for array in arrays)
    return pl.pallas_call(
        functools.partial(join_kernel, len(arrays)),
        out_shape=jax.ShapeDtypeStruct((rows, HD), BF16),
        in_specs=[IN_VMEM] * (len(arrays) + len(after)),
        out_specs=IN_VMEM,
        compiler_params=params(),
        cost_estimate=cost(0, 4 * rows * HD),
    )(*arrays, *after)


def touch_kernel(after_ref, cache_ref, out_ref):
    out_ref[...] = cache_ref[0, :HALF, :HD]


def touch(kv_cache, after):
    return pl.pallas_call(
        touch_kernel,
        out_shape=jax.ShapeDtypeStruct((HALF, HD), BF16),
        in_specs=[IN_VMEM, IN_VMEM],
        out_specs=IN_VMEM,
        compiler_params=params(),
        cost_estimate=cost(0, 2 * HALF * HD),
    )(after, kv_cache)


def item_kernel(slots, visitors, place_ref, cache_ref, *refs):
    sides = len(slots)
    arrays, (out_ref, level_ref, code_ref) = refs[:-3], refs[-3:]
    each = len(slots[0])
    unit = sum(ref.shape[0] for ref in arrays) // sides
    query_refs = [ref.at[at : at + unit] for ref in arrays for at in range(0, ref.shape[0], unit)]
    for side, query_ref in enumerate(query_refs):
        lists = query_ref.shape[0] - each * BODY
        rows = lax.broadcasted_iota(jnp.int32, (lists, LANES), 0)
        table = query_ref[each * BODY :, :].astype(F32)
        table = jnp.where(lane_ids(lists) == place_ref[1], table, 0.0)
        for number, slot in enumerate(slots[side]):
            row = place_ref[0] ^ slot
            code = jnp.where(rows == row, table, jnp.where(rows == row + visitors, table * 256.0, 0.0))
            code_ref[side * each + number] = jnp.sum(code).astype(jnp.int32)
    tokens = lax.broadcasted_iota(jnp.int32, (ROWS, PAGE), 1)

    def one(side, number):
        entry = side * each + number
        query_ref = query_refs[side]
        code = code_ref[entry]
        count, page = code & 255, code >> 8
        start = number * BODY
        out = (entry // 2) * PAIR + (entry % 2) * BODY

        @pl.when(count > 0)
        def _():
            queries = [query_ref[pl.ds(pl.multiple_of(start + h * ROWS, HALF), ROWS), :] for h in range(KVH)]
            keys = [cache_ref[page, :, h * HD : (h + 1) * HD] for h in range(KVH)]
            values = [cache_ref[page, :, (KVH + h) * HD : (KVH + h + 1) * HD] for h in range(KVH)]
            mixed, level = attend(queries, keys, values, tokens < count)
            for head, part in enumerate(mixed):
                out_ref[pl.ds(pl.multiple_of(out + head * ROWS, HALF), ROWS), :] = part.astype(BF16)
            level_ref[entry] = level

        @pl.when(count <= 0)
        def _():
            out_ref[pl.ds(pl.multiple_of(out, HALF), BODY), :] = jnp.zeros((BODY, HD), BF16)
            level_ref[entry] = jnp.full((HALF, LANES), EMPTY, F32)

    for side in range(sides):

        @pl.loop(0, each)
        def _(number):
            one(side, number)

    lanes = lane_ids()
    for pair in range(sides * each // 2):
        level = jnp.where(lanes < COLS, level_ref[2 * pair], pltpu.roll(level_ref[2 * pair + 1], SECOND, 1))
        start = pair * PAIR + 2 * BODY
        out_ref[start : start + HALF, :] = pack_stats(level)


def items(place, kv_cache, payloads, slots, visitors):
    count = sum(len(row) for row in slots)
    return pl.pallas_call(
        functools.partial(item_kernel, slots, visitors),
        out_shape=jax.ShapeDtypeStruct((count // 2 * PAIR, HD), BF16),
        in_specs=[IN_SMEM] + [IN_VMEM] * (1 + len(payloads)),
        out_specs=IN_VMEM,
        scratch_shapes=[pltpu.VMEM((count, HALF, LANES), F32), pltpu.SMEM((count,), jnp.int32)],
        compiler_params=params(),
        cost_estimate=cost(count * KVH * 4 * ROWS * HD * PAGE, count * PAGE * kv_cache.shape[2] * 2),
    )(place, kv_cache, *payloads)


def blend(levels):
    peak = functools.reduce(jnp.maximum, levels)
    shares = [jnp.exp2(level - peak) for level in levels]
    total = functools.reduce(jnp.add, shares)
    return [share / total for share in shares], peak + jnp.log2(total)


def mix(shares, refs, start, first_lane):
    values = []
    for index in range(COLS):
        row, lane = start + tile_start(index), first_lane + index
        tiles = [ref[row : row + HALF, :].astype(F32) for ref in refs]
        total = tiles[0]
        for share, tile in zip(shares[1:], tiles[1:]):
            total = total + share[:, lane : lane + 1] * (tile - tiles[0])
        values.append(total)
    return values


def merge_kernel(base, arrived_ref, own_ref, *outs):
    arrived_pairs = arrived_ref.shape[0] // PAIR
    each = outs[0].shape[0] // PAIR
    for pair in range(own_ref.shape[0] // PAIR):
        own = own_ref.at[pair * PAIR : (pair + 1) * PAIR]
        out = outs[pair // each].at[pair % each * PAIR : (pair % each + 1) * PAIR]
        if not base <= pair < base + arrived_pairs:
            out[...] = own[...]
            continue
        arrived = arrived_ref.at[(pair - base) * PAIR : (pair - base + 1) * PAIR]
        shares, level = blend([unpack_stats(ref[2 * BODY : PAIR, :]) for ref in (arrived, own)])
        values = [mix(shares, (arrived, own), second * BODY, second * SECOND) for second in range(2)]
        for second in range(2):
            for index in range(COLS):
                row = second * BODY + tile_start(index)
                out[row : row + HALF, :] = values[second][index].astype(BF16)
        out[2 * BODY : PAIR, :] = pack_stats(level)


def merge(arrived, own, base, outs=1):
    rows = own.shape[0] // outs
    return pl.pallas_call(
        functools.partial(merge_kernel, base),
        out_shape=[jax.ShapeDtypeStruct((rows, HD), BF16)] * outs,
        in_specs=[IN_VMEM, IN_VMEM],
        out_specs=[IN_VMEM] * outs,
        compiler_params=params(),
        cost_estimate=cost(0, 6 * own.size),
    )(arrived, own)


def gather_kernel(base, ahead_ref, behind_ref, own_ref, *outs):
    for pair in range(len(outs) // 2):
        part = slice(pair * PAIR, (pair + 1) * PAIR)
        sources = [own_ref.at[(base + pair) * PAIR : (base + pair + 1) * PAIR], ahead_ref.at[part], behind_ref.at[part]]
        shares, level = blend([unpack_stats(ref[2 * BODY : PAIR, :]) for ref in sources])
        values = [mix(shares, sources, second * BODY, second * SECOND) for second in range(2)]
        for second in range(2):
            out = outs[2 * pair + second]
            for index in range(COLS):
                row = tile_start(index)
                out[row : row + HALF, :] = values[second][index].astype(BF16)
            here = pltpu.roll(level, LANES - SECOND, 1) if second else level
            out[BODY:LONE, :] = pack_stats(here)


def gather(ahead, behind, own, base):
    pairs = ahead.shape[0] // PAIR
    return pl.pallas_call(
        functools.partial(gather_kernel, base),
        out_shape=[jax.ShapeDtypeStruct((LONE, HD), BF16)] * (2 * pairs),
        in_specs=[IN_VMEM] * 3,
        out_specs=[IN_VMEM] * (2 * pairs),
        compiler_params=params(),
        cost_estimate=cost(0, 8 * pairs * PAIR * HD),
    )(ahead, behind, own)


def final_kernel(first, early, place_ref, *refs):
    earlier, parts = refs[:early], refs[early:-4]
    new_ref, level_ref, out_ref, rows_ref = refs[-4:]
    for number, part in enumerate(parts):
        d = first + number
        shares, _ = blend([unpack_stats(part[BODY:LONE, :]), level_ref[d]])
        for index, tile in enumerate(mix(shares, (part, new_ref.at[d]), 0, 0)):
            row = tile_start(index)
            rows_ref[number, row : row + HALF, :] = tile
    for number in range(len(parts)):
        row = place_ref[0] ^ (first + number) if early else number
        for head in range(KVH * GQ):
            tile = rows_ref[number, head * STEPS : (head + 1) * STEPS, :]
            out_ref[row, :, head * HD : (head + 1) * HD] = tile.astype(BF16)
    for ref in earlier:
        for d in range(ref.shape[0]):
            out_ref[place_ref[0] ^ (len(parts) + d)] = ref[d]


def final(place, parts, first, new_out, new_level, earlier=()):
    requests = len(parts) + sum(e.shape[0] for e in earlier)
    return pl.pallas_call(
        functools.partial(final_kernel, first, len(earlier)),
        out_shape=jax.ShapeDtypeStruct((requests, STEPS, KVH * GQ * HD), BF16),
        in_specs=[IN_SMEM] + [IN_VMEM] * (len(earlier) + len(parts) + 2),
        out_specs=IN_VMEM,
        scratch_shapes=[pltpu.VMEM((len(parts), BODY, HD), F32)],
        compiler_params=params(),
        cost_estimate=cost(0, len(parts) * BODY * HD * 8),
    )(place, *earlier, *parts, new_out, new_level)


def ring_order(owners):
    return list(range(0, owners, 2)) + list(range(owners - 1, 0, -2))


def per_device(queries, new_kv, kv_cache, page_owner, page_index, lengths):
    groups = lax.axis_size("grp")
    owners = lax.axis_size("cache")
    requests = queries.shape[0]
    assert requests == groups and requests % 4 == 0 and owners <= LANES
    reach = owners // 2
    order = ring_order(owners)
    forward = [(order[i], order[(i + 1) % owners]) for i in range(owners)]
    backward = [(b, a) for a, b in forward]
    place = jnp.stack([lax.axis_index("grp"), lax.axis_index("cache")]).astype(jnp.int32)

    def swap(array, d):
        return lax.ppermute(array, "grp", [(g, g ^ d) for g in range(groups)]) if d else array

    rows = relayout(place, queries)
    visits = [rows[0]] + [None] * (groups - 1)
    for d in range(groups - 1, 0, -1):
        visits[d] = swap(rows[d], d)
    new_out, new_level = new_tokens(place, rows, new_kv)
    lists = page_lists(page_owner, page_index, lengths)

    cut = requests // 2
    slots = [list(range(cut)), list(range(cut, requests))]
    owned = functools.partial(items, place, kv_cache, visitors=requests)

    def up(array):
        return lax.ppermute(array, "cache", forward)

    def down(array):
        return lax.ppermute(array, "cache", backward)

    def after(array, *others):
        return lax.optimization_barrier((array, others))[0]

    blocks = [payload(lists, visits[:cut])]
    front = up(blocks[0])
    blocks.append(payload(lists, visits[cut:]))
    below = join([front, up(after(blocks[1], front))], [touch(kv_cache, blocks[1])])
    above = down(join(blocks, []))
    parts = {0: owned(blocks, slots)}
    unit = blocks[0].shape[0]
    for step in range(1, reach):
        last = step == reach - 1
        parts[-step] = owned([below], slots)
        parts[step] = owned([above], slots)
        ready = [] if step == 1 else [parts[step - 1], parts[0]]
        below, above = after(below, *ready), after(above, parts[-step])
        below, above = up(below[:unit] if last else below), down(above[unit:] if last else above)

    ahead, behind = [owned([below], slots[:1])], [owned([above], slots[1:])]
    for step in range(reach - 1, 0, -1):
        base = cut // 2 if step == reach - 1 else 0
        outs = 2 if step == 1 else 1
        own = after(parts[step], new_level) if step == 1 else parts[step]
        ahead = merge(up(ahead[0]), own, 0, outs)
        behind = merge(down(behind[0]), parts[-step], base, outs)
    back = gather(up(ahead[1]), down(behind[1]), parts[0], cut // 2)
    front = gather(up(ahead[0]), down(behind[0]), after(parts[0], *back), 0)
    home = [swap(part, d) for d, part in enumerate(front)]
    home = home + [swap(part, cut + d) for d, part in enumerate(back)]
    early = final(place, home[cut:], cut, new_out, new_level)
    return final(place, home[:cut], 0, new_out, new_level, [early])


def solution(mesh):
    in_specs = (
        P(("grp", "cache"), None, None),
        P(("grp", "cache"), None, None),
        P(("grp", "cache"), None, None),
        P(("grp", "cache"), None),
        P(("grp", "cache"), None, None),
        P(("grp", "cache")),
    )
    out_specs = P(("grp", "cache"), None, None)
    return jax.shard_map(
        per_device, mesh=mesh, in_specs=in_specs, out_specs=out_specs, check_vma=False
    )
```

```python
import functools
import math

import jax
import jax.numpy as jnp
from jax import lax
from jax.experimental import pallas as pl
from jax.experimental.pallas import tpu as pltpu
from jax.sharding import PartitionSpec as P

KVH = 8
HD = 128
GQ = 8
STEPS = 4
PAGE = 128
SEL = 4

LANES = 128
ROWS = GQ * STEPS
HALF = 16
BODY = KVH * ROWS
COLS = BODY // HALF
SECOND = 3 * COLS
PAIR = 2 * BODY + HALF
LONE = BODY + HALF
EMPTY = -1e30
SCALE = math.log2(math.e) / math.sqrt(HD)
VMEM_BYTES = 24 * 1024 * 1024
BF16 = jnp.bfloat16
F32 = jnp.float32
IN_VMEM = pl.BlockSpec(memory_space=pltpu.VMEM)
IN_SMEM = pl.BlockSpec(memory_space=pltpu.SMEM)


def params():
    return pltpu.CompilerParams(vmem_limit_bytes=VMEM_BYTES)


def cost(flops, moved):
    return pl.CostEstimate(flops=flops, bytes_accessed=moved, transcendentals=0)


def list_rows(requests):
    return -(-2 * requests // HALF) * HALF


def lane_ids(rows=HALF):
    return lax.broadcasted_iota(jnp.int32, (rows, LANES), 1)


def pack_stats(stats):
    lanes = lane_ids()
    used = (lanes < COLS) | ((lanes >= SECOND) & (lanes < SECOND + COLS))
    stats = jnp.where(used, stats, 0.0)
    high = stats.astype(BF16).astype(F32)
    rest = stats - high
    middle = rest.astype(BF16).astype(F32)
    low = rest - middle
    return (high + pltpu.roll(middle, COLS, 1) + pltpu.roll(low, 2 * COLS, 1)).astype(BF16)


def unpack_stats(tile):
    tile = tile.astype(F32)
    return tile + pltpu.roll(tile, LANES - COLS, 1) + pltpu.roll(tile, LANES - 2 * COLS, 1)


def tile_start(index):
    half, head = divmod(index, KVH)
    return head * ROWS + half * HALF


def by_lane(columns, first=0):
    lanes = lane_ids() - first
    tile = jnp.zeros((HALF, LANES), F32)
    for head, values in enumerate(columns):
        for half in range(ROWS // HALF):
            part = values[half * HALF : (half + 1) * HALF, :]
            tile = jnp.where(lanes == half * KVH + head, part, tile)
    return tile


def attend(queries, keys, values, usable, first=0):
    across = (((1,), (1,)), ((), ()))
    along = (((1,), (0,)), ((), ()))
    ones = jnp.ones(values[0].shape, BF16)
    scores = [lax.dot_general(q, k, across, preferred_element_type=F32) for q, k in zip(queries, keys)]
    scores = [jnp.where(usable, s * SCALE, EMPTY) for s in scores]
    tops = [jnp.max(s, axis=1, keepdims=True) for s in scores]
    weights = [jnp.exp2(s - t).astype(BF16) for s, t in zip(scores, tops)]
    both = [
        lax.dot_general(w, jnp.concatenate([v, ones], axis=1), along, preferred_element_type=F32)
        for w, v in zip(weights, values)
    ]
    mixed, totals = [b[:, :HD] for b in both], [b[:, HD:] for b in both]
    level = by_lane(tops, first) + jnp.log2(jnp.maximum(by_lane(totals, first), 1.0))
    return [m / t for m, t in zip(mixed, totals)], level


def relayout_kernel(place_ref, queries_ref, *outs):
    for d, out in enumerate(outs):
        values = queries_ref[place_ref[0] ^ d].astype(F32)
        for head in range(KVH):
            first = head * GQ
            parts = [values[:, (first + g) * HD : (first + g + 1) * HD] for g in range(GQ)]
            out[head * ROWS : (head + 1) * ROWS, :] = jnp.concatenate(parts, axis=0).astype(BF16)


def relayout(place, queries):
    groups = queries.shape[0]
    return pl.pallas_call(
        relayout_kernel,
        out_shape=[jax.ShapeDtypeStruct((BODY, HD), BF16)] * groups,
        in_specs=[IN_SMEM, IN_VMEM],
        out_specs=[IN_VMEM] * groups,
        compiler_params=params(),
        cost_estimate=cost(0, 4 * queries.size),
    )(place, queries)


def new_kernel(place_ref, *refs):
    queries, (new_ref, out_ref, level_ref) = refs[:-3], refs[-3:]
    step = lax.broadcasted_iota(jnp.int32, (ROWS, STEPS), 0) % STEPS
    usable = lax.broadcasted_iota(jnp.int32, (ROWS, STEPS), 1) <= step
    for d, query in enumerate(queries):
        new = new_ref[place_ref[0] ^ d]
        heads = [new[:, head * HD : (head + 1) * HD] for head in range(2 * KVH)]
        rows = [query[head * ROWS : (head + 1) * ROWS, :] for head in range(KVH)]
        mixed, level = attend(rows, heads[:KVH], heads[KVH:], usable)
        for head, values in enumerate(mixed):
            out_ref[d, head * ROWS : (head + 1) * ROWS, :] = values
        level_ref[d] = level


def new_tokens(place, queries, new_kv):
    groups = len(queries)
    return pl.pallas_call(
        new_kernel,
        out_shape=[
            jax.ShapeDtypeStruct((groups, BODY, HD), F32),
            jax.ShapeDtypeStruct((groups, HALF, LANES), F32),
        ],
        in_specs=[IN_SMEM] + [IN_VMEM] * (groups + 1),
        out_specs=[IN_VMEM, IN_VMEM],
        compiler_params=params(),
        cost_estimate=cost(groups * KVH * 4 * ROWS * HD * HD, groups * BODY * HD * 6),
    )(place, *queries, new_kv)


def page_lists(page_owner, page_index, lengths):
    lanes = jnp.arange(LANES, dtype=jnp.int32)[None, None, :]
    counts = jnp.clip(lengths[:, None] - jnp.arange(SEL, dtype=jnp.int32)[None, :] * PAGE, 0, PAGE)
    named = page_owner[:, :, None] == lanes
    return (
        jnp.sum(jnp.where(named, counts[:, :, None], 0), axis=1),
        jnp.sum(jnp.where(named, page_index, 0), axis=1),
    )


def payload_kernel(after, counts_ref, pages_ref, *refs):
    visits, out = refs[: len(refs) - 1 - after], refs[-1]
    for number, visit in enumerate(visits):
        out[number * BODY : (number + 1) * BODY, :] = visit[...]
    tables = [counts_ref[...].astype(F32), pages_ref[...].astype(F32)]
    short = out.shape[0] - len(visits) * BODY - 2 * tables[0].shape[0]
    if short:
        tables.append(jnp.zeros((short, LANES), F32))
    out[len(visits) * BODY :, :] = jnp.concatenate(tables, axis=0).astype(BF16)


def payload(lists, visits, after=()):
    rows = len(visits) * BODY + list_rows(lists[0].shape[0])
    return pl.pallas_call(
        functools.partial(payload_kernel, len(after)),
        out_shape=jax.ShapeDtypeStruct((rows, HD), BF16),
        in_specs=[IN_VMEM] * (2 + len(visits) + len(after)),
        out_specs=IN_VMEM,
        compiler_params=params(),
        cost_estimate=cost(0, 4 * rows * HD),
    )(*lists, *visits, *after)


def touch_kernel(after_ref, cache_ref, out_ref):
    out_ref[...] = cache_ref[0, :HALF, :HD]


def touch(kv_cache, after):
    return pl.pallas_call(
        touch_kernel,
        out_shape=jax.ShapeDtypeStruct((HALF, HD), BF16),
        in_specs=[IN_VMEM, IN_VMEM],
        out_specs=IN_VMEM,
        compiler_params=params(),
        cost_estimate=cost(0, 2 * HALF * HD),
    )(after, kv_cache)


def item_kernel(slots, visitors, place_ref, cache_ref, *refs):
    sides = len(slots)
    query_refs, out_refs, (level_ref, code_ref) = refs[:sides], refs[sides : 2 * sides], refs[2 * sides :]
    each = len(slots[0])
    for side, query_ref in enumerate(query_refs):
        lists = query_ref.shape[0] - each * BODY
        rows = lax.broadcasted_iota(jnp.int32, (lists, LANES), 0)
        table = query_ref[each * BODY :, :].astype(F32)
        table = jnp.where(lane_ids(lists) == place_ref[1], table, 0.0)
        for pair in range(each // 2):
            factor = jnp.zeros((lists, LANES), F32)
            for second in range(2):
                row = place_ref[0] ^ slots[side][2 * pair + second]
                factor = jnp.where(rows == row, float(4096**second), factor)
                factor = jnp.where(rows == row + visitors, float(256 * 4096**second), factor)
            code_ref[(side * each) // 2 + pair] = jnp.sum(table * factor).astype(jnp.int32)
    tokens = lax.broadcasted_iota(jnp.int32, (ROWS, PAGE), 1)

    def one(side, number):
        entry = side * each + number
        query_ref, out_ref = query_refs[side], out_refs[side]
        odd = number & 1
        code = code_ref[entry >> 1] >> (12 * odd)
        count, page = code & 255, (code >> 8) & 15
        start = number * BODY
        out = (number >> 1) * PAIR + odd * BODY
        first = odd * SECOND

        @pl.when(count > 0)
        def _():
            queries = [query_ref[pl.ds(pl.multiple_of(start + h * ROWS, HALF), ROWS), :] for h in range(KVH)]
            keys = [cache_ref[page, :, h * HD : (h + 1) * HD] for h in range(KVH)]
            values = [cache_ref[page, :, (KVH + h) * HD : (KVH + h + 1) * HD] for h in range(KVH)]
            mixed, level = attend(queries, keys, values, tokens < count, first)
            for head, part in enumerate(mixed):
                out_ref[pl.ds(pl.multiple_of(out + head * ROWS, HALF), ROWS), :] = part.astype(BF16)
            level_ref[entry] = level

        @pl.when(count <= 0)
        def _():
            out_ref[pl.ds(pl.multiple_of(out, HALF), BODY), :] = jnp.zeros((BODY, HD), BF16)
            lanes = lane_ids() - first
            level_ref[entry] = jnp.where((lanes >= 0) & (lanes < COLS), EMPTY, 0.0)

    for side in range(sides):

        @pl.loop(0, each)
        def _(number):
            one(side, number)

    for side, out_ref in enumerate(out_refs):
        for pair in range(each // 2):
            entry = side * each + 2 * pair
            start = pair * PAIR + 2 * BODY
            out_ref[start : start + HALF, :] = pack_stats(level_ref[entry] + level_ref[entry + 1])


def items(place, kv_cache, payloads, slots, visitors):
    count = sum(len(row) for row in slots)
    rows = len(slots[0]) // 2 * PAIR
    return pl.pallas_call(
        functools.partial(item_kernel, slots, visitors),
        out_shape=[jax.ShapeDtypeStruct((rows, HD), BF16)] * len(slots),
        in_specs=[IN_SMEM] + [IN_VMEM] * (1 + len(slots)),
        out_specs=[IN_VMEM] * len(slots),
        scratch_shapes=[pltpu.VMEM((count, HALF, LANES), F32), pltpu.SMEM((count // 2,), jnp.int32)],
        compiler_params=params(),
        cost_estimate=cost(count * KVH * 4 * ROWS * HD * PAGE, count * PAGE * kv_cache.shape[2] * 2),
    )(place, kv_cache, *payloads)


def blend(levels):
    peak = functools.reduce(jnp.maximum, levels)
    shares = [jnp.exp2(level - peak) for level in levels]
    total = functools.reduce(jnp.add, shares)
    return [share / total for share in shares], peak + jnp.log2(total)


def mix(shares, refs, start, first_lane):
    values = []
    for index in range(COLS):
        row, lane = start + tile_start(index), first_lane + index
        tiles = [ref[row : row + HALF, :].astype(F32) for ref in refs]
        total = tiles[0]
        for share, tile in zip(shares[1:], tiles[1:]):
            total = total + share[:, lane : lane + 1] * (tile - tiles[0])
        values.append(total)
    return values


def merge_kernel(arrived_ref, own_ref, out_ref):
    for pair in range(out_ref.shape[0] // PAIR):
        part = slice(pair * PAIR, (pair + 1) * PAIR)
        arrived, own, out = arrived_ref.at[part], own_ref.at[part], out_ref.at[part]
        shares, level = blend([unpack_stats(ref[2 * BODY : PAIR, :]) for ref in (arrived, own)])
        values = [mix(shares, (arrived, own), second * BODY, second * SECOND) for second in range(2)]
        for second in range(2):
            for index in range(COLS):
                row = second * BODY + tile_start(index)
                out[row : row + HALF, :] = values[second][index].astype(BF16)
        out[2 * BODY : PAIR, :] = pack_stats(level)


def merge(arrived, own):
    return pl.pallas_call(
        merge_kernel,
        out_shape=jax.ShapeDtypeStruct(own.shape, BF16),
        in_specs=[IN_VMEM, IN_VMEM],
        out_specs=IN_VMEM,
        compiler_params=params(),
        cost_estimate=cost(0, 6 * own.size),
    )(arrived, own)


def gather_kernel(ahead_ref, behind_ref, own_ref, *outs):
    for pair in range(len(outs) // 2):
        part = slice(pair * PAIR, (pair + 1) * PAIR)
        sources = [ref.at[part] for ref in (own_ref, ahead_ref, behind_ref)]
        shares, level = blend([unpack_stats(ref[2 * BODY : PAIR, :]) for ref in sources])
        values = [mix(shares, sources, second * BODY, second * SECOND) for second in range(2)]
        for second in range(2):
            out = outs[2 * pair + second]
            for index in range(COLS):
                row = tile_start(index)
                out[row : row + HALF, :] = values[second][index].astype(BF16)
            here = pltpu.roll(level, LANES - SECOND, 1) if second else level
            out[BODY:LONE, :] = pack_stats(here)


def gather(ahead, behind, own):
    pairs = own.shape[0] // PAIR
    return pl.pallas_call(
        gather_kernel,
        out_shape=[jax.ShapeDtypeStruct((LONE, HD), BF16)] * (2 * pairs),
        in_specs=[IN_VMEM] * 3,
        out_specs=[IN_VMEM] * (2 * pairs),
        compiler_params=params(),
        cost_estimate=cost(0, 8 * pairs * PAIR * HD),
    )(ahead, behind, own)


def final_kernel(first, early, place_ref, *refs):
    earlier, parts = refs[:early], refs[early:-4]
    new_ref, level_ref, out_ref, rows_ref = refs[-4:]
    for number, part in enumerate(parts):
        d = first + number
        shares, _ = blend([unpack_stats(part[BODY:LONE, :]), level_ref[d]])
        for index, tile in enumerate(mix(shares, (part, new_ref.at[d]), 0, 0)):
            row = tile_start(index)
            rows_ref[number, row : row + HALF, :] = tile
    for number in range(len(parts)):
        row = place_ref[0] ^ (first + number) if early else number
        for head in range(KVH * GQ):
            tile = rows_ref[number, head * STEPS : (head + 1) * STEPS, :]
            out_ref[row, :, head * HD : (head + 1) * HD] = tile.astype(BF16)
    for ref in earlier:
        for d in range(ref.shape[0]):
            out_ref[place_ref[0] ^ d] = ref[d]


def final(place, parts, first, new_out, new_level, earlier=()):
    requests = len(parts) + sum(e.shape[0] for e in earlier)
    return pl.pallas_call(
        functools.partial(final_kernel, first, len(earlier)),
        out_shape=jax.ShapeDtypeStruct((requests, STEPS, KVH * GQ * HD), BF16),
        in_specs=[IN_SMEM] + [IN_VMEM] * (len(earlier) + len(parts) + 2),
        out_specs=IN_VMEM,
        scratch_shapes=[pltpu.VMEM((len(parts), BODY, HD), F32)],
        compiler_params=params(),
        cost_estimate=cost(0, len(parts) * BODY * HD * 8),
    )(place, *earlier, *parts, new_out, new_level)


def ring_order(owners):
    return list(range(0, owners, 2)) + list(range(owners - 1, 0, -2))


def per_device(queries, new_kv, kv_cache, page_owner, page_index, lengths):
    groups = lax.axis_size("grp")
    owners = lax.axis_size("cache")
    requests = queries.shape[0]
    assert requests == groups and requests % 4 == 0 and owners <= LANES
    reach = owners // 2
    order = ring_order(owners)
    forward = [(order[i], order[(i + 1) % owners]) for i in range(owners)]
    backward = [(b, a) for a, b in forward]
    place = jnp.stack([lax.axis_index("grp"), lax.axis_index("cache")]).astype(jnp.int32)

    def swap(array, d):
        return lax.ppermute(array, "grp", [(g, g ^ d) for g in range(groups)]) if d else array

    rows = relayout(place, queries)
    visits = [rows[0]] + [None] * (groups - 1)
    for d in range(groups - 1, 0, -1):
        visits[d] = swap(rows[d], d)
    new_out, new_level = new_tokens(place, rows, new_kv)
    lists = page_lists(page_owner, page_index, lengths)

    cut = requests // 2
    slots = [list(range(cut)), list(range(cut, requests))]
    owned = functools.partial(items, place, kv_cache, visitors=requests)

    def up(array):
        return lax.ppermute(array, "cache", forward)

    def down(array):
        return lax.ppermute(array, "cache", backward)

    def after(array, *others):
        return lax.optimization_barrier((array, others))[0]

    blocks = [payload(lists, visits[:cut])]
    ahead, behind = up(blocks[0]), down(blocks[0])
    blocks.append(payload(lists, visits[cut:], [touch(kv_cache, blocks[0])]))
    second = after(blocks[1], ahead, behind)
    below, above, far = [ahead, up(second)], [behind, down(second)], [None, None]
    parts = {(half, 0): part for half, part in enumerate(owned(blocks, slots))}
    for step in range(1, reach + 1):
        for half in range(2):
            if step == reach:
                arrival = up(below[0]) if half == 0 else down(above[1])
                far[half] = owned([arrival], [slots[half]])[0]
                continue
            done = [parts[half, 0]] if step == 1 else [parts[half, 1 - step], parts[half, step - 1]]
            if step > 1:
                below[half], above[half] = up(below[half]), down(above[half])
            below[half], above[half] = after(below[half], *done), after(above[half], *done)
            parts[half, -step], parts[half, step] = owned([below[half], above[half]], [slots[half]] * 2)

    arrived = []
    for half in range(2):
        for move, sign in ((up, 1), (down, -1)):
            if half == (0 if sign == 1 else 1):
                chain, steps = far[half], range(reach - 1, -1, -1)
            else:
                chain, steps = parts[half, sign * (reach - 1)], range(reach - 2, -1, -1)
            for step in steps:
                chain = move(chain)
                if step > 0:
                    chain = merge(chain, parts[half, sign * step])
            arrived.append(chain)
    returned = gather(arrived[0], arrived[1], parts[0, 0]) + gather(arrived[2], arrived[3], parts[1, 0])
    home = [swap(part, d) for d, part in enumerate(returned)]
    early = final(place, home[:cut], 0, new_out, new_level)
    return final(place, home[cut:], cut, new_out, new_level, [early])


def solution(mesh):
    in_specs = (
        P(("grp", "cache"), None, None),
        P(("grp", "cache"), None, None),
        P(("grp", "cache"), None, None),
        P(("grp", "cache"), None),
        P(("grp", "cache"), None, None),
        P(("grp", "cache")),
    )
    out_specs = P(("grp", "cache"), None, None)
    return jax.shard_map(
        per_device, mesh=mesh, in_specs=in_specs, out_specs=out_specs, check_vma=False
    )
```

```python
import functools
import math

import jax
import jax.numpy as jnp
from jax import lax
from jax.experimental import pallas as pl
from jax.experimental.pallas import tpu as pltpu
from jax.sharding import PartitionSpec as P

KVH = 8
HD = 128
GQ = 8
STEPS = 4
PAGE = 128
SEL = 4

LANES = 128
ROWS = GQ * STEPS
HALF = 16
BODY = KVH * ROWS
COLS = BODY // HALF
SECOND = 3 * COLS
PAIR = 2 * BODY + HALF
LONE = BODY + HALF
EMPTY = -1e30
SCALE = math.log2(math.e) / math.sqrt(HD)
VMEM_BYTES = 24 * 1024 * 1024
BF16 = jnp.bfloat16
F32 = jnp.float32
IN_VMEM = pl.BlockSpec(memory_space=pltpu.VMEM)
IN_SMEM = pl.BlockSpec(memory_space=pltpu.SMEM)


def params():
    return pltpu.CompilerParams(vmem_limit_bytes=VMEM_BYTES)


def cost(flops, moved):
    return pl.CostEstimate(flops=flops, bytes_accessed=moved, transcendentals=0)


def list_rows(requests):
    return -(-2 * requests // HALF) * HALF


def lane_ids(rows=HALF):
    return lax.broadcasted_iota(jnp.int32, (rows, LANES), 1)


def pack_stats(stats):
    lanes = lane_ids()
    used = (lanes < COLS) | ((lanes >= SECOND) & (lanes < SECOND + COLS))
    stats = jnp.where(used, stats, 0.0)
    high = stats.astype(BF16).astype(F32)
    rest = stats - high
    middle = rest.astype(BF16).astype(F32)
    low = rest - middle
    return (high + pltpu.roll(middle, COLS, 1) + pltpu.roll(low, 2 * COLS, 1)).astype(BF16)


def unpack_stats(tile):
    tile = tile.astype(F32)
    return tile + pltpu.roll(tile, LANES - COLS, 1) + pltpu.roll(tile, LANES - 2 * COLS, 1)


def tile_start(index):
    half, head = divmod(index, KVH)
    return head * ROWS + half * HALF


def by_lane(columns, first=0):
    lanes = lane_ids() - first
    tile = jnp.zeros((HALF, LANES), F32)
    for head, values in enumerate(columns):
        for half in range(ROWS // HALF):
            part = values[half * HALF : (half + 1) * HALF, :]
            tile = jnp.where(lanes == half * KVH + head, part, tile)
    return tile


def attend(queries, keys, values, usable, first=0):
    across = (((1,), (1,)), ((), ()))
    along = (((1,), (0,)), ((), ()))
    ones = jnp.ones(values[0].shape, BF16)
    scores = [lax.dot_general(q, k, across, preferred_element_type=F32) for q, k in zip(queries, keys)]
    scores = [jnp.where(usable, s * SCALE, EMPTY) for s in scores]
    tops = [jnp.max(s, axis=1, keepdims=True) for s in scores]
    weights = [jnp.exp2(s - t).astype(BF16) for s, t in zip(scores, tops)]
    both = [
        lax.dot_general(w, jnp.concatenate([v, ones], axis=1), along, preferred_element_type=F32)
        for w, v in zip(weights, values)
    ]
    mixed, totals = [b[:, :HD] for b in both], [b[:, HD:] for b in both]
    level = by_lane(tops, first) + jnp.log2(jnp.maximum(by_lane(totals, first), 1.0))
    return [m / t for m, t in zip(mixed, totals)], level


def relayout_kernel(owners, place_ref, queries_ref, *outs):
    group = lax.div(place_ref[0], owners)
    for d, out in enumerate(outs):
        values = queries_ref[group ^ d].astype(F32)
        for head in range(KVH):
            first = head * GQ
            parts = [values[:, (first + g) * HD : (first + g + 1) * HD] for g in range(GQ)]
            out[head * ROWS : (head + 1) * ROWS, :] = jnp.concatenate(parts, axis=0).astype(BF16)


def relayout(place, owners, queries):
    groups = queries.shape[0]
    return pl.pallas_call(
        functools.partial(relayout_kernel, owners),
        out_shape=[jax.ShapeDtypeStruct((BODY, HD), BF16)] * groups,
        in_specs=[IN_SMEM, IN_VMEM],
        out_specs=[IN_VMEM] * groups,
        compiler_params=params(),
        cost_estimate=cost(0, 4 * queries.size),
    )(place, queries)


def new_kernel(owners, place_ref, *refs):
    group = lax.div(place_ref[0], owners)
    queries, (new_ref, out_ref, level_ref) = refs[:-3], refs[-3:]
    step = lax.broadcasted_iota(jnp.int32, (ROWS, STEPS), 0) % STEPS
    usable = lax.broadcasted_iota(jnp.int32, (ROWS, STEPS), 1) <= step
    for d, query in enumerate(queries):
        new = new_ref[group ^ d]
        heads = [new[:, head * HD : (head + 1) * HD] for head in range(2 * KVH)]
        rows = [query[head * ROWS : (head + 1) * ROWS, :] for head in range(KVH)]
        mixed, level = attend(rows, heads[:KVH], heads[KVH:], usable)
        for head, values in enumerate(mixed):
            out_ref[d, head * ROWS : (head + 1) * ROWS, :] = values
        level_ref[d] = level


def new_tokens(place, owners, queries, new_kv):
    groups = len(queries)
    return pl.pallas_call(
        functools.partial(new_kernel, owners),
        out_shape=[
            jax.ShapeDtypeStruct((groups, BODY, HD), F32),
            jax.ShapeDtypeStruct((groups, HALF, LANES), F32),
        ],
        in_specs=[IN_SMEM] + [IN_VMEM] * (groups + 1),
        out_specs=[IN_VMEM, IN_VMEM],
        compiler_params=params(),
        cost_estimate=cost(groups * KVH * 4 * ROWS * HD * HD, groups * BODY * HD * 6),
    )(place, *queries, new_kv)


def page_lists(page_owner, page_index, lengths):
    lanes = jnp.arange(LANES, dtype=jnp.int32)[None, None, :]
    counts = jnp.clip(lengths[:, None] - jnp.arange(SEL, dtype=jnp.int32)[None, :] * PAGE, 0, PAGE)
    named = page_owner[:, :, None] == lanes
    return (
        jnp.sum(jnp.where(named, counts[:, :, None], 0), axis=1),
        jnp.sum(jnp.where(named, page_index, 0), axis=1),
    )


def payload_kernel(after, counts_ref, pages_ref, *refs):
    visits, out = refs[: len(refs) - 1 - after], refs[-1]
    for number, visit in enumerate(visits):
        out[number * BODY : (number + 1) * BODY, :] = visit[...]
    tables = [counts_ref[...].astype(F32), pages_ref[...].astype(F32)]
    short = out.shape[0] - len(visits) * BODY - 2 * tables[0].shape[0]
    if short:
        tables.append(jnp.zeros((short, LANES), F32))
    out[len(visits) * BODY :, :] = jnp.concatenate(tables, axis=0).astype(BF16)


def payload(lists, visits, after=()):
    rows = len(visits) * BODY + list_rows(lists[0].shape[0])
    return pl.pallas_call(
        functools.partial(payload_kernel, len(after)),
        out_shape=jax.ShapeDtypeStruct((rows, HD), BF16),
        in_specs=[IN_VMEM] * (2 + len(visits) + len(after)),
        out_specs=IN_VMEM,
        compiler_params=params(),
        cost_estimate=cost(0, 4 * rows * HD),
    )(*lists, *visits, *after)


def touch_kernel(after_ref, cache_ref, out_ref):
    out_ref[...] = cache_ref[0, :HALF, :HD]


def touch(kv_cache, after):
    return pl.pallas_call(
        touch_kernel,
        out_shape=jax.ShapeDtypeStruct((HALF, HD), BF16),
        in_specs=[IN_VMEM, IN_VMEM],
        out_specs=IN_VMEM,
        compiler_params=params(),
        cost_estimate=cost(0, 2 * HALF * HD),
    )(after, kv_cache)


def item_kernel(slots, visitors, owners, place_ref, cache_ref, *refs):
    group, owner = lax.div(place_ref[0], owners), lax.rem(place_ref[0], owners)
    sides = len(slots)
    query_refs, out_refs, (level_ref, code_ref) = refs[:sides], refs[sides : 2 * sides], refs[2 * sides :]
    each = len(slots[0])
    for side, query_ref in enumerate(query_refs):
        lists = query_ref.shape[0] - each * BODY
        rows = lax.broadcasted_iota(jnp.int32, (lists, LANES), 0)
        table = query_ref[each * BODY :, :].astype(F32)
        table = jnp.where(lane_ids(lists) == owner, table, 0.0)
        for pair in range(each // 2):
            factor = jnp.zeros((lists, LANES), F32)
            for second in range(2):
                row = group ^ slots[side][2 * pair + second]
                factor = jnp.where(rows == row, float(4096**second), factor)
                factor = jnp.where(rows == row + visitors, float(256 * 4096**second), factor)
            code_ref[(side * each) // 2 + pair] = jnp.sum(table * factor).astype(jnp.int32)
    tokens = lax.broadcasted_iota(jnp.int32, (ROWS, PAGE), 1)

    def one(side, number):
        entry = side * each + number
        query_ref, out_ref = query_refs[side], out_refs[side]
        odd = number & 1
        code = code_ref[entry >> 1] >> (12 * odd)
        count, page = code & 255, (code >> 8) & 15
        start = number * BODY
        out = (number >> 1) * PAIR + odd * BODY
        first = odd * SECOND

        @pl.when(count > 0)
        def _():
            queries = [query_ref[pl.ds(pl.multiple_of(start + h * ROWS, HALF), ROWS), :] for h in range(KVH)]
            keys = [cache_ref[page, :, h * HD : (h + 1) * HD] for h in range(KVH)]
            values = [cache_ref[page, :, (KVH + h) * HD : (KVH + h + 1) * HD] for h in range(KVH)]
            mixed, level = attend(queries, keys, values, tokens < count, first)
            for head, part in enumerate(mixed):
                out_ref[pl.ds(pl.multiple_of(out + head * ROWS, HALF), ROWS), :] = part.astype(BF16)
            level_ref[entry] = level

        @pl.when(count <= 0)
        def _():
            out_ref[pl.ds(pl.multiple_of(out, HALF), BODY), :] = jnp.zeros((BODY, HD), BF16)
            lanes = lane_ids() - first
            level_ref[entry] = jnp.where((lanes >= 0) & (lanes < COLS), EMPTY, 0.0)

    for side in range(sides):

        @pl.loop(0, each)
        def _(number):
            one(side, number)

    for side, out_ref in enumerate(out_refs):
        for pair in range(each // 2):
            entry = side * each + 2 * pair
            start = pair * PAIR + 2 * BODY
            out_ref[start : start + HALF, :] = pack_stats(level_ref[entry] + level_ref[entry + 1])


def items(place, owners, kv_cache, payloads, slots, visitors):
    count = sum(len(row) for row in slots)
    rows = len(slots[0]) // 2 * PAIR
    return pl.pallas_call(
        functools.partial(item_kernel, slots, visitors, owners),
        out_shape=[jax.ShapeDtypeStruct((rows, HD), BF16)] * len(slots),
        in_specs=[IN_SMEM] + [IN_VMEM] * (1 + len(slots)),
        out_specs=[IN_VMEM] * len(slots),
        scratch_shapes=[pltpu.VMEM((count, HALF, LANES), F32), pltpu.SMEM((count // 2,), jnp.int32)],
        compiler_params=params(),
        cost_estimate=cost(count * KVH * 4 * ROWS * HD * PAGE, count * PAGE * kv_cache.shape[2] * 2),
    )(place, kv_cache, *payloads)


def blend(levels):
    peak = functools.reduce(jnp.maximum, levels)
    shares = [jnp.exp2(level - peak) for level in levels]
    total = functools.reduce(jnp.add, shares)
    return [share / total for share in shares], peak + jnp.log2(total)


def mix(shares, refs, start, first_lane):
    values = []
    for index in range(COLS):
        row, lane = start + tile_start(index), first_lane + index
        tiles = [ref[row : row + HALF, :].astype(F32) for ref in refs]
        total = tiles[0]
        for share, tile in zip(shares[1:], tiles[1:]):
            total = total + share[:, lane : lane + 1] * (tile - tiles[0])
        values.append(total)
    return values


def merge_kernel(arrived_ref, own_ref, out_ref):
    for pair in range(out_ref.shape[0] // PAIR):
        part = slice(pair * PAIR, (pair + 1) * PAIR)
        arrived, own, out = arrived_ref.at[part], own_ref.at[part], out_ref.at[part]
        shares, level = blend([unpack_stats(ref[2 * BODY : PAIR, :]) for ref in (arrived, own)])
        values = [mix(shares, (arrived, own), second * BODY, second * SECOND) for second in range(2)]
        for second in range(2):
            for index in range(COLS):
                row = second * BODY + tile_start(index)
                out[row : row + HALF, :] = values[second][index].astype(BF16)
        out[2 * BODY : PAIR, :] = pack_stats(level)


def merge(arrived, own):
    return pl.pallas_call(
        merge_kernel,
        out_shape=jax.ShapeDtypeStruct(own.shape, BF16),
        in_specs=[IN_VMEM, IN_VMEM],
        out_specs=IN_VMEM,
        compiler_params=params(),
        cost_estimate=cost(0, 6 * own.size),
    )(arrived, own)


def gather_kernel(ahead_ref, behind_ref, own_ref, *outs):
    for pair in range(len(outs) // 2):
        part = slice(pair * PAIR, (pair + 1) * PAIR)
        sources = [ref.at[part] for ref in (own_ref, ahead_ref, behind_ref)]
        shares, level = blend([unpack_stats(ref[2 * BODY : PAIR, :]) for ref in sources])
        values = [mix(shares, sources, second * BODY, second * SECOND) for second in range(2)]
        for second in range(2):
            out = outs[2 * pair + second]
            for index in range(COLS):
                row = tile_start(index)
                out[row : row + HALF, :] = values[second][index].astype(BF16)
            here = pltpu.roll(level, LANES - SECOND, 1) if second else level
            out[BODY:LONE, :] = pack_stats(here)


def gather(ahead, behind, own):
    pairs = own.shape[0] // PAIR
    return pl.pallas_call(
        gather_kernel,
        out_shape=[jax.ShapeDtypeStruct((LONE, HD), BF16)] * (2 * pairs),
        in_specs=[IN_VMEM] * 3,
        out_specs=[IN_VMEM] * (2 * pairs),
        compiler_params=params(),
        cost_estimate=cost(0, 8 * pairs * PAIR * HD),
    )(ahead, behind, own)


def final_kernel(first, early, owners, place_ref, *refs):
    earlier, parts = refs[:early], refs[early:-4]
    new_ref, level_ref, out_ref, rows_ref = refs[-4:]
    group = lax.div(place_ref[0], owners)
    for number, part in enumerate(parts):
        d = first + number
        shares, _ = blend([unpack_stats(part[BODY:LONE, :]), level_ref[d]])
        for index, tile in enumerate(mix(shares, (part, new_ref.at[d]), 0, 0)):
            row = tile_start(index)
            rows_ref[number, row : row + HALF, :] = tile
    for number in range(len(parts)):
        row = group ^ (first + number) if early else number
        for head in range(KVH * GQ):
            tile = rows_ref[number, head * STEPS : (head + 1) * STEPS, :]
            out_ref[row, :, head * HD : (head + 1) * HD] = tile.astype(BF16)
    for ref in earlier:
        for number in range(ref.shape[0]):
            out_ref[group ^ (len(parts) + number)] = ref[number]


def final(place, owners, parts, first, new_out, new_level, earlier=()):
    requests = len(parts) + sum(e.shape[0] for e in earlier)
    return pl.pallas_call(
        functools.partial(final_kernel, first, len(earlier), owners),
        out_shape=jax.ShapeDtypeStruct((requests, STEPS, KVH * GQ * HD), BF16),
        in_specs=[IN_SMEM] + [IN_VMEM] * (len(earlier) + len(parts) + 2),
        out_specs=IN_VMEM,
        scratch_shapes=[pltpu.VMEM((len(parts), BODY, HD), F32)],
        compiler_params=params(),
        cost_estimate=cost(0, len(parts) * BODY * HD * 8),
    )(place, *earlier, *parts, new_out, new_level)


def ring_order(owners):
    return list(range(0, owners, 2)) + list(range(owners - 1, 0, -2))


def per_device(queries, new_kv, kv_cache, page_owner, page_index, lengths):
    groups = lax.axis_size("grp")
    owners = lax.axis_size("cache")
    requests = queries.shape[0]
    assert requests == groups and requests % 4 == 0 and owners <= LANES
    reach = owners // 2
    order = ring_order(owners)
    forward = [(order[i], order[(i + 1) % owners]) for i in range(owners)]
    backward = [(b, a) for a, b in forward]
    place = jnp.reshape(lax.axis_index(("grp", "cache")), (1,)).astype(jnp.int32)

    def swap(array, d):
        return lax.ppermute(array, "grp", [(g, g ^ d) for g in range(groups)]) if d else array

    rows = relayout(place, owners, queries)
    visits = [rows[0]] + [None] * (groups - 1)
    for d in range(groups - 1, 0, -1):
        visits[d] = swap(rows[d], d)
    new_out, new_level = new_tokens(place, owners, rows, new_kv)
    lists = page_lists(page_owner, page_index, lengths)

    cut = requests // 2
    slots = [list(range(cut)), list(range(cut, requests))]
    owned = functools.partial(items, place, owners, kv_cache, visitors=requests)

    def up(array):
        return lax.ppermute(array, "cache", forward)

    def down(array):
        return lax.ppermute(array, "cache", backward)

    def after(array, *others):
        return lax.optimization_barrier((array, others))[0]

    blocks = [payload(lists, visits[:cut])]
    blocks.append(payload(lists, visits[cut:], [touch(kv_cache, blocks[0])]))
    below, above, far = list(blocks), list(blocks), [None, None]
    parts = {(half, 0): part for half, part in enumerate(owned(blocks, slots))}
    for step in range(1, reach + 1):
        for half in range(2):
            if step == reach:
                arrival = up(below[0]) if half == 0 else down(above[1])
                far[half] = owned([arrival], [slots[half]])[0]
                continue
            done = [parts[half, 0]] if step == 1 else [parts[half, 1 - step], parts[half, step - 1]]
            below[half] = after(up(below[half]), *done)
            above[half] = after(down(above[half]), *done)
            parts[half, -step], parts[half, step] = owned([below[half], above[half]], [slots[half]] * 2)

    arrived = []
    for half in range(2):
        for move, sign in ((up, 1), (down, -1)):
            if half == (0 if sign == 1 else 1):
                chain, steps = far[half], range(reach - 1, -1, -1)
            else:
                chain, steps = parts[half, sign * (reach - 1)], range(reach - 2, -1, -1)
            for step in steps:
                chain = move(chain)
                if step > 0:
                    chain = merge(chain, parts[half, sign * step])
            arrived.append(chain)
    back = gather(arrived[2], arrived[3], parts[1, 0])
    front = gather(arrived[0], arrived[1], after(parts[0, 0], *back))
    home = [swap(part, d) for d, part in enumerate(front + back)]
    early = final(place, owners, home[cut:], cut, new_out, new_level)
    return final(place, owners, home[:cut], 0, new_out, new_level, [early])


def solution(mesh):
    in_specs = (
        P(("grp", "cache"), None, None),
        P(("grp", "cache"), None, None),
        P(("grp", "cache"), None, None),
        P(("grp", "cache"), None),
        P(("grp", "cache"), None, None),
        P(("grp", "cache")),
    )
    out_specs = P(("grp", "cache"), None, None)
    return jax.shard_map(
        per_device, mesh=mesh, in_specs=in_specs, out_specs=out_specs, check_vma=False
    )
```

```python
import functools
import math

import jax
import jax.numpy as jnp
from jax import lax
from jax.experimental import pallas as pl
from jax.experimental.pallas import tpu as pltpu
from jax.sharding import PartitionSpec as P

KVH = 8
HD = 128
GQ = 8
STEPS = 4
PAGE = 128
SEL = 4

LANES = 128
ROWS = GQ * STEPS
HALF = 16
BODY = KVH * ROWS
COLS = BODY // HALF
SECOND = 3 * COLS
PAIR = 2 * BODY + HALF
LONE = BODY + HALF
EMPTY = -1e30
SCALE = math.log2(math.e) / math.sqrt(HD)
VMEM_BYTES = 24 * 1024 * 1024
BF16 = jnp.bfloat16
F32 = jnp.float32
IN_VMEM = pl.BlockSpec(memory_space=pltpu.VMEM)
IN_SMEM = pl.BlockSpec(memory_space=pltpu.SMEM)


def params():
    return pltpu.CompilerParams(vmem_limit_bytes=VMEM_BYTES)


def cost(flops, moved):
    return pl.CostEstimate(flops=flops, bytes_accessed=moved, transcendentals=0)


def list_rows(requests):
    return -(-2 * requests // HALF) * HALF


def lane_ids(rows=HALF):
    return lax.broadcasted_iota(jnp.int32, (rows, LANES), 1)


def pack_stats(stats):
    lanes = lane_ids()
    used = (lanes < COLS) | ((lanes >= SECOND) & (lanes < SECOND + COLS))
    stats = jnp.where(used, stats, 0.0)
    high = stats.astype(BF16).astype(F32)
    rest = stats - high
    middle = rest.astype(BF16).astype(F32)
    low = rest - middle
    return (high + pltpu.roll(middle, COLS, 1) + pltpu.roll(low, 2 * COLS, 1)).astype(BF16)


def unpack_stats(tile):
    tile = tile.astype(F32)
    return tile + pltpu.roll(tile, LANES - COLS, 1) + pltpu.roll(tile, LANES - 2 * COLS, 1)


def tile_start(index):
    half, head = divmod(index, KVH)
    return head * ROWS + half * HALF


def by_lane(columns, first=0):
    lanes = lane_ids() - first
    tile = jnp.zeros((HALF, LANES), F32)
    for head, values in enumerate(columns):
        for half in range(ROWS // HALF):
            part = values[half * HALF : (half + 1) * HALF, :]
            tile = jnp.where(lanes == half * KVH + head, part, tile)
    return tile


def attend(requests):
    across = (((1,), (1,)), ((), ()))
    along = (((1,), (0,)), ((), ()))
    heads = [(q, k, v, r[3]) for r in requests for q, k, v in zip(*r[:3])]
    ones = jnp.ones(heads[0][2].shape, BF16)
    scores = [lax.dot_general(q, k, across, preferred_element_type=F32) for q, k, _, _ in heads]
    scores = [jnp.where(head[3], s * SCALE, EMPTY) for s, head in zip(scores, heads)]
    tops = [jnp.max(s, axis=1, keepdims=True) for s in scores]
    weights = [jnp.exp2(s - t).astype(BF16) for s, t in zip(scores, tops)]
    both = [
        lax.dot_general(w, jnp.concatenate([head[2], ones], axis=1), along, preferred_element_type=F32)
        for w, head in zip(weights, heads)
    ]
    mixed, totals = [b[:, :HD] for b in both], [b[:, HD:] for b in both]
    results = []
    for number, request in enumerate(requests):
        mine = slice(number * KVH, (number + 1) * KVH)
        first = request[4]
        level = by_lane(tops[mine], first) + jnp.log2(jnp.maximum(by_lane(totals[mine], first), 1.0))
        results.append(([m / t for m, t in zip(mixed[mine], totals[mine])], level))
    return results


def relayout_kernel(owners, place_ref, queries_ref, *outs):
    group = lax.div(place_ref[0], owners)
    for d, out in enumerate(outs):
        values = queries_ref[group ^ d].astype(F32)
        for head in range(KVH):
            first = head * GQ
            parts = [values[:, (first + g) * HD : (first + g + 1) * HD] for g in range(GQ)]
            out[head * ROWS : (head + 1) * ROWS, :] = jnp.concatenate(parts, axis=0).astype(BF16)


def relayout(place, owners, queries):
    groups = queries.shape[0]
    return pl.pallas_call(
        functools.partial(relayout_kernel, owners),
        out_shape=[jax.ShapeDtypeStruct((BODY, HD), BF16)] * groups,
        in_specs=[IN_SMEM, IN_VMEM],
        out_specs=[IN_VMEM] * groups,
        compiler_params=params(),
        cost_estimate=cost(0, 4 * queries.size),
    )(place, queries)


def new_kernel(owners, place_ref, *refs):
    group = lax.div(place_ref[0], owners)
    queries, (new_ref, out_ref, level_ref) = refs[:-3], refs[-3:]
    step = lax.broadcasted_iota(jnp.int32, (ROWS, STEPS), 0) % STEPS
    usable = lax.broadcasted_iota(jnp.int32, (ROWS, STEPS), 1) <= step
    for d, query in enumerate(queries):
        new = new_ref[group ^ d]
        heads = [new[:, head * HD : (head + 1) * HD] for head in range(2 * KVH)]
        rows = [query[head * ROWS : (head + 1) * ROWS, :] for head in range(KVH)]
        [(mixed, level)] = attend([(rows, heads[:KVH], heads[KVH:], usable, 0)])
        for head, values in enumerate(mixed):
            out_ref[d, head * ROWS : (head + 1) * ROWS, :] = values
        level_ref[d] = level


def new_tokens(place, owners, queries, new_kv):
    groups = len(queries)
    return pl.pallas_call(
        functools.partial(new_kernel, owners),
        out_shape=[
            jax.ShapeDtypeStruct((groups, BODY, HD), F32),
            jax.ShapeDtypeStruct((groups, HALF, LANES), F32),
        ],
        in_specs=[IN_SMEM] + [IN_VMEM] * (groups + 1),
        out_specs=[IN_VMEM, IN_VMEM],
        compiler_params=params(),
        cost_estimate=cost(groups * KVH * 4 * ROWS * HD * HD, groups * BODY * HD * 6),
    )(place, *queries, new_kv)


def page_lists(page_owner, page_index, lengths):
    lanes = jnp.arange(LANES, dtype=jnp.int32)[None, None, :]
    counts = jnp.clip(lengths[:, None] - jnp.arange(SEL, dtype=jnp.int32)[None, :] * PAGE, 0, PAGE)
    named = page_owner[:, :, None] == lanes
    return (
        jnp.sum(jnp.where(named, counts[:, :, None], 0), axis=1),
        jnp.sum(jnp.where(named, page_index, 0), axis=1),
    )


def payload_kernel(after, counts_ref, pages_ref, *refs):
    visits, out = refs[: len(refs) - 1 - after], refs[-1]
    for number, visit in enumerate(visits):
        out[number * BODY : (number + 1) * BODY, :] = visit[...]
    tables = [counts_ref[...].astype(F32), pages_ref[...].astype(F32)]
    short = out.shape[0] - len(visits) * BODY - 2 * tables[0].shape[0]
    if short:
        tables.append(jnp.zeros((short, LANES), F32))
    out[len(visits) * BODY :, :] = jnp.concatenate(tables, axis=0).astype(BF16)


def payload(lists, visits, after=()):
    rows = len(visits) * BODY + list_rows(lists[0].shape[0])
    return pl.pallas_call(
        functools.partial(payload_kernel, len(after)),
        out_shape=jax.ShapeDtypeStruct((rows, HD), BF16),
        in_specs=[IN_VMEM] * (2 + len(visits) + len(after)),
        out_specs=IN_VMEM,
        compiler_params=params(),
        cost_estimate=cost(0, 4 * rows * HD),
    )(*lists, *visits, *after)


def touch_kernel(after_ref, cache_ref, out_ref):
    out_ref[...] = cache_ref[0, :HALF, :HD]


def touch(kv_cache, after):
    return pl.pallas_call(
        touch_kernel,
        out_shape=jax.ShapeDtypeStruct((HALF, HD), BF16),
        in_specs=[IN_VMEM, IN_VMEM],
        out_specs=IN_VMEM,
        compiler_params=params(),
        cost_estimate=cost(0, 2 * HALF * HD),
    )(after, kv_cache)


def item_kernel(slots, visitors, owners, place_ref, cache_ref, *refs):
    sides, each = len(slots), len(slots[0])
    entries = sides * each
    query_refs, (out_ref, rows_ref, level_ref, code_ref, order_ref) = refs[:sides], refs[sides:]
    group, owner = lax.div(place_ref[0], owners), lax.rem(place_ref[0], owners)
    lists = list_rows(visitors)
    rows = lax.broadcasted_iota(jnp.int32, (lists, LANES), 0)
    lanes = lane_ids()
    codes = []
    for side, query_ref in enumerate(query_refs):
        table = query_ref[each * BODY :, :].astype(F32)
        table = jnp.where(lane_ids(lists) == owner, table, 0.0)
        for pair in range(each // 2):
            factor = jnp.zeros((lists, LANES), F32)
            for second in range(2):
                row = group ^ slots[side][2 * pair + second]
                factor = jnp.where(rows == row, float(4096**second), factor)
                factor = jnp.where(rows == row + visitors, float(256 * 4096**second), factor)
            codes.append(jnp.sum(table * factor).astype(jnp.int32))
        rows_ref[side * each * BODY : (side + 1) * each * BODY, :] = query_ref[: each * BODY, :]

    for entry in range(entries):
        out = entry // 2 * PAIR + entry % 2 * BODY
        out_ref[out : out + BODY, :] = jnp.zeros((BODY, HD), BF16)
        first = entry % 2 * SECOND
        level_ref[entry] = jnp.where((lanes >= first) & (lanes < first + COLS), EMPTY, 0.0)
    found = jnp.int32(0)
    for entry in range(entries):
        code = (codes[entry // 2] >> (12 * (entry % 2))) & 4095
        code_ref[entry] = code
        order_ref[found] = entry
        found = found + jnp.where((code & 255) > 0, 1, 0)
    order_ref[found] = order_ref[jnp.maximum(found - 1, 0)]
    tokens = lax.broadcasted_iota(jnp.int32, (ROWS, PAGE), 1)

    @pl.loop(0, (found + 1) >> 1)
    def _(two):
        requests, places = [], []
        for number in range(2):
            entry = order_ref[2 * two + number]
            code = code_ref[entry]
            page, odd = code >> 8, entry & 1
            start = entry * BODY
            queries = [rows_ref[pl.ds(pl.multiple_of(start + h * ROWS, HALF), ROWS), :] for h in range(KVH)]
            keys = [cache_ref[page, :, h * HD : (h + 1) * HD] for h in range(KVH)]
            values = [cache_ref[page, :, (KVH + h) * HD : (KVH + h + 1) * HD] for h in range(KVH)]
            requests.append((queries, keys, values, tokens < (code & 255), odd * SECOND))
            places.append((entry, (entry >> 1) * PAIR + odd * BODY))
        for (mixed, level), (entry, out) in zip(attend(requests), places):
            for head, part in enumerate(mixed):
                out_ref[pl.ds(pl.multiple_of(out + head * ROWS, HALF), ROWS), :] = part.astype(BF16)
            level_ref[entry] = level

    for pair in range(entries // 2):
        start = pair * PAIR + 2 * BODY
        out_ref[start : start + HALF, :] = pack_stats(level_ref[2 * pair] + level_ref[2 * pair + 1])


def items(place, owners, kv_cache, payloads, slots, visitors):
    count = sum(len(row) for row in slots)
    return pl.pallas_call(
        functools.partial(item_kernel, slots, visitors, owners),
        out_shape=jax.ShapeDtypeStruct((count // 2 * PAIR, HD), BF16),
        in_specs=[IN_SMEM] + [IN_VMEM] * (1 + len(slots)),
        out_specs=IN_VMEM,
        scratch_shapes=[
            pltpu.VMEM((count * BODY, HD), BF16),
            pltpu.VMEM((count, HALF, LANES), F32),
            pltpu.SMEM((count,), jnp.int32),
            pltpu.SMEM((count + 1,), jnp.int32),
        ],
        compiler_params=params(),
        cost_estimate=cost(count * KVH * 4 * ROWS * HD * PAGE, count * PAGE * kv_cache.shape[2] * 2),
    )(place, kv_cache, *payloads)


def blend(levels):
    peak = functools.reduce(jnp.maximum, levels)
    shares = [jnp.exp2(level - peak) for level in levels]
    total = functools.reduce(jnp.add, shares)
    return [share / total for share in shares], peak + jnp.log2(total)


def mix(shares, refs, start, first_lane):
    values = []
    for index in range(COLS):
        row, lane = start + tile_start(index), first_lane + index
        tiles = [ref[row : row + HALF, :].astype(F32) for ref in refs]
        total = tiles[0]
        for share, tile in zip(shares[1:], tiles[1:]):
            total = total + share[:, lane : lane + 1] * (tile - tiles[0])
        values.append(total)
    return values


def merge_kernel(first, arrived_ref, own_ref, out_ref):
    for pair in range(out_ref.shape[0] // PAIR):
        part = slice(pair * PAIR, (pair + 1) * PAIR)
        arrived, own, out = arrived_ref.at[part], own_ref.at[first + pair * PAIR : first + (pair + 1) * PAIR], out_ref.at[part]
        shares, level = blend([unpack_stats(ref[2 * BODY : PAIR, :]) for ref in (arrived, own)])
        values = [mix(shares, (arrived, own), second * BODY, second * SECOND) for second in range(2)]
        for second in range(2):
            for index in range(COLS):
                row = second * BODY + tile_start(index)
                out[row : row + HALF, :] = values[second][index].astype(BF16)
        out[2 * BODY : PAIR, :] = pack_stats(level)


def merge(arrived, own):
    own, first = own
    return pl.pallas_call(
        functools.partial(merge_kernel, first),
        out_shape=jax.ShapeDtypeStruct(arrived.shape, BF16),
        in_specs=[IN_VMEM, IN_VMEM],
        out_specs=IN_VMEM,
        compiler_params=params(),
        cost_estimate=cost(0, 6 * arrived.size),
    )(arrived, own)


def gather_kernel(first, ahead_ref, behind_ref, own_ref, *outs):
    for pair in range(len(outs) // 2):
        part = slice(pair * PAIR, (pair + 1) * PAIR)
        own = own_ref.at[first + pair * PAIR : first + (pair + 1) * PAIR]
        sources = [own, ahead_ref.at[part], behind_ref.at[part]]
        shares, level = blend([unpack_stats(ref[2 * BODY : PAIR, :]) for ref in sources])
        values = [mix(shares, sources, second * BODY, second * SECOND) for second in range(2)]
        for second in range(2):
            out = outs[2 * pair + second]
            for index in range(COLS):
                row = tile_start(index)
                out[row : row + HALF, :] = values[second][index].astype(BF16)
            here = pltpu.roll(level, LANES - SECOND, 1) if second else level
            out[BODY:LONE, :] = pack_stats(here)


def gather(ahead, behind, own):
    pairs = ahead.shape[0] // PAIR
    own, first = own
    return pl.pallas_call(
        functools.partial(gather_kernel, first),
        out_shape=[jax.ShapeDtypeStruct((LONE, HD), BF16)] * (2 * pairs),
        in_specs=[IN_VMEM] * 3,
        out_specs=[IN_VMEM] * (2 * pairs),
        compiler_params=params(),
        cost_estimate=cost(0, 8 * pairs * PAIR * HD),
    )(ahead, behind, own)


def final_kernel(first, early, owners, place_ref, *refs):
    earlier, parts = refs[:early], refs[early:-4]
    new_ref, level_ref, out_ref, rows_ref = refs[-4:]
    group = lax.div(place_ref[0], owners)
    for number, part in enumerate(parts):
        d = first + number
        shares, _ = blend([unpack_stats(part[BODY:LONE, :]), level_ref[d]])
        for index, tile in enumerate(mix(shares, (part, new_ref.at[d]), 0, 0)):
            row = tile_start(index)
            rows_ref[number, row : row + HALF, :] = tile
    for number in range(len(parts)):
        row = group ^ (first + number) if early else number
        for head in range(KVH * GQ):
            tile = rows_ref[number, head * STEPS : (head + 1) * STEPS, :]
            out_ref[row, :, head * HD : (head + 1) * HD] = tile.astype(BF16)
    for ref in earlier:
        for number in range(ref.shape[0]):
            out_ref[group ^ (len(parts) + number)] = ref[number]


def final(place, owners, parts, first, new_out, new_level, earlier=()):
    requests = len(parts) + sum(e.shape[0] for e in earlier)
    return pl.pallas_call(
        functools.partial(final_kernel, first, len(earlier), owners),
        out_shape=jax.ShapeDtypeStruct((requests, STEPS, KVH * GQ * HD), BF16),
        in_specs=[IN_SMEM] + [IN_VMEM] * (len(earlier) + len(parts) + 2),
        out_specs=IN_VMEM,
        scratch_shapes=[pltpu.VMEM((len(parts), BODY, HD), F32)],
        compiler_params=params(),
        cost_estimate=cost(0, len(parts) * BODY * HD * 8),
    )(place, *earlier, *parts, new_out, new_level)


def ring_order(owners):
    return list(range(0, owners, 2)) + list(range(owners - 1, 0, -2))


def per_device(queries, new_kv, kv_cache, page_owner, page_index, lengths):
    groups = lax.axis_size("grp")
    owners = lax.axis_size("cache")
    requests = queries.shape[0]
    assert requests == groups and requests % 4 == 0 and owners <= LANES
    reach = owners // 2
    order = ring_order(owners)
    forward = [(order[i], order[(i + 1) % owners]) for i in range(owners)]
    backward = [(b, a) for a, b in forward]
    place = jnp.reshape(lax.axis_index(("grp", "cache")), (1,)).astype(jnp.int32)

    def swap(array, d):
        return lax.ppermute(array, "grp", [(g, g ^ d) for g in range(groups)]) if d else array

    rows = relayout(place, owners, queries)
    visits = [rows[0]] + [None] * (groups - 1)
    for d in range(groups - 1, 0, -1):
        visits[d] = swap(rows[d], d)
    new_out, new_level = new_tokens(place, owners, rows, new_kv)
    lists = page_lists(page_owner, page_index, lengths)

    cut = requests // 2
    slots = [list(range(cut)), list(range(cut, requests))]
    owned = functools.partial(items, place, owners, kv_cache, visitors=requests)

    def up(array):
        return lax.ppermute(array, "cache", forward)

    def down(array):
        return lax.ppermute(array, "cache", backward)

    def after(array, *others):
        return lax.optimization_barrier((array, others))[0]

    blocks = [payload(lists, visits[:cut])]
    blocks.append(payload(lists, visits[cut:], [touch(kv_cache, blocks[0])]))
    below, above = [up(block) for block in blocks], [down(block) for block in blocks]
    size = cut // 2 * PAIR
    both = owned(blocks, slots)
    parts = {(0, 0): (both, 0), (1, 0): (both, size)}
    done = [[both], [both]]
    for step in range(1, reach):
        for half in range(2):
            if step > 1:
                below[half], above[half] = up(below[half]), down(above[half])
            below[half], above[half] = after(below[half], *done[half]), after(above[half], *done[half])
            both = owned([below[half], above[half]], [slots[half]] * 2)
            parts[half, -step], parts[half, step] = (both, 0), (both, size)
            done[half] = [both]
    far = owned([up(below[0])], slots[:1]), owned([down(above[1])], slots[1:])

    arrived = []
    for half in range(2):
        for move, sign in ((up, 1), (down, -1)):
            if half == (0 if sign == 1 else 1):
                chain, steps = far[half], range(reach - 1, -1, -1)
            else:
                own, first = parts[half, sign * (reach - 1)]
                chain, steps = own[first : first + size], range(reach - 2, -1, -1)
            for step in steps:
                chain = move(chain)
                if step > 0:
                    chain = merge(chain, parts[half, sign * step])
            arrived.append(chain)
    back = gather(arrived[2], arrived[3], parts[1, 0])
    front = gather(arrived[0], arrived[1], (after(parts[0, 0][0], *back), 0))
    home = [swap(part, d) for d, part in enumerate(front + back)]
    early = final(place, owners, home[cut:], cut, new_out, new_level)
    return final(place, owners, home[:cut], 0, new_out, new_level, [early])


def solution(mesh):
    in_specs = (
        P(("grp", "cache"), None, None),
        P(("grp", "cache"), None, None),
        P(("grp", "cache"), None, None),
        P(("grp", "cache"), None),
        P(("grp", "cache"), None, None),
        P(("grp", "cache")),
    )
    out_specs = P(("grp", "cache"), None, None)
    return jax.shard_map(
        per_device, mesh=mesh, in_specs=in_specs, out_specs=out_specs, check_vma=False
    )
```

```python
import functools
import math

import jax
import jax.numpy as jnp
from jax import lax
from jax.experimental import pallas as pl
from jax.experimental.pallas import tpu as pltpu
from jax.sharding import PartitionSpec as P

KVH = 8
HD = 128
GQ = 8
STEPS = 4
PAGE = 128
SEL = 4

LANES = 128
ROWS = GQ * STEPS
HALF = 16
BODY = KVH * ROWS
COLS = BODY // HALF
SECOND = 3 * COLS
PAIR = 2 * BODY + HALF
LONE = BODY + HALF
EMPTY = -1e30
SCALE = math.log2(math.e) / math.sqrt(HD)
VMEM_BYTES = 24 * 1024 * 1024
LOAD_BYTES = 44 * 1024 * 1024
BF16 = jnp.bfloat16
F32 = jnp.float32
IN_VMEM = pl.BlockSpec(memory_space=pltpu.VMEM)
IN_SMEM = pl.BlockSpec(memory_space=pltpu.SMEM)


def params():
    return pltpu.CompilerParams(vmem_limit_bytes=VMEM_BYTES)


def cost(flops, moved):
    return pl.CostEstimate(flops=flops, bytes_accessed=moved, transcendentals=0)


def list_rows(requests):
    return -(-2 * requests // HALF) * HALF


def lane_ids(rows=HALF):
    return lax.broadcasted_iota(jnp.int32, (rows, LANES), 1)


def pack_stats(stats):
    lanes = lane_ids()
    used = (lanes < COLS) | ((lanes >= SECOND) & (lanes < SECOND + COLS))
    stats = jnp.where(used, stats, 0.0)
    high = stats.astype(BF16).astype(F32)
    rest = stats - high
    middle = rest.astype(BF16).astype(F32)
    low = rest - middle
    return (high + pltpu.roll(middle, COLS, 1) + pltpu.roll(low, 2 * COLS, 1)).astype(BF16)


def unpack_stats(tile):
    tile = tile.astype(F32)
    return tile + pltpu.roll(tile, LANES - COLS, 1) + pltpu.roll(tile, LANES - 2 * COLS, 1)


def tile_start(index):
    half, head = divmod(index, KVH)
    return head * ROWS + half * HALF


def by_lane(columns, first=0):
    lanes = lane_ids() - first
    tile = jnp.zeros((HALF, LANES), F32)
    for head, values in enumerate(columns):
        for half in range(ROWS // HALF):
            part = values[half * HALF : (half + 1) * HALF, :]
            tile = jnp.where(lanes == half * KVH + head, part, tile)
    return tile


def attend(requests):
    across = (((1,), (1,)), ((), ()))
    along = (((1,), (0,)), ((), ()))
    heads = [(q, k, v, r[3]) for r in requests for q, k, v in zip(*r[:3])]
    ones = jnp.ones(heads[0][2].shape, BF16)
    scores = [lax.dot_general(q, k, across, preferred_element_type=F32) for q, k, _, _ in heads]
    scores = [jnp.where(head[3], s * SCALE, EMPTY) for s, head in zip(scores, heads)]
    tops = [jnp.max(s, axis=1, keepdims=True) for s in scores]
    weights = [jnp.exp2(s - t).astype(BF16) for s, t in zip(scores, tops)]
    both = [
        lax.dot_general(w, jnp.concatenate([head[2], ones], axis=1), along, preferred_element_type=F32)
        for w, head in zip(weights, heads)
    ]
    mixed, totals = [b[:, :HD] for b in both], [b[:, HD:] for b in both]
    results = []
    for number, request in enumerate(requests):
        mine = slice(number * KVH, (number + 1) * KVH)
        first = request[4]
        level = by_lane(tops[mine], first) + jnp.log2(jnp.maximum(by_lane(totals[mine], first), 1.0))
        results.append(([m / t for m, t in zip(mixed[mine], totals[mine])], level))
    return results


def relayout_kernel(owners, place_ref, queries_ref, *outs):
    group = lax.div(place_ref[0], owners)
    for d, out in enumerate(outs):
        values = queries_ref[group ^ d].astype(F32)
        for head in range(KVH):
            first = head * GQ
            parts = [values[:, (first + g) * HD : (first + g + 1) * HD] for g in range(GQ)]
            out[head * ROWS : (head + 1) * ROWS, :] = jnp.concatenate(parts, axis=0).astype(BF16)


def relayout(place, owners, queries):
    groups = queries.shape[0]
    return pl.pallas_call(
        functools.partial(relayout_kernel, owners),
        out_shape=[jax.ShapeDtypeStruct((BODY, HD), BF16)] * groups,
        in_specs=[IN_SMEM, IN_VMEM],
        out_specs=[IN_VMEM] * groups,
        compiler_params=params(),
        cost_estimate=cost(0, 4 * queries.size),
    )(place, queries)


def new_kernel(owners, place_ref, *refs):
    group = lax.div(place_ref[0], owners)
    queries, (new_ref, out_ref, level_ref) = refs[:-3], refs[-3:]
    step = lax.broadcasted_iota(jnp.int32, (ROWS, STEPS), 0) % STEPS
    usable = lax.broadcasted_iota(jnp.int32, (ROWS, STEPS), 1) <= step
    for d, query in enumerate(queries):
        new = new_ref[group ^ d]
        heads = [new[:, head * HD : (head + 1) * HD] for head in range(2 * KVH)]
        rows = [query[head * ROWS : (head + 1) * ROWS, :] for head in range(KVH)]
        [(mixed, level)] = attend([(rows, heads[:KVH], heads[KVH:], usable, 0)])
        for head, values in enumerate(mixed):
            out_ref[d, head * ROWS : (head + 1) * ROWS, :] = values
        level_ref[d] = level


def new_tokens(place, owners, queries, new_kv):
    groups = len(queries)
    return pl.pallas_call(
        functools.partial(new_kernel, owners),
        out_shape=[
            jax.ShapeDtypeStruct((groups, BODY, HD), F32),
            jax.ShapeDtypeStruct((groups, HALF, LANES), F32),
        ],
        in_specs=[IN_SMEM] + [IN_VMEM] * (groups + 1),
        out_specs=[IN_VMEM, IN_VMEM],
        compiler_params=params(),
        cost_estimate=cost(groups * KVH * 4 * ROWS * HD * HD, groups * BODY * HD * 6),
    )(place, *queries, new_kv)


def page_lists(page_owner, page_index, lengths):
    lanes = jnp.arange(LANES, dtype=jnp.int32)[None, None, :]
    counts = jnp.clip(lengths[:, None] - jnp.arange(SEL, dtype=jnp.int32)[None, :] * PAGE, 0, PAGE)
    named = page_owner[:, :, None] == lanes
    return (
        jnp.sum(jnp.where(named, counts[:, :, None], 0), axis=1),
        jnp.sum(jnp.where(named, page_index, 0), axis=1),
    )


def payload_kernel(after, counts_ref, pages_ref, *refs):
    visits, out = refs[: len(refs) - 1 - after], refs[-1]
    tables = [counts_ref[...].astype(F32), pages_ref[...].astype(F32)]
    lists = list_rows(len(visits))
    if lists > 2 * len(visits):
        tables.append(jnp.zeros((lists - 2 * len(visits), LANES), F32))
    table = jnp.concatenate(tables, axis=0).astype(BF16)
    cut = len(visits) // 2
    for number, visit in enumerate(visits):
        start = number * BODY + number // cut * lists
        out[start : start + BODY, :] = visit[...]
    for half in range(2):
        start = (half + 1) * cut * BODY + half * lists
        out[start : start + lists, :] = table


def payload(lists, visits, after):
    rows = len(visits) * BODY + 2 * list_rows(len(visits))
    return pl.pallas_call(
        functools.partial(payload_kernel, len(after)),
        out_shape=jax.ShapeDtypeStruct((rows, HD), BF16),
        in_specs=[IN_VMEM] * (2 + len(visits) + len(after)),
        out_specs=IN_VMEM,
        compiler_params=params(),
        cost_estimate=cost(0, 4 * rows * HD),
    )(*lists, *visits, *after)


def load_kernel(owners, parity, place_ref, cache_ref, *refs):
    out_ref, sems = refs[-2:]

    @pl.when((lax.div(place_ref[0], owners) & 1) == parity)
    def _():
        copies = [
            pltpu.make_async_copy(cache_ref.at[page], out_ref.at[page], sems.at[page])
            for page in range(cache_ref.shape[0])
        ]
        for copy in copies:
            copy.start()
        for copy in copies:
            copy.wait()


def load_pages(place, owners, kv_cache, parity, pages=None, after=()):
    given = [] if pages is None else [pages]
    return pl.pallas_call(
        functools.partial(load_kernel, owners, parity),
        out_shape=jax.ShapeDtypeStruct(kv_cache.shape, BF16),
        in_specs=[IN_SMEM, pl.BlockSpec(memory_space=pl.ANY)] + [IN_VMEM] * (len(given) + len(after)),
        out_specs=IN_VMEM,
        scratch_shapes=[pltpu.SemaphoreType.DMA((kv_cache.shape[0],))],
        input_output_aliases={2: 0} if given else {},
        compiler_params=pltpu.CompilerParams(vmem_limit_bytes=LOAD_BYTES),
        cost_estimate=cost(0, 2 * kv_cache.size),
    )(place, kv_cache, *given, *after)


def item_kernel(slots, visitors, owners, place_ref, cache_ref, *refs):
    sides, each = len(slots), len(slots[0])
    entries = sides * each
    arrays, (out_ref, rows_ref, level_ref, code_ref, order_ref) = refs[:-5], refs[-5:]
    unit = each * BODY + list_rows(visitors)
    query_refs = [ref.at[at : at + unit] for ref in arrays for at in range(0, ref.shape[0], unit)]
    group, owner = lax.div(place_ref[0], owners), lax.rem(place_ref[0], owners)
    lists = list_rows(visitors)
    rows = lax.broadcasted_iota(jnp.int32, (lists, LANES), 0)
    lanes = lane_ids()
    codes = []
    for side, query_ref in enumerate(query_refs):
        table = query_ref[each * BODY :, :].astype(F32)
        table = jnp.where(lane_ids(lists) == owner, table, 0.0)
        for pair in range(each // 2):
            factor = jnp.zeros((lists, LANES), F32)
            for second in range(2):
                row = group ^ slots[side][2 * pair + second]
                factor = jnp.where(rows == row, float(4096**second), factor)
                factor = jnp.where(rows == row + visitors, float(256 * 4096**second), factor)
            codes.append(jnp.sum(table * factor).astype(jnp.int32))
        rows_ref[side * each * BODY : (side + 1) * each * BODY, :] = query_ref[: each * BODY, :]

    for entry in range(entries):
        out = entry // 2 * PAIR + entry % 2 * BODY
        out_ref[out : out + BODY, :] = jnp.zeros((BODY, HD), BF16)
        first = entry % 2 * SECOND
        level_ref[entry] = jnp.where((lanes >= first) & (lanes < first + COLS), EMPTY, 0.0)
    found = jnp.int32(0)
    for entry in range(entries):
        code = (codes[entry // 2] >> (12 * (entry % 2))) & 4095
        code_ref[entry] = code
        order_ref[found] = entry
        found = found + jnp.where((code & 255) > 0, 1, 0)
    order_ref[found] = order_ref[jnp.maximum(found - 1, 0)]
    tokens = lax.broadcasted_iota(jnp.int32, (ROWS, PAGE), 1)

    @pl.loop(0, (found + 1) >> 1)
    def _(two):
        requests, places = [], []
        for number in range(2):
            entry = order_ref[2 * two + number]
            code = code_ref[entry]
            page, odd = code >> 8, entry & 1
            start = entry * BODY
            queries = [rows_ref[pl.ds(pl.multiple_of(start + h * ROWS, HALF), ROWS), :] for h in range(KVH)]
            keys = [cache_ref[page, :, h * HD : (h + 1) * HD] for h in range(KVH)]
            values = [cache_ref[page, :, (KVH + h) * HD : (KVH + h + 1) * HD] for h in range(KVH)]
            requests.append((queries, keys, values, tokens < (code & 255), odd * SECOND))
            places.append((entry, (entry >> 1) * PAIR + odd * BODY))
        for (mixed, level), (entry, out) in zip(attend(requests), places):
            for head, part in enumerate(mixed):
                out_ref[pl.ds(pl.multiple_of(out + head * ROWS, HALF), ROWS), :] = part.astype(BF16)
            level_ref[entry] = level

    for pair in range(entries // 2):
        start = pair * PAIR + 2 * BODY
        out_ref[start : start + HALF, :] = pack_stats(level_ref[2 * pair] + level_ref[2 * pair + 1])


def items(place, owners, kv_cache, payloads, slots, visitors):
    count = sum(len(row) for row in slots)
    return pl.pallas_call(
        functools.partial(item_kernel, slots, visitors, owners),
        out_shape=jax.ShapeDtypeStruct((count // 2 * PAIR, HD), BF16),
        in_specs=[IN_SMEM] + [IN_VMEM] * (1 + len(payloads)),
        out_specs=IN_VMEM,
        scratch_shapes=[
            pltpu.VMEM((count * BODY, HD), BF16),
            pltpu.VMEM((count, HALF, LANES), F32),
            pltpu.SMEM((count,), jnp.int32),
            pltpu.SMEM((count + 1,), jnp.int32),
        ],
        compiler_params=params(),
        cost_estimate=cost(count * KVH * 4 * ROWS * HD * PAGE, count * PAGE * kv_cache.shape[2] * 2),
    )(place, kv_cache, *payloads)


def blend(levels):
    peak = functools.reduce(jnp.maximum, levels)
    shares = [jnp.exp2(level - peak) for level in levels]
    total = functools.reduce(jnp.add, shares)
    return [share / total for share in shares], peak + jnp.log2(total)


def mix(shares, refs, start, first_lane):
    values = []
    for index in range(COLS):
        row, lane = start + tile_start(index), first_lane + index
        tiles = [ref[row : row + HALF, :].astype(F32) for ref in refs]
        total = tiles[0]
        for share, tile in zip(shares[1:], tiles[1:]):
            total = total + share[:, lane : lane + 1] * (tile - tiles[0])
        values.append(total)
    return values


def merge_kernel(first, base, arrived_ref, own_ref, *outs):
    arrived_pairs = arrived_ref.shape[0] // PAIR
    each = outs[0].shape[0] // PAIR
    for pair in range(len(outs) * each):
        own = own_ref.at[first + pair * PAIR : first + (pair + 1) * PAIR]
        out = outs[pair // each].at[pair % each * PAIR : (pair % each + 1) * PAIR]
        if not base <= pair < base + arrived_pairs:
            out[...] = own[...]
            continue
        arrived = arrived_ref.at[(pair - base) * PAIR : (pair - base + 1) * PAIR]
        shares, level = blend([unpack_stats(ref[2 * BODY : PAIR, :]) for ref in (arrived, own)])
        values = [mix(shares, (arrived, own), second * BODY, second * SECOND) for second in range(2)]
        for second in range(2):
            for index in range(COLS):
                row = second * BODY + tile_start(index)
                out[row : row + HALF, :] = values[second][index].astype(BF16)
        out[2 * BODY : PAIR, :] = pack_stats(level)


def merge(arrived, own, base, rows, outs):
    own, first = own
    return pl.pallas_call(
        functools.partial(merge_kernel, first, base),
        out_shape=[jax.ShapeDtypeStruct((rows // outs, HD), BF16)] * outs,
        in_specs=[IN_VMEM, IN_VMEM],
        out_specs=[IN_VMEM] * outs,
        compiler_params=params(),
        cost_estimate=cost(0, 6 * rows * HD),
    )(arrived, own)


def gather_kernel(first, ahead_ref, behind_ref, own_ref, *outs):
    for pair in range(len(outs) // 2):
        part = slice(pair * PAIR, (pair + 1) * PAIR)
        own = own_ref.at[first + pair * PAIR : first + (pair + 1) * PAIR]
        sources = [own, ahead_ref.at[part], behind_ref.at[part]]
        shares, level = blend([unpack_stats(ref[2 * BODY : PAIR, :]) for ref in sources])
        values = [mix(shares, sources, second * BODY, second * SECOND) for second in range(2)]
        for second in range(2):
            out = outs[2 * pair + second]
            for index in range(COLS):
                row = tile_start(index)
                out[row : row + HALF, :] = values[second][index].astype(BF16)
            here = pltpu.roll(level, LANES - SECOND, 1) if second else level
            out[BODY:LONE, :] = pack_stats(here)


def gather(ahead, behind, own):
    pairs = ahead.shape[0] // PAIR
    own, first = own
    return pl.pallas_call(
        functools.partial(gather_kernel, first),
        out_shape=[jax.ShapeDtypeStruct((LONE, HD), BF16)] * (2 * pairs),
        in_specs=[IN_VMEM] * 3,
        out_specs=[IN_VMEM] * (2 * pairs),
        compiler_params=params(),
        cost_estimate=cost(0, 8 * pairs * PAIR * HD),
    )(ahead, behind, own)


def final_kernel(first, early, owners, place_ref, *refs):
    earlier, parts = refs[:early], refs[early:-4]
    new_ref, level_ref, out_ref, rows_ref = refs[-4:]
    group = lax.div(place_ref[0], owners)
    for number, part in enumerate(parts):
        d = first + number
        shares, _ = blend([unpack_stats(part[BODY:LONE, :]), level_ref[d]])
        for index, tile in enumerate(mix(shares, (part, new_ref.at[d]), 0, 0)):
            row = tile_start(index)
            rows_ref[number, row : row + HALF, :] = tile
    for number in range(len(parts)):
        row = group ^ (first + number) if early else number
        for head in range(KVH * GQ):
            tile = rows_ref[number, head * STEPS : (head + 1) * STEPS, :]
            out_ref[row, :, head * HD : (head + 1) * HD] = tile.astype(BF16)
    for ref in earlier:
        for number in range(ref.shape[0]):
            out_ref[group ^ (len(parts) + number)] = ref[number]


def final(place, owners, parts, first, new_out, new_level, earlier=()):
    requests = len(parts) + sum(e.shape[0] for e in earlier)
    return pl.pallas_call(
        functools.partial(final_kernel, first, len(earlier), owners),
        out_shape=jax.ShapeDtypeStruct((requests, STEPS, KVH * GQ * HD), BF16),
        in_specs=[IN_SMEM] + [IN_VMEM] * (len(earlier) + len(parts) + 2),
        out_specs=IN_VMEM,
        scratch_shapes=[pltpu.VMEM((len(parts), BODY, HD), F32)],
        compiler_params=params(),
        cost_estimate=cost(0, len(parts) * BODY * HD * 8),
    )(place, *earlier, *parts, new_out, new_level)


def ring_order(owners):
    return list(range(0, owners, 2)) + list(range(owners - 1, 0, -2))


def per_device(queries, new_kv, kv_cache, page_owner, page_index, lengths):
    groups = lax.axis_size("grp")
    owners = lax.axis_size("cache")
    requests = queries.shape[0]
    assert requests == groups and requests % 4 == 0 and owners <= LANES
    reach = owners // 2
    order = ring_order(owners)
    forward = [(order[i], order[(i + 1) % owners]) for i in range(owners)]
    backward = [(b, a) for a, b in forward]
    place = jnp.reshape(lax.axis_index(("grp", "cache")), (1,)).astype(jnp.int32)

    def swap(array, d):
        return lax.ppermute(array, "grp", [(g, g ^ d) for g in range(groups)]) if d else array

    rows = relayout(place, owners, queries)
    visits = [rows[0]] + [None] * (groups - 1)
    for d in range(groups - 1, 0, -1):
        visits[d] = swap(rows[d], d)
    new_out, new_level = new_tokens(place, owners, rows, new_kv)
    lists = page_lists(page_owner, page_index, lengths)

    cut = requests // 2
    slots = [list(range(cut)), list(range(cut, requests))]
    def up(array):
        return lax.ppermute(array, "cache", forward)

    def down(array):
        return lax.ppermute(array, "cache", backward)

    def after(array, *others):
        return lax.optimization_barrier((array, others))[0]

    pages = load_pages(place, owners, kv_cache, 1, after=[visits[1]])
    block = payload(lists, visits, [pages])
    below, above = up(block), down(block)
    pages = load_pages(place, owners, kv_cache, 0, pages, [block])
    owned = functools.partial(items, place, owners, pages, visitors=requests)

    size = requests // 2 * PAIR
    parts = {0: (owned([block], slots), 0)}
    unit = block.shape[0] // 2
    for step in range(1, reach):
        below, above = after(below, parts[1 - step][0]), after(above, parts[1 - step][0])
        both = owned([below, above], slots * 2)
        parts[-step], parts[step] = (both, 0), (both, size)
        last = step == reach - 1
        below, above = up(below[:unit] if last else below), down(above[unit:] if last else above)
    ahead, behind = [owned([below], slots[:1])], [owned([above], slots[1:])]

    for step in range(reach - 1, 0, -1):
        base = cut // 2 if step == reach - 1 else 0
        own = parts[step]
        if step == 1:
            own = (after(own[0], new_level), own[1])
        outs = 2 if step == 1 else 1
        ahead = merge(up(ahead[0]), own, 0, size, outs)
        behind = merge(down(behind[0]), parts[-step], base, size, outs)
    both = parts[0][0]
    back = gather(up(ahead[1]), down(behind[1]), (both, size // 2))
    front = gather(up(ahead[0]), down(behind[0]), (after(both, *back), 0))
    home = [swap(part, d) for d, part in enumerate(front + back)]
    early = final(place, owners, home[cut:], cut, new_out, new_level)
    return final(place, owners, home[:cut], 0, new_out, new_level, [early])


def solution(mesh):
    in_specs = (
        P(("grp", "cache"), None, None),
        P(("grp", "cache"), None, None),
        P(("grp", "cache"), None, None),
        P(("grp", "cache"), None),
        P(("grp", "cache"), None, None),
        P(("grp", "cache")),
    )
    out_specs = P(("grp", "cache"), None, None)
    return jax.shard_map(
        per_device, mesh=mesh, in_specs=in_specs, out_specs=out_specs, check_vma=False
    )
```

```python
import functools
import math

import jax
import jax.numpy as jnp
from jax import lax
from jax.experimental import pallas as pl
from jax.experimental.pallas import tpu as pltpu
from jax.sharding import PartitionSpec as P

KVH = 8
HD = 128
GQ = 8
STEPS = 4
PAGE = 128
SEL = 4

LANES = 128
ROWS = GQ * STEPS
HALF = 16
BODY = KVH * ROWS
COLS = BODY // HALF
SECOND = 3 * COLS
PAIR = 2 * BODY + HALF
LONE = BODY + HALF
EMPTY = -1e30
SCALE = math.log2(math.e) / math.sqrt(HD)
VMEM_BYTES = 24 * 1024 * 1024
BF16 = jnp.bfloat16
F32 = jnp.float32
IN_VMEM = pl.BlockSpec(memory_space=pltpu.VMEM)
IN_SMEM = pl.BlockSpec(memory_space=pltpu.SMEM)


def params():
    return pltpu.CompilerParams(vmem_limit_bytes=VMEM_BYTES)


def cost(flops, moved):
    return pl.CostEstimate(flops=flops, bytes_accessed=moved, transcendentals=0)


def list_rows(requests):
    return -(-2 * requests // HALF) * HALF


def lane_ids(rows=HALF):
    return lax.broadcasted_iota(jnp.int32, (rows, LANES), 1)


def pack_stats(stats):
    lanes = lane_ids()
    used = (lanes < COLS) | ((lanes >= SECOND) & (lanes < SECOND + COLS))
    stats = jnp.where(used, stats, 0.0)
    high = stats.astype(BF16).astype(F32)
    rest = stats - high
    middle = rest.astype(BF16).astype(F32)
    low = rest - middle
    return (high + pltpu.roll(middle, COLS, 1) + pltpu.roll(low, 2 * COLS, 1)).astype(BF16)


def unpack_stats(tile):
    tile = tile.astype(F32)
    return tile + pltpu.roll(tile, LANES - COLS, 1) + pltpu.roll(tile, LANES - 2 * COLS, 1)


def tile_start(index):
    half, head = divmod(index, KVH)
    return head * ROWS + half * HALF


def by_lane(columns, first=0):
    lanes = lane_ids() - first
    tile = jnp.zeros((HALF, LANES), F32)
    for head, values in enumerate(columns):
        for half in range(ROWS // HALF):
            part = values[half * HALF : (half + 1) * HALF, :]
            tile = jnp.where(lanes == half * KVH + head, part, tile)
    return tile


def attend(requests):
    across = (((1,), (1,)), ((), ()))
    along = (((1,), (0,)), ((), ()))
    heads = [(q, k, v, r[3]) for r in requests for q, k, v in zip(*r[:3])]
    scores = [lax.dot_general(q, k, across, preferred_element_type=F32) for q, k, _, _ in heads]
    scores = [jnp.where(head[3], s * SCALE, EMPTY) for s, head in zip(scores, heads)]
    tops = [jnp.max(s, axis=1, keepdims=True) for s in scores]
    weights = [jnp.exp2(s - t).astype(BF16) for s, t in zip(scores, tops)]
    mixed = [lax.dot_general(w, head[2], along, preferred_element_type=F32) for w, head in zip(weights, heads)]
    ones = jnp.ones((weights[0].shape[1], LANES), BF16)
    total = lax.dot_general(jnp.concatenate(weights, axis=0), ones, along, preferred_element_type=F32)
    totals = [total[number * ROWS : (number + 1) * ROWS, :] for number in range(len(heads))]
    results = []
    for number, request in enumerate(requests):
        mine = slice(number * KVH, (number + 1) * KVH)
        first = request[4]
        level = by_lane(tops[mine], first) + jnp.log2(jnp.maximum(by_lane(totals[mine], first), 1.0))
        results.append(([m / t for m, t in zip(mixed[mine], totals[mine])], level))
    return results


def relayout_kernel(owners, place_ref, queries_ref, *outs):
    group = lax.div(place_ref[0], owners)
    for d, out in enumerate(outs):
        values = queries_ref[group ^ d].astype(F32)
        for head in range(KVH):
            first = head * GQ
            parts = [values[:, (first + g) * HD : (first + g + 1) * HD] for g in range(GQ)]
            out[head * ROWS : (head + 1) * ROWS, :] = jnp.concatenate(parts, axis=0).astype(BF16)


def relayout(place, owners, queries):
    groups = queries.shape[0]
    return pl.pallas_call(
        functools.partial(relayout_kernel, owners),
        out_shape=[jax.ShapeDtypeStruct((BODY, HD), BF16)] * groups,
        in_specs=[IN_SMEM, IN_VMEM],
        out_specs=[IN_VMEM] * groups,
        compiler_params=params(),
        cost_estimate=cost(0, 4 * queries.size),
    )(place, queries)


def new_kernel(owners, place_ref, *refs):
    group = lax.div(place_ref[0], owners)
    queries, (new_ref, out_ref, level_ref) = refs[:-3], refs[-3:]
    step = lax.broadcasted_iota(jnp.int32, (ROWS, STEPS), 0) % STEPS
    usable = lax.broadcasted_iota(jnp.int32, (ROWS, STEPS), 1) <= step
    for d, query in enumerate(queries):
        new = new_ref[group ^ d]
        heads = [new[:, head * HD : (head + 1) * HD] for head in range(2 * KVH)]
        rows = [query[head * ROWS : (head + 1) * ROWS, :] for head in range(KVH)]
        [(mixed, level)] = attend([(rows, heads[:KVH], heads[KVH:], usable, 0)])
        for head, values in enumerate(mixed):
            out_ref[d, head * ROWS : (head + 1) * ROWS, :] = values
        level_ref[d] = level


def new_tokens(place, owners, queries, new_kv):
    groups = len(queries)
    return pl.pallas_call(
        functools.partial(new_kernel, owners),
        out_shape=[
            jax.ShapeDtypeStruct((groups, BODY, HD), F32),
            jax.ShapeDtypeStruct((groups, HALF, LANES), F32),
        ],
        in_specs=[IN_SMEM] + [IN_VMEM] * (groups + 1),
        out_specs=[IN_VMEM, IN_VMEM],
        compiler_params=params(),
        cost_estimate=cost(groups * KVH * 4 * ROWS * HD * HD, groups * BODY * HD * 6),
    )(place, *queries, new_kv)


def page_lists(page_owner, page_index, lengths):
    lanes = jnp.arange(LANES, dtype=jnp.int32)[None, None, :]
    counts = jnp.clip(lengths[:, None] - jnp.arange(SEL, dtype=jnp.int32)[None, :] * PAGE, 0, PAGE)
    named = page_owner[:, :, None] == lanes
    return (
        jnp.sum(jnp.where(named, counts[:, :, None], 0), axis=1),
        jnp.sum(jnp.where(named, page_index, 0), axis=1),
    )


def payload_kernel(after, counts_ref, pages_ref, *refs):
    visits, out = refs[: len(refs) - 1 - after], refs[-1]
    for number, visit in enumerate(visits):
        out[number * BODY : (number + 1) * BODY, :] = visit[...]
    tables = [counts_ref[...].astype(F32), pages_ref[...].astype(F32)]
    short = out.shape[0] - len(visits) * BODY - 2 * tables[0].shape[0]
    if short:
        tables.append(jnp.zeros((short, LANES), F32))
    out[len(visits) * BODY :, :] = jnp.concatenate(tables, axis=0).astype(BF16)


def payload(lists, visits, after=()):
    rows = len(visits) * BODY + list_rows(lists[0].shape[0])
    return pl.pallas_call(
        functools.partial(payload_kernel, len(after)),
        out_shape=jax.ShapeDtypeStruct((rows, HD), BF16),
        in_specs=[IN_VMEM] * (2 + len(visits) + len(after)),
        out_specs=IN_VMEM,
        compiler_params=params(),
        cost_estimate=cost(0, 4 * rows * HD),
    )(*lists, *visits, *after)


def touch_kernel(after_ref, cache_ref, out_ref):
    out_ref[...] = cache_ref[0, :HALF, :HD]


def touch(kv_cache, after):
    return pl.pallas_call(
        touch_kernel,
        out_shape=jax.ShapeDtypeStruct((HALF, HD), BF16),
        in_specs=[IN_VMEM, IN_VMEM],
        out_specs=IN_VMEM,
        compiler_params=params(),
        cost_estimate=cost(0, 2 * HALF * HD),
    )(after, kv_cache)


def item_kernel(slots, visitors, owners, place_ref, cache_ref, *refs):
    sides, each = len(slots), len(slots[0])
    entries = sides * each
    query_refs, (out_ref, rows_ref, level_ref, code_ref, order_ref) = refs[:sides], refs[sides:]
    group, owner = lax.div(place_ref[0], owners), lax.rem(place_ref[0], owners)
    lists = list_rows(visitors)
    rows = lax.broadcasted_iota(jnp.int32, (lists, LANES), 0)
    lanes = lane_ids()
    codes = []
    for side, query_ref in enumerate(query_refs):
        table = query_ref[each * BODY :, :].astype(F32)
        table = jnp.where(lane_ids(lists) == owner, table, 0.0)
        for pair in range(each // 2):
            factor = jnp.zeros((lists, LANES), F32)
            for second in range(2):
                row = group ^ slots[side][2 * pair + second]
                factor = jnp.where(rows == row, float(4096**second), factor)
                factor = jnp.where(rows == row + visitors, float(256 * 4096**second), factor)
            codes.append(jnp.sum(table * factor).astype(jnp.int32))
        rows_ref[side * each * BODY : (side + 1) * each * BODY, :] = query_ref[: each * BODY, :]

    for entry in range(entries):
        out = entry // 2 * PAIR + entry % 2 * BODY
        out_ref[out : out + BODY, :] = jnp.zeros((BODY, HD), BF16)
        first = entry % 2 * SECOND
        level_ref[entry] = jnp.where((lanes >= first) & (lanes < first + COLS), EMPTY, 0.0)
    found = jnp.int32(0)
    for entry in range(entries):
        code = (codes[entry // 2] >> (12 * (entry % 2))) & 4095
        code_ref[entry] = code
        order_ref[found] = entry
        found = found + jnp.where((code & 255) > 0, 1, 0)
    order_ref[found] = order_ref[jnp.maximum(found - 1, 0)]
    tokens = lax.broadcasted_iota(jnp.int32, (ROWS, PAGE), 1)

    @pl.loop(0, (found + 1) >> 1)
    def _(two):
        requests, places = [], []
        for number in range(2):
            entry = order_ref[2 * two + number]
            code = code_ref[entry]
            page, odd = code >> 8, entry & 1
            start = entry * BODY
            queries = [rows_ref[pl.ds(pl.multiple_of(start + h * ROWS, HALF), ROWS), :] for h in range(KVH)]
            keys = [cache_ref[page, :, h * HD : (h + 1) * HD] for h in range(KVH)]
            values = [cache_ref[page, :, (KVH + h) * HD : (KVH + h + 1) * HD] for h in range(KVH)]
            requests.append((queries, keys, values, tokens < (code & 255), odd * SECOND))
            places.append((entry, (entry >> 1) * PAIR + odd * BODY))
        for (mixed, level), (entry, out) in zip(attend(requests), places):
            for head, part in enumerate(mixed):
                out_ref[pl.ds(pl.multiple_of(out + head * ROWS, HALF), ROWS), :] = part.astype(BF16)
            level_ref[entry] = level

    for pair in range(entries // 2):
        start = pair * PAIR + 2 * BODY
        out_ref[start : start + HALF, :] = pack_stats(level_ref[2 * pair] + level_ref[2 * pair + 1])


def items(place, owners, kv_cache, payloads, slots, visitors):
    count = sum(len(row) for row in slots)
    return pl.pallas_call(
        functools.partial(item_kernel, slots, visitors, owners),
        out_shape=jax.ShapeDtypeStruct((count // 2 * PAIR, HD), BF16),
        in_specs=[IN_SMEM] + [IN_VMEM] * (1 + len(slots)),
        out_specs=IN_VMEM,
        scratch_shapes=[
            pltpu.VMEM((count * BODY, HD), BF16),
            pltpu.VMEM((count, HALF, LANES), F32),
            pltpu.SMEM((count,), jnp.int32),
            pltpu.SMEM((count + 1,), jnp.int32),
        ],
        compiler_params=params(),
        cost_estimate=cost(count * KVH * 4 * ROWS * HD * PAGE, count * PAGE * kv_cache.shape[2] * 2),
    )(place, kv_cache, *payloads)


def blend(levels):
    peak = functools.reduce(jnp.maximum, levels)
    shares = [jnp.exp2(level - peak) for level in levels]
    total = functools.reduce(jnp.add, shares)
    return [share / total for share in shares], peak + jnp.log2(total)


def mix(shares, refs, start, first_lane):
    values = []
    for index in range(COLS):
        row, lane = start + tile_start(index), first_lane + index
        tiles = [ref[row : row + HALF, :].astype(F32) for ref in refs]
        total = tiles[0]
        for share, tile in zip(shares[1:], tiles[1:]):
            total = total + share[:, lane : lane + 1] * (tile - tiles[0])
        values.append(total)
    return values


def merge_kernel(first, arrived_ref, own_ref, out_ref):
    for pair in range(out_ref.shape[0] // PAIR):
        part = slice(pair * PAIR, (pair + 1) * PAIR)
        arrived, own, out = arrived_ref.at[part], own_ref.at[first + pair * PAIR : first + (pair + 1) * PAIR], out_ref.at[part]
        shares, level = blend([unpack_stats(ref[2 * BODY : PAIR, :]) for ref in (arrived, own)])
        values = [mix(shares, (arrived, own), second * BODY, second * SECOND) for second in range(2)]
        for second in range(2):
            for index in range(COLS):
                row = second * BODY + tile_start(index)
                out[row : row + HALF, :] = values[second][index].astype(BF16)
        out[2 * BODY : PAIR, :] = pack_stats(level)


def merge(arrived, own):
    own, first = own
    return pl.pallas_call(
        functools.partial(merge_kernel, first),
        out_shape=jax.ShapeDtypeStruct(arrived.shape, BF16),
        in_specs=[IN_VMEM, IN_VMEM],
        out_specs=IN_VMEM,
        compiler_params=params(),
        cost_estimate=cost(0, 6 * arrived.size),
    )(arrived, own)


def gather_kernel(first, ahead_ref, behind_ref, own_ref, *outs):
    for pair in range(len(outs) // 2):
        part = slice(pair * PAIR, (pair + 1) * PAIR)
        own = own_ref.at[first + pair * PAIR : first + (pair + 1) * PAIR]
        sources = [own, ahead_ref.at[part], behind_ref.at[part]]
        shares, level = blend([unpack_stats(ref[2 * BODY : PAIR, :]) for ref in sources])
        values = [mix(shares, sources, second * BODY, second * SECOND) for second in range(2)]
        for second in range(2):
            out = outs[2 * pair + second]
            for index in range(COLS):
                row = tile_start(index)
                out[row : row + HALF, :] = values[second][index].astype(BF16)
            here = pltpu.roll(level, LANES - SECOND, 1) if second else level
            out[BODY:LONE, :] = pack_stats(here)


def gather(ahead, behind, own):
    pairs = ahead.shape[0] // PAIR
    own, first = own
    return pl.pallas_call(
        functools.partial(gather_kernel, first),
        out_shape=[jax.ShapeDtypeStruct((LONE, HD), BF16)] * (2 * pairs),
        in_specs=[IN_VMEM] * 3,
        out_specs=[IN_VMEM] * (2 * pairs),
        compiler_params=params(),
        cost_estimate=cost(0, 8 * pairs * PAIR * HD),
    )(ahead, behind, own)


def final_kernel(first, early, owners, place_ref, *refs):
    earlier, parts = refs[:early], refs[early:-4]
    new_ref, level_ref, out_ref, rows_ref = refs[-4:]
    group = lax.div(place_ref[0], owners)
    for number, part in enumerate(parts):
        d = first + number
        shares, _ = blend([unpack_stats(part[BODY:LONE, :]), level_ref[d]])
        for index, tile in enumerate(mix(shares, (part, new_ref.at[d]), 0, 0)):
            row = tile_start(index)
            rows_ref[number, row : row + HALF, :] = tile
    for number in range(len(parts)):
        row = group ^ (first + number) if early else number
        for head in range(KVH * GQ):
            tile = rows_ref[number, head * STEPS : (head + 1) * STEPS, :]
            out_ref[row, :, head * HD : (head + 1) * HD] = tile.astype(BF16)
    for ref in earlier:
        for number in range(ref.shape[0]):
            out_ref[group ^ (len(parts) + number)] = ref[number]


def final(place, owners, parts, first, new_out, new_level, earlier=()):
    requests = len(parts) + sum(e.shape[0] for e in earlier)
    return pl.pallas_call(
        functools.partial(final_kernel, first, len(earlier), owners),
        out_shape=jax.ShapeDtypeStruct((requests, STEPS, KVH * GQ * HD), BF16),
        in_specs=[IN_SMEM] + [IN_VMEM] * (len(earlier) + len(parts) + 2),
        out_specs=IN_VMEM,
        scratch_shapes=[pltpu.VMEM((len(parts), BODY, HD), F32)],
        compiler_params=params(),
        cost_estimate=cost(0, len(parts) * BODY * HD * 8),
    )(place, *earlier, *parts, new_out, new_level)


def ring_order(owners):
    return list(range(0, owners, 2)) + list(range(owners - 1, 0, -2))


def per_device(queries, new_kv, kv_cache, page_owner, page_index, lengths):
    groups = lax.axis_size("grp")
    owners = lax.axis_size("cache")
    requests = queries.shape[0]
    assert requests == groups and requests % 4 == 0 and owners <= LANES
    reach = owners // 2
    order = ring_order(owners)
    forward = [(order[i], order[(i + 1) % owners]) for i in range(owners)]
    backward = [(b, a) for a, b in forward]
    place = jnp.reshape(lax.axis_index(("grp", "cache")), (1,)).astype(jnp.int32)

    def swap(array, d):
        return lax.ppermute(array, "grp", [(g, g ^ d) for g in range(groups)]) if d else array

    rows = relayout(place, owners, queries)
    visits = [rows[0]] + [None] * (groups - 1)
    for d in range(groups - 1, 0, -1):
        visits[d] = swap(rows[d], d)
    lists = page_lists(page_owner, page_index, lengths)

    cut = requests // 2
    slots = [list(range(cut)), list(range(cut, requests))]
    owned = functools.partial(items, place, owners, kv_cache, visitors=requests)

    def up(array):
        return lax.ppermute(array, "cache", forward)

    def down(array):
        return lax.ppermute(array, "cache", backward)

    def after(array, *others):
        return lax.optimization_barrier((array, others))[0]

    blocks = [payload(lists, visits[:cut])]
    blocks.append(payload(lists, visits[cut:], [touch(kv_cache, blocks[0])]))
    below, above = [up(block) for block in blocks], [down(block) for block in blocks]
    size = cut // 2 * PAIR
    both = owned(blocks, slots)
    parts = {(0, 0): (both, 0), (1, 0): (both, size)}
    new_out, new_level = new_tokens(place, owners, [after(rows[0], both), *rows[1:]], new_kv)
    done = [[both], [both, new_level]]
    for step in range(1, reach):
        for half in range(2):
            if step > 1:
                below[half], above[half] = up(below[half]), down(above[half])
            below[half], above[half] = after(below[half], *done[half]), after(above[half], *done[half])
            both = owned([below[half], above[half]], [slots[half]] * 2)
            parts[half, -step], parts[half, step] = (both, 0), (both, size)
            done[half] = [both]
    far = owned([up(below[0])], slots[:1]), owned([down(above[1])], slots[1:])

    arrived = []
    for half in range(2):
        for move, sign in ((up, 1), (down, -1)):
            if half == (0 if sign == 1 else 1):
                chain, steps = far[half], range(reach - 1, -1, -1)
            else:
                own, first = parts[half, sign * (reach - 1)]
                chain, steps = own[first : first + size], range(reach - 2, -1, -1)
            for step in steps:
                chain = move(chain)
                if step > 0:
                    chain = merge(chain, parts[half, sign * step])
            arrived.append(chain)
    back = gather(arrived[2], arrived[3], parts[1, 0])
    front = gather(arrived[0], arrived[1], (after(parts[0, 0][0], *back), 0))
    home = [swap(part, d) for d, part in enumerate(front + back)]
    early = final(place, owners, home[cut:], cut, new_out, new_level)
    return final(place, owners, home[:cut], 0, new_out, new_level, [early])


def solution(mesh):
    in_specs = (
        P(("grp", "cache"), None, None),
        P(("grp", "cache"), None, None),
        P(("grp", "cache"), None, None),
        P(("grp", "cache"), None),
        P(("grp", "cache"), None, None),
        P(("grp", "cache")),
    )
    out_specs = P(("grp", "cache"), None, None)
    return jax.shard_map(
        per_device, mesh=mesh, in_specs=in_specs, out_specs=out_specs, check_vma=False
    )
```

```python
import functools
import math

import jax
import jax.numpy as jnp
from jax import lax
from jax.experimental import pallas as pl
from jax.experimental.pallas import tpu as pltpu
from jax.sharding import PartitionSpec as P

KVH = 8
HD = 128
GQ = 8
STEPS = 4
PAGE = 128
SEL = 4

LANES = 128
ROWS = GQ * STEPS
HALF = 16
BODY = KVH * ROWS
COLS = BODY // HALF
SECOND = 3 * COLS
PAIR = 2 * BODY + HALF
LONE = BODY + HALF
EMPTY = -1e30
SCALE = math.log2(math.e) / math.sqrt(HD)
VMEM_BYTES = 24 * 1024 * 1024
BF16 = jnp.bfloat16
F32 = jnp.float32
IN_VMEM = pl.BlockSpec(memory_space=pltpu.VMEM)
IN_SMEM = pl.BlockSpec(memory_space=pltpu.SMEM)


def params():
    return pltpu.CompilerParams(vmem_limit_bytes=VMEM_BYTES)


def cost(flops, moved):
    return pl.CostEstimate(flops=flops, bytes_accessed=moved, transcendentals=0)


def list_rows(requests):
    return -(-2 * requests // HALF) * HALF


def lane_ids(rows=HALF):
    return lax.broadcasted_iota(jnp.int32, (rows, LANES), 1)


def pack_stats(stats):
    lanes = lane_ids()
    used = (lanes < COLS) | ((lanes >= SECOND) & (lanes < SECOND + COLS))
    stats = jnp.where(used, stats, 0.0)
    high = stats.astype(BF16).astype(F32)
    rest = stats - high
    middle = rest.astype(BF16).astype(F32)
    low = rest - middle
    return (high + pltpu.roll(middle, COLS, 1) + pltpu.roll(low, 2 * COLS, 1)).astype(BF16)


def unpack_stats(tile):
    tile = tile.astype(F32)
    return tile + pltpu.roll(tile, LANES - COLS, 1) + pltpu.roll(tile, LANES - 2 * COLS, 1)


def tile_start(index):
    half, head = divmod(index, KVH)
    return head * ROWS + half * HALF


def by_lane(columns, first=0):
    lanes = lane_ids() - first
    tile = jnp.zeros((HALF, LANES), F32)
    for head, values in enumerate(columns):
        for half in range(ROWS // HALF):
            part = values[half * HALF : (half + 1) * HALF, :]
            tile = jnp.where(lanes == half * KVH + head, part, tile)
    return tile


def attend(requests):
    across = (((1,), (1,)), ((), ()))
    along = (((1,), (0,)), ((), ()))
    heads = [(q, k, v, r[3]) for r in requests for q, k, v in zip(*r[:3])]
    scores = [lax.dot_general(q, k, across, preferred_element_type=F32) for q, k, _, _ in heads]
    scores = [jnp.where(head[3], s * SCALE, EMPTY) for s, head in zip(scores, heads)]
    tops = [jnp.max(s, axis=1, keepdims=True) for s in scores]
    weights = [jnp.exp2(s - t).astype(BF16) for s, t in zip(scores, tops)]
    mixed = [lax.dot_general(w, head[2], along, preferred_element_type=F32) for w, head in zip(weights, heads)]
    ones = jnp.ones((weights[0].shape[1], LANES), BF16)
    total = lax.dot_general(jnp.concatenate(weights, axis=0), ones, along, preferred_element_type=F32)
    totals = [total[number * ROWS : (number + 1) * ROWS, :] for number in range(len(heads))]
    results = []
    for number, request in enumerate(requests):
        mine = slice(number * KVH, (number + 1) * KVH)
        first = request[4]
        level = by_lane(tops[mine], first) + jnp.log2(jnp.maximum(by_lane(totals[mine], first), 1.0))
        results.append(([m / t for m, t in zip(mixed[mine], totals[mine])], level))
    return results


def relayout_kernel(owners, place_ref, queries_ref, *outs):
    group = lax.div(place_ref[0], owners)
    for d, out in enumerate(outs):
        values = queries_ref[group ^ d].astype(F32)
        for head in range(KVH):
            first = head * GQ
            parts = [values[:, (first + g) * HD : (first + g + 1) * HD] for g in range(GQ)]
            out[head * ROWS : (head + 1) * ROWS, :] = jnp.concatenate(parts, axis=0).astype(BF16)


def relayout(place, owners, queries):
    groups = queries.shape[0]
    return pl.pallas_call(
        functools.partial(relayout_kernel, owners),
        out_shape=[jax.ShapeDtypeStruct((BODY, HD), BF16)] * groups,
        in_specs=[IN_SMEM, IN_VMEM],
        out_specs=[IN_VMEM] * groups,
        compiler_params=params(),
        cost_estimate=cost(0, 4 * queries.size),
    )(place, queries)


def new_kernel(owners, place_ref, *refs):
    group = lax.div(place_ref[0], owners)
    queries, (new_ref, out_ref, level_ref) = refs[:-3], refs[-3:]
    step = lax.broadcasted_iota(jnp.int32, (ROWS, STEPS), 0) % STEPS
    usable = lax.broadcasted_iota(jnp.int32, (ROWS, STEPS), 1) <= step
    for d, query in enumerate(queries):
        new = new_ref[group ^ d]
        heads = [new[:, head * HD : (head + 1) * HD] for head in range(2 * KVH)]
        rows = [query[head * ROWS : (head + 1) * ROWS, :] for head in range(KVH)]
        [(mixed, level)] = attend([(rows, heads[:KVH], heads[KVH:], usable, 0)])
        for head, values in enumerate(mixed):
            out_ref[d, head * ROWS : (head + 1) * ROWS, :] = values
        level_ref[d] = level


def new_tokens(place, owners, queries, new_kv):
    groups = len(queries)
    return pl.pallas_call(
        functools.partial(new_kernel, owners),
        out_shape=[
            jax.ShapeDtypeStruct((groups, BODY, HD), F32),
            jax.ShapeDtypeStruct((groups, HALF, LANES), F32),
        ],
        in_specs=[IN_SMEM] + [IN_VMEM] * (groups + 1),
        out_specs=[IN_VMEM, IN_VMEM],
        compiler_params=params(),
        cost_estimate=cost(groups * KVH * 4 * ROWS * HD * HD, groups * BODY * HD * 6),
    )(place, *queries, new_kv)


def page_lists(page_owner, page_index, lengths):
    shape = page_owner.shape + (LANES,)
    named = page_owner[:, :, None] == lax.broadcasted_iota(jnp.int32, shape, 2)
    counts = jnp.clip(lengths[:, None, None] - lax.broadcasted_iota(jnp.int32, shape, 1) * PAGE, 0, PAGE)
    return (
        jnp.sum(jnp.where(named, counts, 0), axis=1),
        jnp.sum(jnp.where(named, page_index, 0), axis=1),
    )


def payload_kernel(after, counts_ref, pages_ref, *refs):
    visits, out = refs[: len(refs) - 1 - after], refs[-1]
    for number, visit in enumerate(visits):
        out[number * BODY : (number + 1) * BODY, :] = visit[...]
    tables = [counts_ref[...].astype(F32), pages_ref[...].astype(F32)]
    short = out.shape[0] - len(visits) * BODY - 2 * tables[0].shape[0]
    if short:
        tables.append(jnp.zeros((short, LANES), F32))
    out[len(visits) * BODY :, :] = jnp.concatenate(tables, axis=0).astype(BF16)


def payload(lists, visits, after=()):
    rows = len(visits) * BODY + list_rows(lists[0].shape[0])
    return pl.pallas_call(
        functools.partial(payload_kernel, len(after)),
        out_shape=jax.ShapeDtypeStruct((rows, HD), BF16),
        in_specs=[IN_VMEM] * (2 + len(visits) + len(after)),
        out_specs=IN_VMEM,
        compiler_params=params(),
        cost_estimate=cost(0, 4 * rows * HD),
    )(*lists, *visits, *after)


def touch_kernel(after_ref, cache_ref, out_ref):
    out_ref[...] = cache_ref[0, :HALF, :HD]


def touch(kv_cache, after):
    return pl.pallas_call(
        touch_kernel,
        out_shape=jax.ShapeDtypeStruct((HALF, HD), BF16),
        in_specs=[IN_VMEM, IN_VMEM],
        out_specs=IN_VMEM,
        compiler_params=params(),
        cost_estimate=cost(0, 2 * HALF * HD),
    )(after, kv_cache)


def item_kernel(slots, visitors, owners, place_ref, cache_ref, *refs):
    sides, each = len(slots), len(slots[0])
    entries = sides * each
    query_refs, (out_ref, rows_ref, level_ref, code_ref, order_ref) = refs[:sides], refs[sides:]
    group, owner = lax.div(place_ref[0], owners), lax.rem(place_ref[0], owners)
    lists = list_rows(visitors)
    rows = lax.broadcasted_iota(jnp.int32, (lists, LANES), 0)
    lanes = lane_ids()
    codes = []
    for side, query_ref in enumerate(query_refs):
        table = query_ref[each * BODY :, :].astype(F32)
        table = jnp.where(lane_ids(lists) == owner, table, 0.0)
        for pair in range(each // 2):
            factor = jnp.zeros((lists, LANES), F32)
            for second in range(2):
                row = group ^ slots[side][2 * pair + second]
                factor = jnp.where(rows == row, float(4096**second), factor)
                factor = jnp.where(rows == row + visitors, float(256 * 4096**second), factor)
            codes.append(jnp.sum(table * factor).astype(jnp.int32))
        rows_ref[side * each * BODY : (side + 1) * each * BODY, :] = query_ref[: each * BODY, :]

    for entry in range(entries):
        out = entry // 2 * PAIR + entry % 2 * BODY
        out_ref[out : out + BODY, :] = jnp.zeros((BODY, HD), BF16)
        first = entry % 2 * SECOND
        level_ref[entry] = jnp.where((lanes >= first) & (lanes < first + COLS), EMPTY, 0.0)
    found = jnp.int32(0)
    for entry in range(entries):
        code = (codes[entry // 2] >> (12 * (entry % 2))) & 4095
        code_ref[entry] = code
        order_ref[found] = entry
        found = found + jnp.where((code & 255) > 0, 1, 0)
    order_ref[found] = order_ref[jnp.maximum(found - 1, 0)]
    tokens = lax.broadcasted_iota(jnp.int32, (ROWS, PAGE), 1)

    @pl.loop(0, (found + 1) >> 1)
    def _(two):
        requests, places = [], []
        for number in range(2):
            entry = order_ref[2 * two + number]
            code = code_ref[entry]
            page, odd = code >> 8, entry & 1
            start = entry * BODY
            queries = [rows_ref[pl.ds(pl.multiple_of(start + h * ROWS, HALF), ROWS), :] for h in range(KVH)]
            keys = [cache_ref[page, :, h * HD : (h + 1) * HD] for h in range(KVH)]
            values = [cache_ref[page, :, (KVH + h) * HD : (KVH + h + 1) * HD] for h in range(KVH)]
            requests.append((queries, keys, values, tokens < (code & 255), odd * SECOND))
            places.append((entry, (entry >> 1) * PAIR + odd * BODY))
        for (mixed, level), (entry, out) in zip(attend(requests), places):
            for head, part in enumerate(mixed):
                out_ref[pl.ds(pl.multiple_of(out + head * ROWS, HALF), ROWS), :] = part.astype(BF16)
            level_ref[entry] = level

    for pair in range(entries // 2):
        start = pair * PAIR + 2 * BODY
        out_ref[start : start + HALF, :] = pack_stats(level_ref[2 * pair] + level_ref[2 * pair + 1])


def items(place, owners, kv_cache, payloads, slots, visitors):
    count = sum(len(row) for row in slots)
    return pl.pallas_call(
        functools.partial(item_kernel, slots, visitors, owners),
        out_shape=jax.ShapeDtypeStruct((count // 2 * PAIR, HD), BF16),
        in_specs=[IN_SMEM] + [IN_VMEM] * (1 + len(slots)),
        out_specs=IN_VMEM,
        scratch_shapes=[
            pltpu.VMEM((count * BODY, HD), BF16),
            pltpu.VMEM((count, HALF, LANES), F32),
            pltpu.SMEM((count,), jnp.int32),
            pltpu.SMEM((count + 1,), jnp.int32),
        ],
        compiler_params=params(),
        cost_estimate=cost(count * KVH * 4 * ROWS * HD * PAGE, count * PAGE * kv_cache.shape[2] * 2),
    )(place, kv_cache, *payloads)


def blend(levels):
    peak = functools.reduce(jnp.maximum, levels)
    shares = [jnp.exp2(level - peak) for level in levels]
    total = functools.reduce(jnp.add, shares)
    return [share / total for share in shares], peak + jnp.log2(total)


def mix(shares, refs, start, first_lane):
    values = []
    for index in range(COLS):
        row, lane = start + tile_start(index), first_lane + index
        tiles = [ref[row : row + HALF, :].astype(F32) for ref in refs]
        total = tiles[0]
        for share, tile in zip(shares[1:], tiles[1:]):
            total = total + share[:, lane : lane + 1] * (tile - tiles[0])
        values.append(total)
    return values


def merge_kernel(first, arrived_ref, own_ref, out_ref):
    for pair in range(out_ref.shape[0] // PAIR):
        part = slice(pair * PAIR, (pair + 1) * PAIR)
        arrived, own, out = arrived_ref.at[part], own_ref.at[first + pair * PAIR : first + (pair + 1) * PAIR], out_ref.at[part]
        shares, level = blend([unpack_stats(ref[2 * BODY : PAIR, :]) for ref in (arrived, own)])
        values = [mix(shares, (arrived, own), second * BODY, second * SECOND) for second in range(2)]
        for second in range(2):
            for index in range(COLS):
                row = second * BODY + tile_start(index)
                out[row : row + HALF, :] = values[second][index].astype(BF16)
        out[2 * BODY : PAIR, :] = pack_stats(level)


def merge(arrived, own):
    own, first = own
    return pl.pallas_call(
        functools.partial(merge_kernel, first),
        out_shape=jax.ShapeDtypeStruct(arrived.shape, BF16),
        in_specs=[IN_VMEM, IN_VMEM],
        out_specs=IN_VMEM,
        compiler_params=params(),
        cost_estimate=cost(0, 6 * arrived.size),
    )(arrived, own)


def split_kernel(firsts, *refs):
    arrays, outs = refs[: len(firsts)], refs[len(firsts) :]
    for pair in range(len(outs) // 2):
        start = pair * PAIR
        sources = [ref.at[first + start : first + start + PAIR] for ref, first in zip(arrays, firsts)]
        shares, level = blend([unpack_stats(ref[2 * BODY : PAIR, :]) for ref in sources])
        values = [mix(shares, sources, second * BODY, second * SECOND) for second in range(2)]
        for second in range(2):
            out = outs[2 * pair + second]
            for index in range(COLS):
                row = tile_start(index)
                out[row : row + HALF, :] = values[second][index].astype(BF16)
            here = pltpu.roll(level, LANES - SECOND, 1) if second else level
            out[BODY:LONE, :] = pack_stats(here)


def split(sources, requests):
    return pl.pallas_call(
        functools.partial(split_kernel, [first for _, first in sources]),
        out_shape=[jax.ShapeDtypeStruct((LONE, HD), BF16)] * requests,
        in_specs=[IN_VMEM] * len(sources),
        out_specs=[IN_VMEM] * requests,
        compiler_params=params(),
        cost_estimate=cost(0, 6 * requests * LONE * HD),
    )(*[array for array, _ in sources])


def final_kernel(first, early, owners, place_ref, *refs):
    earlier, parts = refs[:early], refs[early:-4]
    new_ref, level_ref, out_ref, rows_ref = refs[-4:]
    group = lax.div(place_ref[0], owners)
    count = len(parts) // 2
    for number in range(count):
        d = first + number
        both = (parts[2 * number], parts[2 * number + 1])
        shares, _ = blend([unpack_stats(part[BODY:LONE, :]) for part in both] + [level_ref[d]])
        for index, tile in enumerate(mix(shares, both + (new_ref.at[d],), 0, 0)):
            row = tile_start(index)
            rows_ref[number, row : row + HALF, :] = tile
    for number in range(count):
        row = group ^ (first + number) if early else number
        for head in range(KVH * GQ):
            tile = rows_ref[number, head * STEPS : (head + 1) * STEPS, :]
            out_ref[row, :, head * HD : (head + 1) * HD] = tile.astype(BF16)
    for ref in earlier:
        for number in range(ref.shape[0]):
            out_ref[group ^ (count + number)] = ref[number]


def final(place, owners, parts, first, new_out, new_level, earlier=()):
    count = len(parts) // 2
    requests = count + sum(e.shape[0] for e in earlier)
    return pl.pallas_call(
        functools.partial(final_kernel, first, len(earlier), owners),
        out_shape=jax.ShapeDtypeStruct((requests, STEPS, KVH * GQ * HD), BF16),
        in_specs=[IN_SMEM] + [IN_VMEM] * (len(earlier) + len(parts) + 2),
        out_specs=IN_VMEM,
        scratch_shapes=[pltpu.VMEM((count, BODY, HD), F32)],
        compiler_params=params(),
        cost_estimate=cost(0, count * BODY * HD * 10),
    )(place, *earlier, *parts, new_out, new_level)


def ring_order(owners):
    return list(range(0, owners, 2)) + list(range(owners - 1, 0, -2))


def per_device(queries, new_kv, kv_cache, page_owner, page_index, lengths):
    groups = lax.axis_size("grp")
    owners = lax.axis_size("cache")
    requests = queries.shape[0]
    assert requests == groups and requests % 4 == 0 and owners <= LANES
    reach = owners // 2
    order = ring_order(owners)
    forward = [(order[i], order[(i + 1) % owners]) for i in range(owners)]
    backward = [(b, a) for a, b in forward]
    place = jnp.reshape(lax.axis_index(("grp", "cache")), (1,)).astype(jnp.int32)

    def swap(array, d):
        return lax.ppermute(array, "grp", [(g, g ^ d) for g in range(groups)]) if d else array

    rows = relayout(place, owners, queries)
    visits = [rows[0]] + [None] * (groups - 1)
    for d in range(groups - 1, 0, -1):
        visits[d] = swap(rows[d], d)
    lists = page_lists(page_owner, page_index, lengths)

    cut = requests // 2
    slots = [list(range(cut)), list(range(cut, requests))]
    owned = functools.partial(items, place, owners, kv_cache, visitors=requests)

    def up(array):
        return lax.ppermute(array, "cache", forward)

    def down(array):
        return lax.ppermute(array, "cache", backward)

    def after(array, *others):
        return lax.optimization_barrier((array, others))[0]

    blocks = [payload(lists, visits[:cut])]
    blocks.append(payload(lists, visits[cut:], [touch(kv_cache, blocks[0])]))
    below, above = [up(block) for block in blocks], [down(block) for block in blocks]
    size = cut // 2 * PAIR
    both = owned(blocks, slots)
    parts = {(0, 0): (both, 0), (1, 0): (both, size)}
    new_out, new_level = new_tokens(place, owners, [after(rows[0], both), *rows[1:]], new_kv)
    done = [[both], [both, new_level]]
    for step in range(1, reach):
        for half in range(2):
            if step > 1:
                below[half], above[half] = up(below[half]), down(above[half])
            below[half], above[half] = after(below[half], *done[half]), after(above[half], *done[half])
            both = owned([below[half], above[half]], [slots[half]] * 2)
            parts[half, -step], parts[half, step] = (both, 0), (both, size)
            done[half] = [both]
    far = owned([up(below[0])], slots[:1]), owned([down(above[1])], slots[1:])

    def straight(array, ring, d):
        pairs = [(g * owners + a, (g ^ d) * owners + b) for g in range(groups) for a, b in ring]
        return lax.ppermute(array, ("grp", "cache"), pairs)

    home = [None] * requests
    for half in range(2):
        move, ring, sign = ((up, forward, 1), (down, backward, -1))[half]
        chain = far[half]
        for step in range(reach - 1, 1, -1):
            chain = merge(move(chain), parts[half, sign * step])
        long = split([(move(chain), 0), parts[half, sign]], cut)
        move, sign = ((down, -1), (up, 1))[half]
        own, first = parts[half, sign * (reach - 1)]
        chain = move(own[first : first + size])
        for step in range(reach - 2, 0, -1):
            chain = move(merge(chain, parts[half, sign * step]))
        short = split([parts[half, 0], (chain, 0)], cut)
        for number, d in enumerate(slots[half]):
            home[d] = [swap(short[number], d), straight(long[number], ring, d)]
    early = final(place, owners, sum(home[cut:], []), cut, new_out, new_level)
    return final(place, owners, sum(home[:cut], []), 0, new_out, new_level, [early])


def solution(mesh):
    in_specs = (
        P(("grp", "cache"), None, None),
        P(("grp", "cache"), None, None),
        P(("grp", "cache"), None, None),
        P(("grp", "cache"), None),
        P(("grp", "cache"), None, None),
        P(("grp", "cache")),
    )
    out_specs = P(("grp", "cache"), None, None)
    return jax.shard_map(
        per_device, mesh=mesh, in_specs=in_specs, out_specs=out_specs, check_vma=False
    )
```

```python
import functools
import math

import jax
import jax.numpy as jnp
from jax import lax
from jax.experimental import pallas as pl
from jax.experimental.pallas import tpu as pltpu
from jax.sharding import PartitionSpec as P

KVH = 8
HD = 128
GQ = 8
STEPS = 4
PAGE = 128
SEL = 4

LANES = 128
ROWS = GQ * STEPS
HALF = 16
BODY = KVH * ROWS
BATCH = 4
COLS = BODY // HALF
SECOND = 3 * COLS
PAIR = 2 * BODY + HALF
LONE = BODY + HALF
EMPTY = -1e30
SCALE = math.log2(math.e) / math.sqrt(HD)
VMEM_BYTES = 24 * 1024 * 1024
BF16 = jnp.bfloat16
F32 = jnp.float32
IN_VMEM = pl.BlockSpec(memory_space=pltpu.VMEM)
IN_SMEM = pl.BlockSpec(memory_space=pltpu.SMEM)


def params():
    return pltpu.CompilerParams(vmem_limit_bytes=VMEM_BYTES)


def cost(flops, moved):
    return pl.CostEstimate(flops=flops, bytes_accessed=moved, transcendentals=0)


def list_rows(requests):
    return -(-2 * requests // HALF) * HALF


def lane_ids(rows=HALF):
    return lax.broadcasted_iota(jnp.int32, (rows, LANES), 1)


def pack_stats(stats):
    lanes = lane_ids()
    used = (lanes < COLS) | ((lanes >= SECOND) & (lanes < SECOND + COLS))
    stats = jnp.where(used, stats, 0.0)
    high = stats.astype(BF16).astype(F32)
    rest = stats - high
    middle = rest.astype(BF16).astype(F32)
    low = rest - middle
    return (high + pltpu.roll(middle, COLS, 1) + pltpu.roll(low, 2 * COLS, 1)).astype(BF16)


def unpack_stats(tile):
    tile = tile.astype(F32)
    return tile + pltpu.roll(tile, LANES - COLS, 1) + pltpu.roll(tile, LANES - 2 * COLS, 1)


def tile_start(index):
    half, head = divmod(index, KVH)
    return head * ROWS + half * HALF


def by_lane(columns, first=0):
    lanes = lane_ids() - first
    tile = jnp.zeros((HALF, LANES), F32)
    for head, values in enumerate(columns):
        for half in range(ROWS // HALF):
            part = values[half * HALF : (half + 1) * HALF, :]
            tile = jnp.where(lanes == half * KVH + head, part, tile)
    return tile


def attend(requests):
    across = (((1,), (1,)), ((), ()))
    along = (((1,), (0,)), ((), ()))
    ones = jnp.ones((requests[0][2][0].shape[0], LANES), BF16)
    tops, mixed, totals = [[[] for _ in requests] for _ in range(3)]
    for batch in range(0, KVH, BATCH):
        heads = [(n, r[0][h], r[1][h], r[2][h], r[3]) for n, r in enumerate(requests) for h in range(batch, batch + BATCH)]
        scores = [lax.dot_general(q, k, across, preferred_element_type=F32) for _, q, k, _, _ in heads]
        scores = [jnp.where(head[4], s * SCALE, EMPTY) for s, head in zip(scores, heads)]
        top = [jnp.max(s, axis=1, keepdims=True) for s in scores]
        weights = [jnp.exp2(s - t).astype(BF16) for s, t in zip(scores, top)]
        total = lax.dot_general(jnp.concatenate(weights, axis=0), ones, along, preferred_element_type=F32)
        for place, (number, _, _, value, _) in enumerate(heads):
            tops[number].append(top[place])
            totals[number].append(total[place * ROWS : (place + 1) * ROWS, :])
            out = lax.dot_general(weights[place], value, along, preferred_element_type=F32)
            mixed[number].append(out / totals[number][-1])
    return [
        (m, by_lane(t, r[4]) + jnp.log2(jnp.maximum(by_lane(s, r[4]), 1.0)))
        for m, t, s, r in zip(mixed, tops, totals, requests)
    ]


def relayout_kernel(owners, place_ref, queries_ref, *outs):
    group = lax.div(place_ref[0], owners)
    for d, out in enumerate(outs):
        values = queries_ref[group ^ d].astype(F32)
        for head in range(KVH):
            first = head * GQ
            parts = [values[:, (first + g) * HD : (first + g + 1) * HD] for g in range(GQ)]
            out[head * ROWS : (head + 1) * ROWS, :] = jnp.concatenate(parts, axis=0).astype(BF16)


def relayout(place, owners, queries):
    groups = queries.shape[0]
    return pl.pallas_call(
        functools.partial(relayout_kernel, owners),
        out_shape=[jax.ShapeDtypeStruct((BODY, HD), BF16)] * groups,
        in_specs=[IN_SMEM, IN_VMEM],
        out_specs=[IN_VMEM] * groups,
        compiler_params=params(),
        cost_estimate=cost(0, 4 * queries.size),
    )(place, queries)


def new_kernel(owners, place_ref, *refs):
    group = lax.div(place_ref[0], owners)
    queries, (new_ref, out_ref, level_ref) = refs[:-3], refs[-3:]
    step = lax.broadcasted_iota(jnp.int32, (ROWS, STEPS), 0) % STEPS
    usable = lax.broadcasted_iota(jnp.int32, (ROWS, STEPS), 1) <= step
    for d, query in enumerate(queries):
        new = new_ref[group ^ d]
        heads = [new[:, head * HD : (head + 1) * HD] for head in range(2 * KVH)]
        rows = [query[head * ROWS : (head + 1) * ROWS, :] for head in range(KVH)]
        [(mixed, level)] = attend([(rows, heads[:KVH], heads[KVH:], usable, 0)])
        for head, values in enumerate(mixed):
            out_ref[d, head * ROWS : (head + 1) * ROWS, :] = values
        level_ref[d] = level


def new_tokens(place, owners, queries, new_kv):
    groups = len(queries)
    return pl.pallas_call(
        functools.partial(new_kernel, owners),
        out_shape=[
            jax.ShapeDtypeStruct((groups, BODY, HD), F32),
            jax.ShapeDtypeStruct((groups, HALF, LANES), F32),
        ],
        in_specs=[IN_SMEM] + [IN_VMEM] * (groups + 1),
        out_specs=[IN_VMEM, IN_VMEM],
        compiler_params=params(),
        cost_estimate=cost(groups * KVH * 4 * ROWS * HD * HD, groups * BODY * HD * 6),
    )(place, *queries, new_kv)


def page_lists(page_owner, page_index, lengths):
    shape = page_owner.shape + (LANES,)
    named = page_owner[:, :, None] == lax.broadcasted_iota(jnp.int32, shape, 2)
    counts = jnp.clip(lengths[:, None, None] - lax.broadcasted_iota(jnp.int32, shape, 1) * PAGE, 0, PAGE)
    return (
        jnp.sum(jnp.where(named, counts, 0), axis=1),
        jnp.sum(jnp.where(named, page_index, 0), axis=1),
    )


def payload_kernel(after, counts_ref, pages_ref, *refs):
    visits, out = refs[: len(refs) - 1 - after], refs[-1]
    for number, visit in enumerate(visits):
        out[number * BODY : (number + 1) * BODY, :] = visit[...]
    tables = [counts_ref[...].astype(F32), pages_ref[...].astype(F32)]
    short = out.shape[0] - len(visits) * BODY - 2 * tables[0].shape[0]
    if short:
        tables.append(jnp.zeros((short, LANES), F32))
    out[len(visits) * BODY :, :] = jnp.concatenate(tables, axis=0).astype(BF16)


def payload(lists, visits, after=()):
    rows = len(visits) * BODY + list_rows(lists[0].shape[0])
    return pl.pallas_call(
        functools.partial(payload_kernel, len(after)),
        out_shape=jax.ShapeDtypeStruct((rows, HD), BF16),
        in_specs=[IN_VMEM] * (2 + len(visits) + len(after)),
        out_specs=IN_VMEM,
        compiler_params=params(),
        cost_estimate=cost(0, 4 * rows * HD),
    )(*lists, *visits, *after)


def touch_kernel(after_ref, cache_ref, out_ref):
    out_ref[...] = cache_ref[0, :HALF, :HD]


def touch(kv_cache, after):
    return pl.pallas_call(
        touch_kernel,
        out_shape=jax.ShapeDtypeStruct((HALF, HD), BF16),
        in_specs=[IN_VMEM, IN_VMEM],
        out_specs=IN_VMEM,
        compiler_params=params(),
        cost_estimate=cost(0, 2 * HALF * HD),
    )(after, kv_cache)


def item_kernel(slots, visitors, owners, place_ref, cache_ref, *refs):
    sides, each = len(slots), len(slots[0])
    entries = sides * each
    query_refs, (out_ref, rows_ref, level_ref, code_ref, order_ref) = refs[:sides], refs[sides:]
    group, owner = lax.div(place_ref[0], owners), lax.rem(place_ref[0], owners)
    lists = list_rows(visitors)
    rows = lax.broadcasted_iota(jnp.int32, (lists, LANES), 0)
    lanes = lane_ids()
    codes = []
    for side, query_ref in enumerate(query_refs):
        table = query_ref[each * BODY :, :].astype(F32)
        table = jnp.where(lane_ids(lists) == owner, table, 0.0)
        for pair in range(each // 2):
            factor = jnp.zeros((lists, LANES), F32)
            for second in range(2):
                row = group ^ slots[side][2 * pair + second]
                factor = jnp.where(rows == row, float(4096**second), factor)
                factor = jnp.where(rows == row + visitors, float(256 * 4096**second), factor)
            codes.append(jnp.sum(table * factor).astype(jnp.int32))
        rows_ref[side * each * BODY : (side + 1) * each * BODY, :] = query_ref[: each * BODY, :]

    for entry in range(entries):
        out = entry // 2 * PAIR + entry % 2 * BODY
        out_ref[out : out + BODY, :] = jnp.zeros((BODY, HD), BF16)
        first = entry % 2 * SECOND
        level_ref[entry] = jnp.where((lanes >= first) & (lanes < first + COLS), EMPTY, 0.0)
    found = jnp.int32(0)
    for entry in range(entries):
        code = (codes[entry // 2] >> (12 * (entry % 2))) & 4095
        code_ref[entry] = code
        order_ref[found] = entry
        found = found + jnp.where((code & 255) > 0, 1, 0)
    order_ref[found] = order_ref[jnp.maximum(found - 1, 0)]
    tokens = lax.broadcasted_iota(jnp.int32, (ROWS, PAGE), 1)

    @pl.loop(0, (found + 1) >> 1)
    def _(two):
        requests, places = [], []
        for number in range(2):
            entry = order_ref[2 * two + number]
            code = code_ref[entry]
            page, odd = code >> 8, entry & 1
            start = entry * BODY
            queries = [rows_ref[pl.ds(pl.multiple_of(start + h * ROWS, HALF), ROWS), :] for h in range(KVH)]
            keys = [cache_ref[page, :, h * HD : (h + 1) * HD] for h in range(KVH)]
            values = [cache_ref[page, :, (KVH + h) * HD : (KVH + h + 1) * HD] for h in range(KVH)]
            requests.append((queries, keys, values, tokens < (code & 255), odd * SECOND))
            places.append((entry, (entry >> 1) * PAIR + odd * BODY))
        for (mixed, level), (entry, out) in zip(attend(requests), places):
            for head, part in enumerate(mixed):
                out_ref[pl.ds(pl.multiple_of(out + head * ROWS, HALF), ROWS), :] = part.astype(BF16)
            level_ref[entry] = level

    for pair in range(entries // 2):
        start = pair * PAIR + 2 * BODY
        out_ref[start : start + HALF, :] = pack_stats(level_ref[2 * pair] + level_ref[2 * pair + 1])


def items(place, owners, kv_cache, payloads, slots, visitors):
    count = sum(len(row) for row in slots)
    return pl.pallas_call(
        functools.partial(item_kernel, slots, visitors, owners),
        out_shape=jax.ShapeDtypeStruct((count // 2 * PAIR, HD), BF16),
        in_specs=[IN_SMEM] + [IN_VMEM] * (1 + len(slots)),
        out_specs=IN_VMEM,
        scratch_shapes=[
            pltpu.VMEM((count * BODY, HD), BF16),
            pltpu.VMEM((count, HALF, LANES), F32),
            pltpu.SMEM((count,), jnp.int32),
            pltpu.SMEM((count + 1,), jnp.int32),
        ],
        compiler_params=params(),
        cost_estimate=cost(count * KVH * 4 * ROWS * HD * PAGE, count * PAGE * kv_cache.shape[2] * 2),
    )(place, kv_cache, *payloads)


def blend(levels):
    peak = functools.reduce(jnp.maximum, levels)
    shares = [jnp.exp2(level - peak) for level in levels]
    total = functools.reduce(jnp.add, shares)
    return [share / total for share in shares], peak + jnp.log2(total)


def mix(shares, refs, start, first_lane):
    values = []
    for index in range(COLS):
        row, lane = start + tile_start(index), first_lane + index
        tiles = [ref[row : row + HALF, :].astype(F32) for ref in refs]
        total = tiles[0]
        for share, tile in zip(shares[1:], tiles[1:]):
            total = total + share[:, lane : lane + 1] * (tile - tiles[0])
        values.append(total)
    return values


def merge_kernel(first, arrived_ref, own_ref, out_ref):
    for pair in range(out_ref.shape[0] // PAIR):
        part = slice(pair * PAIR, (pair + 1) * PAIR)
        arrived, own, out = arrived_ref.at[part], own_ref.at[first + pair * PAIR : first + (pair + 1) * PAIR], out_ref.at[part]
        shares, level = blend([unpack_stats(ref[2 * BODY : PAIR, :]) for ref in (arrived, own)])
        values = [mix(shares, (arrived, own), second * BODY, second * SECOND) for second in range(2)]
        for second in range(2):
            for index in range(COLS):
                row = second * BODY + tile_start(index)
                out[row : row + HALF, :] = values[second][index].astype(BF16)
        out[2 * BODY : PAIR, :] = pack_stats(level)


def merge(arrived, own):
    own, first = own
    return pl.pallas_call(
        functools.partial(merge_kernel, first),
        out_shape=jax.ShapeDtypeStruct(arrived.shape, BF16),
        in_specs=[IN_VMEM, IN_VMEM],
        out_specs=IN_VMEM,
        compiler_params=params(),
        cost_estimate=cost(0, 6 * arrived.size),
    )(arrived, own)


def split_kernel(firsts, *refs):
    arrays, outs = refs[: len(firsts)], refs[len(firsts) :]
    for pair in range(len(outs) // 2):
        start = pair * PAIR
        sources = [ref.at[first + start : first + start + PAIR] for ref, first in zip(arrays, firsts)]
        shares, level = blend([unpack_stats(ref[2 * BODY : PAIR, :]) for ref in sources])
        values = [mix(shares, sources, second * BODY, second * SECOND) for second in range(2)]
        for second in range(2):
            out = outs[2 * pair + second]
            for index in range(COLS):
                row = tile_start(index)
                out[row : row + HALF, :] = values[second][index].astype(BF16)
            here = pltpu.roll(level, LANES - SECOND, 1) if second else level
            out[BODY:LONE, :] = pack_stats(here)


def split(sources, requests):
    return pl.pallas_call(
        functools.partial(split_kernel, [first for _, first in sources]),
        out_shape=[jax.ShapeDtypeStruct((LONE, HD), BF16)] * requests,
        in_specs=[IN_VMEM] * len(sources),
        out_specs=[IN_VMEM] * requests,
        compiler_params=params(),
        cost_estimate=cost(0, 6 * requests * LONE * HD),
    )(*[array for array, _ in sources])


def final_kernel(first, early, owners, place_ref, *refs):
    earlier, parts = refs[:early], refs[early:-4]
    new_ref, level_ref, out_ref, rows_ref = refs[-4:]
    group = lax.div(place_ref[0], owners)
    count = len(parts) // 2
    for number in range(count):
        d = first + number
        both = (parts[2 * number], parts[2 * number + 1])
        shares, _ = blend([unpack_stats(part[BODY:LONE, :]) for part in both] + [level_ref[d]])
        for index, tile in enumerate(mix(shares, both + (new_ref.at[d],), 0, 0)):
            row = tile_start(index)
            rows_ref[number, row : row + HALF, :] = tile
    for number in range(count):
        row = group ^ (first + number) if early else number
        for head in range(KVH * GQ):
            tile = rows_ref[number, head * STEPS : (head + 1) * STEPS, :]
            out_ref[row, :, head * HD : (head + 1) * HD] = tile.astype(BF16)
    for ref in earlier:
        for number in range(ref.shape[0]):
            out_ref[group ^ (count + number)] = ref[number]


def final(place, owners, parts, first, new_out, new_level, earlier=()):
    count = len(parts) // 2
    requests = count + sum(e.shape[0] for e in earlier)
    return pl.pallas_call(
        functools.partial(final_kernel, first, len(earlier), owners),
        out_shape=jax.ShapeDtypeStruct((requests, STEPS, KVH * GQ * HD), BF16),
        in_specs=[IN_SMEM] + [IN_VMEM] * (len(earlier) + len(parts) + 2),
        out_specs=IN_VMEM,
        scratch_shapes=[pltpu.VMEM((count, BODY, HD), F32)],
        compiler_params=params(),
        cost_estimate=cost(0, count * BODY * HD * 10),
    )(place, *earlier, *parts, new_out, new_level)


def ring_order(owners):
    return list(range(0, owners, 2)) + list(range(owners - 1, 0, -2))


def per_device(queries, new_kv, kv_cache, page_owner, page_index, lengths):
    groups = lax.axis_size("grp")
    owners = lax.axis_size("cache")
    requests = queries.shape[0]
    assert requests == groups and requests % 4 == 0 and owners <= LANES
    reach = owners // 2
    order = ring_order(owners)
    forward = [(order[i], order[(i + 1) % owners]) for i in range(owners)]
    backward = [(b, a) for a, b in forward]
    place = jnp.reshape(lax.axis_index(("grp", "cache")), (1,)).astype(jnp.int32)

    def swap(array, d):
        return lax.ppermute(array, "grp", [(g, g ^ d) for g in range(groups)]) if d else array

    rows = relayout(place, owners, queries)
    visits = [rows[0]] + [None] * (groups - 1)
    for d in range(groups - 1, 0, -1):
        visits[d] = swap(rows[d], d)
    lists = page_lists(page_owner, page_index, lengths)

    cut = requests // 2
    slots = [list(range(cut)), list(range(cut, requests))]
    owned = functools.partial(items, place, owners, kv_cache, visitors=requests)

    def up(array):
        return lax.ppermute(array, "cache", forward)

    def down(array):
        return lax.ppermute(array, "cache", backward)

    def after(array, *others):
        return lax.optimization_barrier((array, others))[0]

    blocks = [payload(lists, visits[:cut])]
    blocks.append(payload(lists, visits[cut:], [touch(kv_cache, blocks[0])]))
    below, above = [up(block) for block in blocks], [down(block) for block in blocks]
    size = cut // 2 * PAIR
    both = owned(blocks, slots)
    parts = {(0, 0): (both, 0), (1, 0): (both, size)}
    new_out, new_level = new_tokens(place, owners, [after(rows[0], both), *rows[1:]], new_kv)
    done = [[both], [both, new_level]]
    for step in range(1, reach):
        for half in range(2):
            if step > 1:
                below[half], above[half] = up(below[half]), down(above[half])
            below[half], above[half] = after(below[half], *done[half]), after(above[half], *done[half])
            both = owned([below[half], above[half]], [slots[half]] * 2)
            parts[half, -step], parts[half, step] = (both, 0), (both, size)
            done[half] = [both]
    far = owned([up(below[0])], slots[:1]), owned([down(above[1])], slots[1:])

    def straight(array, ring, d):
        pairs = [(g * owners + a, (g ^ d) * owners + b) for g in range(groups) for a, b in ring]
        return lax.ppermute(array, ("grp", "cache"), pairs)

    home = [None] * requests
    for half in range(2):
        move, ring, sign = ((up, forward, 1), (down, backward, -1))[half]
        chain = far[half]
        for step in range(reach - 1, 1, -1):
            chain = merge(move(chain), parts[half, sign * step])
        long = split([(move(chain), 0), parts[half, sign]], cut)
        move, sign = ((down, -1), (up, 1))[half]
        own, first = parts[half, sign * (reach - 1)]
        chain = move(own[first : first + size])
        for step in range(reach - 2, 0, -1):
            chain = move(merge(chain, parts[half, sign * step]))
        short = split([parts[half, 0], (chain, 0)], cut)
        for number, d in enumerate(slots[half]):
            home[d] = [swap(short[number], d), straight(long[number], ring, d)]
    early = final(place, owners, sum(home[cut:], []), cut, new_out, new_level)
    return final(place, owners, sum(home[:cut], []), 0, new_out, new_level, [early])


def solution(mesh):
    in_specs = (
        P(("grp", "cache"), None, None),
        P(("grp", "cache"), None, None),
        P(("grp", "cache"), None, None),
        P(("grp", "cache"), None),
        P(("grp", "cache"), None, None),
        P(("grp", "cache")),
    )
    out_specs = P(("grp", "cache"), None, None)
    return jax.shard_map(
        per_device, mesh=mesh, in_specs=in_specs, out_specs=out_specs, check_vma=False
    )
```

```python
import functools
import math

import jax
import jax.numpy as jnp
from jax import lax
from jax.experimental import pallas as pl
from jax.experimental.pallas import tpu as pltpu
from jax.sharding import PartitionSpec as P

KVH = 8
HD = 128
GQ = 8
STEPS = 4
PAGE = 128
SEL = 4

LANES = 128
ROWS = GQ * STEPS
HALF = 16
BODY = KVH * ROWS
COLS = BODY // HALF
SECOND = 3 * COLS
PAIR = 2 * BODY + HALF
LONE = BODY + HALF
EMPTY = -1e30
SCALE = math.log2(math.e) / math.sqrt(HD)
VMEM_BYTES = 24 * 1024 * 1024
BF16 = jnp.bfloat16
F32 = jnp.float32
IN_VMEM = pl.BlockSpec(memory_space=pltpu.VMEM)
IN_SMEM = pl.BlockSpec(memory_space=pltpu.SMEM)


def params():
    return pltpu.CompilerParams(vmem_limit_bytes=VMEM_BYTES)


def cost(flops, moved):
    return pl.CostEstimate(flops=flops, bytes_accessed=moved, transcendentals=0)


def list_rows(requests):
    return -(-2 * requests // HALF) * HALF


def lane_ids(rows=HALF):
    return lax.broadcasted_iota(jnp.int32, (rows, LANES), 1)


def pack_stats(stats):
    lanes = lane_ids()
    used = (lanes < COLS) | ((lanes >= SECOND) & (lanes < SECOND + COLS))
    stats = jnp.where(used, stats, 0.0)
    high = stats.astype(BF16).astype(F32)
    rest = stats - high
    middle = rest.astype(BF16).astype(F32)
    low = rest - middle
    return (high + pltpu.roll(middle, COLS, 1) + pltpu.roll(low, 2 * COLS, 1)).astype(BF16)


def unpack_stats(tile):
    tile = tile.astype(F32)
    return tile + pltpu.roll(tile, LANES - COLS, 1) + pltpu.roll(tile, LANES - 2 * COLS, 1)


def tile_start(index):
    half, head = divmod(index, KVH)
    return head * ROWS + half * HALF


def by_lane(columns, first=0):
    lanes = lane_ids() - first
    tile = jnp.zeros((HALF, LANES), F32)
    for head, values in enumerate(columns):
        for half in range(ROWS // HALF):
            part = values[half * HALF : (half + 1) * HALF, :]
            tile = jnp.where(lanes == half * KVH + head, part, tile)
    return tile


def attend(requests):
    across = (((1,), (1,)), ((), ()))
    along = (((1,), (0,)), ((), ()))
    heads = [(q, k, v, r[3]) for r in requests for q, k, v in zip(*r[:3])]
    scores = [lax.dot_general(q, k, across, preferred_element_type=F32) for q, k, _, _ in heads]
    scores = [jnp.where(head[3], s * SCALE, EMPTY) for s, head in zip(scores, heads)]
    tops = [jnp.max(s, axis=1, keepdims=True) for s in scores]
    weights = [jnp.exp2(s - t).astype(BF16) for s, t in zip(scores, tops)]
    mixed = [lax.dot_general(w, head[2], along, preferred_element_type=F32) for w, head in zip(weights, heads)]
    ones = jnp.ones((weights[0].shape[1], LANES), BF16)
    total = lax.dot_general(jnp.concatenate(weights, axis=0), ones, along, preferred_element_type=F32)
    totals = [total[number * ROWS : (number + 1) * ROWS, :] for number in range(len(heads))]
    results = []
    for number, request in enumerate(requests):
        mine = slice(number * KVH, (number + 1) * KVH)
        first = request[4]
        level = by_lane(tops[mine], first) + jnp.log2(jnp.maximum(by_lane(totals[mine], first), 1.0))
        results.append(([m / t for m, t in zip(mixed[mine], totals[mine])], level))
    return results


def relayout_kernel(owners, place_ref, queries_ref, *outs):
    group = lax.div(place_ref[0], owners)
    for d, out in enumerate(outs):
        values = queries_ref[group ^ d].astype(F32)
        for head in range(KVH):
            first = head * GQ
            parts = [values[:, (first + g) * HD : (first + g + 1) * HD] for g in range(GQ)]
            out[head * ROWS : (head + 1) * ROWS, :] = jnp.concatenate(parts, axis=0).astype(BF16)


def relayout(place, owners, queries):
    groups = queries.shape[0]
    return pl.pallas_call(
        functools.partial(relayout_kernel, owners),
        out_shape=[jax.ShapeDtypeStruct((BODY, HD), BF16)] * groups,
        in_specs=[IN_SMEM, IN_VMEM],
        out_specs=[IN_VMEM] * groups,
        compiler_params=params(),
        cost_estimate=cost(0, 4 * queries.size),
    )(place, queries)


def new_kernel(owners, place_ref, *refs):
    group = lax.div(place_ref[0], owners)
    queries, (new_ref, out_ref, level_ref) = refs[:-3], refs[-3:]
    step = lax.broadcasted_iota(jnp.int32, (ROWS, STEPS), 0) % STEPS
    usable = lax.broadcasted_iota(jnp.int32, (ROWS, STEPS), 1) <= step
    for pair in range(0, len(queries), 2):
        requests = []
        for d in (pair, pair + 1):
            new = new_ref[group ^ d]
            heads = [new[:, head * HD : (head + 1) * HD] for head in range(2 * KVH)]
            rows = [queries[d][head * ROWS : (head + 1) * ROWS, :] for head in range(KVH)]
            requests.append((rows, heads[:KVH], heads[KVH:], usable, 0))
        for d, (mixed, level) in zip((pair, pair + 1), attend(requests)):
            for head, values in enumerate(mixed):
                out_ref[d, head * ROWS : (head + 1) * ROWS, :] = values
            level_ref[d] = level


def new_tokens(place, owners, queries, new_kv):
    groups = len(queries)
    return pl.pallas_call(
        functools.partial(new_kernel, owners),
        out_shape=[
            jax.ShapeDtypeStruct((groups, BODY, HD), F32),
            jax.ShapeDtypeStruct((groups, HALF, LANES), F32),
        ],
        in_specs=[IN_SMEM] + [IN_VMEM] * (groups + 1),
        out_specs=[IN_VMEM, IN_VMEM],
        compiler_params=params(),
        cost_estimate=cost(groups * KVH * 4 * ROWS * HD * HD, groups * BODY * HD * 6),
    )(place, *queries, new_kv)


def page_lists(page_owner, page_index, lengths):
    shape = page_owner.shape + (LANES,)
    named = page_owner[:, :, None] == lax.broadcasted_iota(jnp.int32, shape, 2)
    counts = jnp.clip(lengths[:, None, None] - lax.broadcasted_iota(jnp.int32, shape, 1) * PAGE, 0, PAGE)
    return (
        jnp.sum(jnp.where(named, counts, 0), axis=1),
        jnp.sum(jnp.where(named, page_index, 0), axis=1),
    )


def payload_kernel(after, counts_ref, pages_ref, *refs):
    visits, out = refs[: len(refs) - 1 - after], refs[-1]
    for number, visit in enumerate(visits):
        out[number * BODY : (number + 1) * BODY, :] = visit[...]
    tables = [counts_ref[...].astype(F32), pages_ref[...].astype(F32)]
    short = out.shape[0] - len(visits) * BODY - 2 * tables[0].shape[0]
    if short:
        tables.append(jnp.zeros((short, LANES), F32))
    out[len(visits) * BODY :, :] = jnp.concatenate(tables, axis=0).astype(BF16)


def payload(lists, visits, after=()):
    rows = len(visits) * BODY + list_rows(lists[0].shape[0])
    return pl.pallas_call(
        functools.partial(payload_kernel, len(after)),
        out_shape=jax.ShapeDtypeStruct((rows, HD), BF16),
        in_specs=[IN_VMEM] * (2 + len(visits) + len(after)),
        out_specs=IN_VMEM,
        compiler_params=params(),
        cost_estimate=cost(0, 4 * rows * HD),
    )(*lists, *visits, *after)


def touch_kernel(after_ref, cache_ref, out_ref):
    out_ref[...] = cache_ref[0, :HALF, :HD]


def touch(kv_cache, after):
    return pl.pallas_call(
        touch_kernel,
        out_shape=jax.ShapeDtypeStruct((HALF, HD), BF16),
        in_specs=[IN_VMEM, IN_VMEM],
        out_specs=IN_VMEM,
        compiler_params=params(),
        cost_estimate=cost(0, 2 * HALF * HD),
    )(after, kv_cache)


def item_kernel(slots, visitors, owners, place_ref, cache_ref, *refs):
    sides, each = len(slots), len(slots[0])
    entries = sides * each
    query_refs, (out_ref, rows_ref, level_ref, code_ref, order_ref) = refs[:sides], refs[sides:]
    group, owner = lax.div(place_ref[0], owners), lax.rem(place_ref[0], owners)
    lists = list_rows(visitors)
    rows = lax.broadcasted_iota(jnp.int32, (lists, LANES), 0)
    lanes = lane_ids()
    codes = []
    for side, query_ref in enumerate(query_refs):
        table = query_ref[each * BODY :, :].astype(F32)
        table = jnp.where(lane_ids(lists) == owner, table, 0.0)
        for pair in range(each // 2):
            factor = jnp.zeros((lists, LANES), F32)
            for second in range(2):
                row = group ^ slots[side][2 * pair + second]
                factor = jnp.where(rows == row, float(4096**second), factor)
                factor = jnp.where(rows == row + visitors, float(256 * 4096**second), factor)
            codes.append(jnp.sum(table * factor).astype(jnp.int32))
        rows_ref[side * each * BODY : (side + 1) * each * BODY, :] = query_ref[: each * BODY, :]

    for entry in range(entries):
        out = entry // 2 * PAIR + entry % 2 * BODY
        out_ref[out : out + BODY, :] = jnp.zeros((BODY, HD), BF16)
        first = entry % 2 * SECOND
        level_ref[entry] = jnp.where((lanes >= first) & (lanes < first + COLS), EMPTY, 0.0)
    found = jnp.int32(0)
    for entry in range(entries):
        code = (codes[entry // 2] >> (12 * (entry % 2))) & 4095
        code_ref[entry] = code
        order_ref[found] = entry
        found = found + jnp.where((code & 255) > 0, 1, 0)
    tokens = lax.broadcasted_iota(jnp.int32, (ROWS, PAGE), 1)

    def work(numbers):
        requests, places = [], []
        for number in numbers:
            entry = order_ref[number]
            code = code_ref[entry]
            page, odd = code >> 8, entry & 1
            start = entry * BODY
            queries = [rows_ref[pl.ds(pl.multiple_of(start + h * ROWS, HALF), ROWS), :] for h in range(KVH)]
            keys = [cache_ref[page, :, h * HD : (h + 1) * HD] for h in range(KVH)]
            values = [cache_ref[page, :, (KVH + h) * HD : (KVH + h + 1) * HD] for h in range(KVH)]
            requests.append((queries, keys, values, tokens < (code & 255), odd * SECOND))
            places.append((entry, (entry >> 1) * PAIR + odd * BODY))
        for (mixed, level), (entry, out) in zip(attend(requests), places):
            for head, part in enumerate(mixed):
                out_ref[pl.ds(pl.multiple_of(out + head * ROWS, HALF), ROWS), :] = part.astype(BF16)
            level_ref[entry] = level

    @pl.loop(0, found >> 1)
    def _(two):
        work([2 * two, 2 * two + 1])

    @pl.when((found & 1) == 1)
    def _():
        work([found - 1])

    for pair in range(entries // 2):
        start = pair * PAIR + 2 * BODY
        out_ref[start : start + HALF, :] = pack_stats(level_ref[2 * pair] + level_ref[2 * pair + 1])


def items(place, owners, kv_cache, payloads, slots, visitors):
    count = sum(len(row) for row in slots)
    return pl.pallas_call(
        functools.partial(item_kernel, slots, visitors, owners),
        out_shape=jax.ShapeDtypeStruct((count // 2 * PAIR, HD), BF16),
        in_specs=[IN_SMEM] + [IN_VMEM] * (1 + len(slots)),
        out_specs=IN_VMEM,
        scratch_shapes=[
            pltpu.VMEM((count * BODY, HD), BF16),
            pltpu.VMEM((count, HALF, LANES), F32),
            pltpu.SMEM((count,), jnp.int32),
            pltpu.SMEM((count + 1,), jnp.int32),
        ],
        compiler_params=params(),
        cost_estimate=cost(count * KVH * 4 * ROWS * HD * PAGE, count * PAGE * kv_cache.shape[2] * 2),
    )(place, kv_cache, *payloads)


def blend(levels):
    peak = functools.reduce(jnp.maximum, levels)
    shares = [jnp.exp2(level - peak) for level in levels]
    total = functools.reduce(jnp.add, shares)
    return [share / total for share in shares], peak + jnp.log2(total)


def mix(shares, refs, start, first_lane):
    values = []
    for index in range(COLS):
        row, lane = start + tile_start(index), first_lane + index
        tiles = [ref[row : row + HALF, :].astype(F32) for ref in refs]
        total = tiles[0]
        for share, tile in zip(shares[1:], tiles[1:]):
            total = total + share[:, lane : lane + 1] * (tile - tiles[0])
        values.append(total)
    return values


def merge_kernel(first, arrived_ref, own_ref, out_ref):
    for pair in range(out_ref.shape[0] // PAIR):
        part = slice(pair * PAIR, (pair + 1) * PAIR)
        arrived, own, out = arrived_ref.at[part], own_ref.at[first + pair * PAIR : first + (pair + 1) * PAIR], out_ref.at[part]
        shares, level = blend([unpack_stats(ref[2 * BODY : PAIR, :]) for ref in (arrived, own)])
        values = [mix(shares, (arrived, own), second * BODY, second * SECOND) for second in range(2)]
        for second in range(2):
            for index in range(COLS):
                row = second * BODY + tile_start(index)
                out[row : row + HALF, :] = values[second][index].astype(BF16)
        out[2 * BODY : PAIR, :] = pack_stats(level)


def merge(arrived, own):
    own, first = own
    return pl.pallas_call(
        functools.partial(merge_kernel, first),
        out_shape=jax.ShapeDtypeStruct(arrived.shape, BF16),
        in_specs=[IN_VMEM, IN_VMEM],
        out_specs=IN_VMEM,
        compiler_params=params(),
        cost_estimate=cost(0, 6 * arrived.size),
    )(arrived, own)


def split_kernel(firsts, *refs):
    arrays, outs = refs[: len(firsts)], refs[len(firsts) :]
    for pair in range(len(outs) // 2):
        start = pair * PAIR
        sources = [ref.at[first + start : first + start + PAIR] for ref, first in zip(arrays, firsts)]
        shares, level = blend([unpack_stats(ref[2 * BODY : PAIR, :]) for ref in sources])
        values = [mix(shares, sources, second * BODY, second * SECOND) for second in range(2)]
        for second in range(2):
            out = outs[2 * pair + second]
            for index in range(COLS):
                row = tile_start(index)
                out[row : row + HALF, :] = values[second][index].astype(BF16)
            here = pltpu.roll(level, LANES - SECOND, 1) if second else level
            out[BODY:LONE, :] = pack_stats(here)


def split(sources, requests):
    return pl.pallas_call(
        functools.partial(split_kernel, [first for _, first in sources]),
        out_shape=[jax.ShapeDtypeStruct((LONE, HD), BF16)] * requests,
        in_specs=[IN_VMEM] * len(sources),
        out_specs=[IN_VMEM] * requests,
        compiler_params=params(),
        cost_estimate=cost(0, 6 * requests * LONE * HD),
    )(*[array for array, _ in sources])


def final_kernel(first, early, owners, place_ref, *refs):
    earlier, parts = refs[:early], refs[early:-4]
    new_ref, level_ref, out_ref, rows_ref = refs[-4:]
    group = lax.div(place_ref[0], owners)
    count = len(parts) // 2
    for number in range(count):
        d = first + number
        both = (parts[2 * number], parts[2 * number + 1])
        shares, _ = blend([unpack_stats(part[BODY:LONE, :]) for part in both] + [level_ref[d]])
        for index, tile in enumerate(mix(shares, both + (new_ref.at[d],), 0, 0)):
            row = tile_start(index)
            rows_ref[number, row : row + HALF, :] = tile
    for number in range(count):
        row = group ^ (first + number) if early else number
        for head in range(KVH * GQ):
            tile = rows_ref[number, head * STEPS : (head + 1) * STEPS, :]
            out_ref[row, :, head * HD : (head + 1) * HD] = tile.astype(BF16)
    for ref in earlier:
        for number in range(ref.shape[0]):
            out_ref[group ^ (count + number)] = ref[number]


def final(place, owners, parts, first, new_out, new_level, earlier=()):
    count = len(parts) // 2
    requests = count + sum(e.shape[0] for e in earlier)
    return pl.pallas_call(
        functools.partial(final_kernel, first, len(earlier), owners),
        out_shape=jax.ShapeDtypeStruct((requests, STEPS, KVH * GQ * HD), BF16),
        in_specs=[IN_SMEM] + [IN_VMEM] * (len(earlier) + len(parts) + 2),
        out_specs=IN_VMEM,
        scratch_shapes=[pltpu.VMEM((count, BODY, HD), F32)],
        compiler_params=params(),
        cost_estimate=cost(0, count * BODY * HD * 10),
    )(place, *earlier, *parts, new_out, new_level)


def ring_order(owners):
    return list(range(0, owners, 2)) + list(range(owners - 1, 0, -2))


def per_device(queries, new_kv, kv_cache, page_owner, page_index, lengths):
    groups = lax.axis_size("grp")
    owners = lax.axis_size("cache")
    requests = queries.shape[0]
    assert requests == groups and requests % 4 == 0 and owners <= LANES
    reach = owners // 2
    order = ring_order(owners)
    forward = [(order[i], order[(i + 1) % owners]) for i in range(owners)]
    backward = [(b, a) for a, b in forward]
    place = jnp.reshape(lax.axis_index(("grp", "cache")), (1,)).astype(jnp.int32)

    def swap(array, d):
        return lax.ppermute(array, "grp", [(g, g ^ d) for g in range(groups)]) if d else array

    rows = relayout(place, owners, queries)
    visits = [rows[0]] + [None] * (groups - 1)
    for d in range(groups - 1, 0, -1):
        visits[d] = swap(rows[d], d)
    lists = page_lists(page_owner, page_index, lengths)

    cut = requests // 2
    slots = [list(range(cut)), list(range(cut, requests))]
    owned = functools.partial(items, place, owners, kv_cache, visitors=requests)

    def up(array):
        return lax.ppermute(array, "cache", forward)

    def down(array):
        return lax.ppermute(array, "cache", backward)

    def after(array, *others):
        return lax.optimization_barrier((array, others))[0]

    blocks = [payload(lists, visits[:cut])]
    blocks.append(payload(lists, visits[cut:], [touch(kv_cache, blocks[0])]))
    below, above = [up(block) for block in blocks], [down(block) for block in blocks]
    size = cut // 2 * PAIR
    both = owned(blocks, slots)
    parts = {(0, 0): (both, 0), (1, 0): (both, size)}
    new_out, new_level = new_tokens(place, owners, [after(rows[0], both), *rows[1:]], new_kv)
    done = [[both], [both, new_level]]
    for step in range(1, reach):
        for half in range(2):
            if step > 1:
                below[half], above[half] = up(below[half]), down(above[half])
            below[half], above[half] = after(below[half], *done[half]), after(above[half], *done[half])
            both = owned([below[half], above[half]], [slots[half]] * 2)
            parts[half, -step], parts[half, step] = (both, 0), (both, size)
            done[half] = [both]
    far = owned([up(below[0])], slots[:1]), owned([down(above[1])], slots[1:])

    def straight(array, ring, d):
        pairs = [(g * owners + a, (g ^ d) * owners + b) for g in range(groups) for a, b in ring]
        return lax.ppermute(array, ("grp", "cache"), pairs)

    home = [None] * requests
    for half in range(2):
        move, ring, sign = ((up, forward, 1), (down, backward, -1))[half]
        chain = far[half]
        for step in range(reach - 1, 1, -1):
            chain = merge(move(chain), parts[half, sign * step])
        long = split([(move(chain), 0), parts[half, sign]], cut)
        move, sign = ((down, -1), (up, 1))[half]
        own, first = parts[half, sign * (reach - 1)]
        chain = move(own[first : first + size])
        for step in range(reach - 2, 0, -1):
            chain = move(merge(chain, parts[half, sign * step]))
        short = split([parts[half, 0], (chain, 0)], cut)
        for number, d in enumerate(slots[half]):
            home[d] = [swap(short[number], d), straight(long[number], ring, d)]
    early = final(place, owners, sum(home[cut:], []), cut, new_out, new_level)
    return final(place, owners, sum(home[:cut], []), 0, new_out, new_level, [early])


def solution(mesh):
    in_specs = (
        P(("grp", "cache"), None, None),
        P(("grp", "cache"), None, None),
        P(("grp", "cache"), None, None),
        P(("grp", "cache"), None),
        P(("grp", "cache"), None, None),
        P(("grp", "cache")),
    )
    out_specs = P(("grp", "cache"), None, None)
    return jax.shard_map(
        per_device, mesh=mesh, in_specs=in_specs, out_specs=out_specs, check_vma=False
    )
```

```python
import functools
import math

import jax
import jax.numpy as jnp
from jax import lax
from jax.experimental import pallas as pl
from jax.experimental.pallas import tpu as pltpu
from jax.sharding import PartitionSpec as P

KVH = 8
HD = 128
GQ = 8
STEPS = 4
PAGE = 128
SEL = 4

LANES = 128
ROWS = GQ * STEPS
HALF = 16
BODY = KVH * ROWS
COLS = BODY // HALF
SECOND = 3 * COLS
PAIR = 2 * BODY + HALF
LONE = BODY + HALF
EMPTY = -1e30
SCALE = math.log2(math.e) / math.sqrt(HD)
VMEM_BYTES = 24 * 1024 * 1024
BF16 = jnp.bfloat16
F32 = jnp.float32
IN_VMEM = pl.BlockSpec(memory_space=pltpu.VMEM)
IN_SMEM = pl.BlockSpec(memory_space=pltpu.SMEM)


def params():
    return pltpu.CompilerParams(vmem_limit_bytes=VMEM_BYTES)


def cost(flops, moved):
    return pl.CostEstimate(flops=flops, bytes_accessed=moved, transcendentals=0)


def list_rows(requests):
    return -(-2 * requests // HALF) * HALF


def lane_ids(rows=HALF):
    return lax.broadcasted_iota(jnp.int32, (rows, LANES), 1)


def pack_stats(stats):
    lanes = lane_ids()
    used = (lanes < COLS) | ((lanes >= SECOND) & (lanes < SECOND + COLS))
    stats = jnp.where(used, stats, 0.0)
    high = stats.astype(BF16).astype(F32)
    rest = stats - high
    middle = rest.astype(BF16).astype(F32)
    low = rest - middle
    return (high + pltpu.roll(middle, COLS, 1) + pltpu.roll(low, 2 * COLS, 1)).astype(BF16)


def unpack_stats(tile):
    tile = tile.astype(F32)
    return tile + pltpu.roll(tile, LANES - COLS, 1) + pltpu.roll(tile, LANES - 2 * COLS, 1)


def tile_start(index):
    half, head = divmod(index, KVH)
    return head * ROWS + half * HALF


def by_lane(columns, first=0):
    lanes = lane_ids() - first
    tile = jnp.zeros((HALF, LANES), F32)
    for head, values in enumerate(columns):
        for half in range(ROWS // HALF):
            part = values[half * HALF : (half + 1) * HALF, :]
            tile = jnp.where(lanes == half * KVH + head, part, tile)
    return tile


def attend(requests):
    across = (((1,), (1,)), ((), ()))
    along = (((1,), (0,)), ((), ()))
    heads = [(q, k, v, r[3]) for r in requests for q, k, v in zip(*r[:3])]
    scores = [lax.dot_general(q, k, across, preferred_element_type=F32) for q, k, _, _ in heads]
    scores = [jnp.where(head[3], s * SCALE, EMPTY) for s, head in zip(scores, heads)]
    tops = [jnp.max(s, axis=1, keepdims=True) for s in scores]
    weights = [jnp.exp2(s - t).astype(BF16) for s, t in zip(scores, tops)]
    mixed = [lax.dot_general(w, head[2], along, preferred_element_type=F32) for w, head in zip(weights, heads)]
    ones = jnp.ones((weights[0].shape[1], LANES), BF16)
    total = lax.dot_general(jnp.concatenate(weights, axis=0), ones, along, preferred_element_type=F32)
    totals = [total[number * ROWS : (number + 1) * ROWS, :] for number in range(len(heads))]
    results = []
    for number, request in enumerate(requests):
        mine = slice(number * KVH, (number + 1) * KVH)
        first = request[4]
        level = by_lane(tops[mine], first) + jnp.log2(jnp.maximum(by_lane(totals[mine], first), 1.0))
        results.append(([m / t for m, t in zip(mixed[mine], totals[mine])], level))
    return results


def relayout_kernel(owners, place_ref, queries_ref, *outs):
    group = lax.div(place_ref[0], owners)
    for d, out in enumerate(outs):
        values = queries_ref[group ^ d].astype(F32)
        for head in range(KVH):
            first = head * GQ
            parts = [values[:, (first + g) * HD : (first + g + 1) * HD] for g in range(GQ)]
            out[head * ROWS : (head + 1) * ROWS, :] = jnp.concatenate(parts, axis=0).astype(BF16)


def relayout(place, owners, queries):
    groups = queries.shape[0]
    return pl.pallas_call(
        functools.partial(relayout_kernel, owners),
        out_shape=[jax.ShapeDtypeStruct((BODY, HD), BF16)] * groups,
        in_specs=[IN_SMEM, IN_VMEM],
        out_specs=[IN_VMEM] * groups,
        compiler_params=params(),
        cost_estimate=cost(0, 4 * queries.size),
    )(place, queries)


def new_kernel(owners, place_ref, *refs):
    group = lax.div(place_ref[0], owners)
    queries, (new_ref, out_ref, level_ref) = refs[:-3], refs[-3:]
    step = lax.broadcasted_iota(jnp.int32, (ROWS, STEPS), 0) % STEPS
    usable = lax.broadcasted_iota(jnp.int32, (ROWS, STEPS), 1) <= step
    for pair in range(0, len(queries), 2):
        requests = []
        for d in (pair, pair + 1):
            new = new_ref[group ^ d]
            heads = [new[:, head * HD : (head + 1) * HD] for head in range(2 * KVH)]
            rows = [queries[d][head * ROWS : (head + 1) * ROWS, :] for head in range(KVH)]
            requests.append((rows, heads[:KVH], heads[KVH:], usable, 0))
        for d, (mixed, level) in zip((pair, pair + 1), attend(requests)):
            for head, values in enumerate(mixed):
                out_ref[d, head * ROWS : (head + 1) * ROWS, :] = values
            level_ref[d] = level


def new_tokens(place, owners, queries, new_kv):
    groups = len(queries)
    return pl.pallas_call(
        functools.partial(new_kernel, owners),
        out_shape=[
            jax.ShapeDtypeStruct((groups, BODY, HD), F32),
            jax.ShapeDtypeStruct((groups, HALF, LANES), F32),
        ],
        in_specs=[IN_SMEM] + [IN_VMEM] * (groups + 1),
        out_specs=[IN_VMEM, IN_VMEM],
        compiler_params=params(),
        cost_estimate=cost(groups * KVH * 4 * ROWS * HD * HD, groups * BODY * HD * 6),
    )(place, *queries, new_kv)


def page_lists(page_owner, page_index, lengths):
    shape = page_owner.shape + (LANES,)
    named = page_owner[:, :, None] == lax.broadcasted_iota(jnp.int32, shape, 2)
    counts = jnp.clip(lengths[:, None, None] - lax.broadcasted_iota(jnp.int32, shape, 1) * PAGE, 0, PAGE)
    return (
        jnp.sum(jnp.where(named, counts, 0), axis=1),
        jnp.sum(jnp.where(named, page_index, 0), axis=1),
    )


def payload_kernel(after, counts_ref, pages_ref, *refs):
    visits, out = refs[: len(refs) - 1 - after], refs[-1]
    for number, visit in enumerate(visits):
        out[number * BODY : (number + 1) * BODY, :] = visit[...]
    tables = [counts_ref[...].astype(F32), pages_ref[...].astype(F32)]
    short = out.shape[0] - len(visits) * BODY - 2 * tables[0].shape[0]
    if short:
        tables.append(jnp.zeros((short, LANES), F32))
    out[len(visits) * BODY :, :] = jnp.concatenate(tables, axis=0).astype(BF16)


def payload(lists, visits, after=()):
    rows = len(visits) * BODY + list_rows(lists[0].shape[0])
    return pl.pallas_call(
        functools.partial(payload_kernel, len(after)),
        out_shape=jax.ShapeDtypeStruct((rows, HD), BF16),
        in_specs=[IN_VMEM] * (2 + len(visits) + len(after)),
        out_specs=IN_VMEM,
        compiler_params=params(),
        cost_estimate=cost(0, 4 * rows * HD),
    )(*lists, *visits, *after)


def touch_kernel(after_ref, cache_ref, out_ref):
    out_ref[...] = cache_ref[0, :HALF, :HD]


def touch(kv_cache, after):
    return pl.pallas_call(
        touch_kernel,
        out_shape=jax.ShapeDtypeStruct((HALF, HD), BF16),
        in_specs=[IN_VMEM, IN_VMEM],
        out_specs=IN_VMEM,
        compiler_params=params(),
        cost_estimate=cost(0, 2 * HALF * HD),
    )(after, kv_cache)


def item_kernel(slots, visitors, owners, place_ref, cache_ref, *refs):
    sides, each = len(slots), len(slots[0])
    entries = sides * each
    query_refs, (out_ref, rows_ref, level_ref, code_ref, order_ref) = refs[:sides], refs[sides:]
    group, owner = lax.div(place_ref[0], owners), lax.rem(place_ref[0], owners)
    lists = list_rows(visitors)
    rows = lax.broadcasted_iota(jnp.int32, (lists, LANES), 0)
    lanes = lane_ids()
    codes = []
    for side, query_ref in enumerate(query_refs):
        table = query_ref[each * BODY :, :].astype(F32)
        table = jnp.where(lane_ids(lists) == owner, table, 0.0)
        for pair in range(each // 2):
            factor = jnp.zeros((lists, LANES), F32)
            for second in range(2):
                row = group ^ slots[side][2 * pair + second]
                factor = jnp.where(rows == row, float(4096**second), factor)
                factor = jnp.where(rows == row + visitors, float(256 * 4096**second), factor)
            codes.append(jnp.sum(table * factor).astype(jnp.int32))
        rows_ref[side * each * BODY : (side + 1) * each * BODY, :] = query_ref[: each * BODY, :]

    for entry in range(entries):
        out = entry // 2 * PAIR + entry % 2 * BODY
        out_ref[out : out + BODY, :] = jnp.zeros((BODY, HD), BF16)
        first = entry % 2 * SECOND
        level_ref[entry] = jnp.where((lanes >= first) & (lanes < first + COLS), EMPTY, 0.0)
    found = jnp.int32(0)
    for entry in range(entries):
        code = (codes[entry // 2] >> (12 * (entry % 2))) & 4095
        code_ref[entry] = code
        order_ref[found] = entry
        found = found + jnp.where((code & 255) > 0, 1, 0)
    tokens = lax.broadcasted_iota(jnp.int32, (ROWS, PAGE), 1)

    def work(numbers):
        requests, places = [], []
        for number in numbers:
            entry = order_ref[number]
            code = code_ref[entry]
            page, odd = code >> 8, entry & 1
            start = entry * BODY
            queries = [rows_ref[pl.ds(pl.multiple_of(start + h * ROWS, HALF), ROWS), :] for h in range(KVH)]
            keys = [cache_ref[page, :, h * HD : (h + 1) * HD] for h in range(KVH)]
            values = [cache_ref[page, :, (KVH + h) * HD : (KVH + h + 1) * HD] for h in range(KVH)]
            requests.append((queries, keys, values, tokens < (code & 255), odd * SECOND))
            places.append((entry, (entry >> 1) * PAIR + odd * BODY))
        for (mixed, level), (entry, out) in zip(attend(requests), places):
            for head, part in enumerate(mixed):
                out_ref[pl.ds(pl.multiple_of(out + head * ROWS, HALF), ROWS), :] = part.astype(BF16)
            level_ref[entry] = level

    three = ((found & 1) == 1) & (found > 1)

    @pl.loop(0, (found - jnp.where(three, 3, 0)) >> 1)
    def _(two):
        work([2 * two, 2 * two + 1])

    @pl.when(three)
    def _():
        work([found - 3, found - 2, found - 1])

    @pl.when(found == 1)
    def _():
        work([found - 1])

    for pair in range(entries // 2):
        start = pair * PAIR + 2 * BODY
        out_ref[start : start + HALF, :] = pack_stats(level_ref[2 * pair] + level_ref[2 * pair + 1])


def items(place, owners, kv_cache, payloads, slots, visitors):
    count = sum(len(row) for row in slots)
    return pl.pallas_call(
        functools.partial(item_kernel, slots, visitors, owners),
        out_shape=jax.ShapeDtypeStruct((count // 2 * PAIR, HD), BF16),
        in_specs=[IN_SMEM] + [IN_VMEM] * (1 + len(slots)),
        out_specs=IN_VMEM,
        scratch_shapes=[
            pltpu.VMEM((count * BODY, HD), BF16),
            pltpu.VMEM((count, HALF, LANES), F32),
            pltpu.SMEM((count,), jnp.int32),
            pltpu.SMEM((count + 1,), jnp.int32),
        ],
        compiler_params=params(),
        cost_estimate=cost(count * KVH * 4 * ROWS * HD * PAGE, count * PAGE * kv_cache.shape[2] * 2),
    )(place, kv_cache, *payloads)


def blend(levels):
    peak = functools.reduce(jnp.maximum, levels)
    shares = [jnp.exp2(level - peak) for level in levels]
    total = functools.reduce(jnp.add, shares)
    return [share / total for share in shares], peak + jnp.log2(total)


def mix(shares, refs, start, first_lane):
    values = []
    for index in range(COLS):
        row, lane = start + tile_start(index), first_lane + index
        tiles = [ref[row : row + HALF, :].astype(F32) for ref in refs]
        total = tiles[0]
        for share, tile in zip(shares[1:], tiles[1:]):
            total = total + share[:, lane : lane + 1] * (tile - tiles[0])
        values.append(total)
    return values


def merge_kernel(first, arrived_ref, own_ref, out_ref):
    for pair in range(out_ref.shape[0] // PAIR):
        part = slice(pair * PAIR, (pair + 1) * PAIR)
        arrived, own, out = arrived_ref.at[part], own_ref.at[first + pair * PAIR : first + (pair + 1) * PAIR], out_ref.at[part]
        shares, level = blend([unpack_stats(ref[2 * BODY : PAIR, :]) for ref in (arrived, own)])
        values = [mix(shares, (arrived, own), second * BODY, second * SECOND) for second in range(2)]
        for second in range(2):
            for index in range(COLS):
                row = second * BODY + tile_start(index)
                out[row : row + HALF, :] = values[second][index].astype(BF16)
        out[2 * BODY : PAIR, :] = pack_stats(level)


def merge(arrived, own):
    own, first = own
    return pl.pallas_call(
        functools.partial(merge_kernel, first),
        out_shape=jax.ShapeDtypeStruct(arrived.shape, BF16),
        in_specs=[IN_VMEM, IN_VMEM],
        out_specs=IN_VMEM,
        compiler_params=params(),
        cost_estimate=cost(0, 6 * arrived.size),
    )(arrived, own)


def split_kernel(firsts, *refs):
    arrays, outs = refs[: len(firsts)], refs[len(firsts) :]
    for pair in range(len(outs) // 2):
        start = pair * PAIR
        sources = [ref.at[first + start : first + start + PAIR] for ref, first in zip(arrays, firsts)]
        shares, level = blend([unpack_stats(ref[2 * BODY : PAIR, :]) for ref in sources])
        values = [mix(shares, sources, second * BODY, second * SECOND) for second in range(2)]
        for second in range(2):
            out = outs[2 * pair + second]
            for index in range(COLS):
                row = tile_start(index)
                out[row : row + HALF, :] = values[second][index].astype(BF16)
            here = pltpu.roll(level, LANES - SECOND, 1) if second else level
            out[BODY:LONE, :] = pack_stats(here)


def split(sources, requests):
    return pl.pallas_call(
        functools.partial(split_kernel, [first for _, first in sources]),
        out_shape=[jax.ShapeDtypeStruct((LONE, HD), BF16)] * requests,
        in_specs=[IN_VMEM] * len(sources),
        out_specs=[IN_VMEM] * requests,
        compiler_params=params(),
        cost_estimate=cost(0, 6 * requests * LONE * HD),
    )(*[array for array, _ in sources])


def final_kernel(first, early, owners, place_ref, *refs):
    earlier, parts = refs[:early], refs[early:-4]
    new_ref, level_ref, out_ref, rows_ref = refs[-4:]
    group = lax.div(place_ref[0], owners)
    count = len(parts) // 2
    for number in range(count):
        d = first + number
        both = (parts[2 * number], parts[2 * number + 1])
        shares, _ = blend([unpack_stats(part[BODY:LONE, :]) for part in both] + [level_ref[d]])
        for index, tile in enumerate(mix(shares, both + (new_ref.at[d],), 0, 0)):
            row = tile_start(index)
            rows_ref[number, row : row + HALF, :] = tile
    for number in range(count):
        row = group ^ (first + number) if early else number
        for head in range(KVH * GQ):
            tile = rows_ref[number, head * STEPS : (head + 1) * STEPS, :]
            out_ref[row, :, head * HD : (head + 1) * HD] = tile.astype(BF16)
    for ref in earlier:
        for number in range(ref.shape[0]):
            out_ref[group ^ (count + number)] = ref[number]


def final(place, owners, parts, first, new_out, new_level, earlier=()):
    count = len(parts) // 2
    requests = count + sum(e.shape[0] for e in earlier)
    return pl.pallas_call(
        functools.partial(final_kernel, first, len(earlier), owners),
        out_shape=jax.ShapeDtypeStruct((requests, STEPS, KVH * GQ * HD), BF16),
        in_specs=[IN_SMEM] + [IN_VMEM] * (len(earlier) + len(parts) + 2),
        out_specs=IN_VMEM,
        scratch_shapes=[pltpu.VMEM((count, BODY, HD), F32)],
        compiler_params=params(),
        cost_estimate=cost(0, count * BODY * HD * 10),
    )(place, *earlier, *parts, new_out, new_level)


def ring_order(owners):
    return list(range(0, owners, 2)) + list(range(owners - 1, 0, -2))


def per_device(queries, new_kv, kv_cache, page_owner, page_index, lengths):
    groups = lax.axis_size("grp")
    owners = lax.axis_size("cache")
    requests = queries.shape[0]
    assert requests == groups and requests % 4 == 0 and owners <= LANES
    reach = owners // 2
    order = ring_order(owners)
    forward = [(order[i], order[(i + 1) % owners]) for i in range(owners)]
    backward = [(b, a) for a, b in forward]
    place = jnp.reshape(lax.axis_index(("grp", "cache")), (1,)).astype(jnp.int32)

    def swap(array, d):
        return lax.ppermute(array, "grp", [(g, g ^ d) for g in range(groups)]) if d else array

    rows = relayout(place, owners, queries)
    visits = [rows[0]] + [None] * (groups - 1)
    for d in range(groups - 1, 0, -1):
        visits[d] = swap(rows[d], d)
    lists = page_lists(page_owner, page_index, lengths)

    cut = requests // 2
    slots = [list(range(cut)), list(range(cut, requests))]
    owned = functools.partial(items, place, owners, kv_cache, visitors=requests)

    def up(array):
        return lax.ppermute(array, "cache", forward)

    def down(array):
        return lax.ppermute(array, "cache", backward)

    def after(array, *others):
        return lax.optimization_barrier((array, others))[0]

    blocks = [payload(lists, visits[:cut])]
    blocks.append(payload(lists, visits[cut:], [touch(kv_cache, blocks[0])]))
    below, above = [up(block) for block in blocks], [down(block) for block in blocks]
    size = cut // 2 * PAIR
    both = owned(blocks, slots)
    parts = {(0, 0): (both, 0), (1, 0): (both, size)}
    new_out, new_level = new_tokens(place, owners, [after(rows[0], both), *rows[1:]], new_kv)
    done = [[both], [both, new_level]]
    for step in range(1, reach):
        for half in range(2):
            if step > 1:
                below[half], above[half] = up(below[half]), down(above[half])
            below[half], above[half] = after(below[half], *done[half]), after(above[half], *done[half])
            both = owned([below[half], above[half]], [slots[half]] * 2)
            parts[half, -step], parts[half, step] = (both, 0), (both, size)
            done[half] = [both]
    far = owned([up(below[0])], slots[:1]), owned([down(above[1])], slots[1:])

    def straight(array, ring, d):
        pairs = [(g * owners + a, (g ^ d) * owners + b) for g in range(groups) for a, b in ring]
        return lax.ppermute(array, ("grp", "cache"), pairs)

    home = [None] * requests
    for half in range(2):
        move, ring, sign = ((up, forward, 1), (down, backward, -1))[half]
        chain = far[half]
        for step in range(reach - 1, 1, -1):
            chain = merge(move(chain), parts[half, sign * step])
        long = split([(move(chain), 0), parts[half, sign]], cut)
        move, sign = ((down, -1), (up, 1))[half]
        own, first = parts[half, sign * (reach - 1)]
        chain = move(own[first : first + size])
        for step in range(reach - 2, 0, -1):
            chain = move(merge(chain, parts[half, sign * step]))
        short = split([parts[half, 0], (chain, 0)], cut)
        for number, d in enumerate(slots[half]):
            home[d] = [swap(short[number], d), straight(long[number], ring, d)]
    early = final(place, owners, sum(home[cut:], []), cut, new_out, new_level)
    return final(place, owners, sum(home[:cut], []), 0, new_out, new_level, [early])


def solution(mesh):
    in_specs = (
        P(("grp", "cache"), None, None),
        P(("grp", "cache"), None, None),
        P(("grp", "cache"), None, None),
        P(("grp", "cache"), None),
        P(("grp", "cache"), None, None),
        P(("grp", "cache")),
    )
    out_specs = P(("grp", "cache"), None, None)
    return jax.shard_map(
        per_device, mesh=mesh, in_specs=in_specs, out_specs=out_specs, check_vma=False
    )
```

```python
import functools
import math

import jax
import jax.numpy as jnp
from jax import lax
from jax.experimental import pallas as pl
from jax.experimental.pallas import tpu as pltpu
from jax.sharding import PartitionSpec as P

KVH = 8
HD = 128
GQ = 8
STEPS = 4
PAGE = 128
SEL = 4

LANES = 128
ROWS = GQ * STEPS
HALF = 16
BODY = KVH * ROWS
COLS = BODY // HALF
SECOND = 3 * COLS
PAIR = 2 * BODY + HALF
LONE = BODY + HALF
EMPTY = -1e30
SCALE = math.log2(math.e) / math.sqrt(HD)
VMEM_BYTES = 24 * 1024 * 1024
BF16 = jnp.bfloat16
F32 = jnp.float32
IN_VMEM = pl.BlockSpec(memory_space=pltpu.VMEM)
IN_SMEM = pl.BlockSpec(memory_space=pltpu.SMEM)


def params():
    return pltpu.CompilerParams(vmem_limit_bytes=VMEM_BYTES)


def cost(flops, moved):
    return pl.CostEstimate(flops=flops, bytes_accessed=moved, transcendentals=0)


def list_rows(requests):
    return -(-2 * requests // HALF) * HALF


def lane_ids(rows=HALF):
    return lax.broadcasted_iota(jnp.int32, (rows, LANES), 1)


def pack_stats(stats):
    lanes = lane_ids()
    used = (lanes < COLS) | ((lanes >= SECOND) & (lanes < SECOND + COLS))
    stats = jnp.where(used, stats, 0.0)
    high = stats.astype(BF16).astype(F32)
    rest = stats - high
    middle = rest.astype(BF16).astype(F32)
    low = rest - middle
    return (high + pltpu.roll(middle, COLS, 1) + pltpu.roll(low, 2 * COLS, 1)).astype(BF16)


def unpack_stats(tile):
    tile = tile.astype(F32)
    return tile + pltpu.roll(tile, LANES - COLS, 1) + pltpu.roll(tile, LANES - 2 * COLS, 1)


def tile_start(index):
    half, head = divmod(index, KVH)
    return head * ROWS + half * HALF


def by_lane(columns, first=0):
    lanes = lane_ids() - first
    tile = jnp.zeros((HALF, LANES), F32)
    for head, values in enumerate(columns):
        for half in range(ROWS // HALF):
            part = values[half * HALF : (half + 1) * HALF, :]
            tile = jnp.where(lanes == half * KVH + head, part, tile)
    return tile


def attend(requests):
    across = (((1,), (1,)), ((), ()))
    along = (((1,), (0,)), ((), ()))
    heads = [(q, k, v, r[3]) for r in requests for q, k, v in zip(*r[:3])]
    scores = [lax.dot_general(q, k, across, preferred_element_type=F32) for q, k, _, _ in heads]
    scores = [jnp.where(head[3], s * SCALE, EMPTY) for s, head in zip(scores, heads)]
    tops = [jnp.max(s, axis=1, keepdims=True) for s in scores]
    weights = [jnp.exp2(s - t).astype(BF16) for s, t in zip(scores, tops)]
    mixed = [lax.dot_general(w, head[2], along, preferred_element_type=F32) for w, head in zip(weights, heads)]
    ones = jnp.ones((weights[0].shape[1], LANES), BF16)
    total = lax.dot_general(jnp.concatenate(weights, axis=0), ones, along, preferred_element_type=F32)
    totals = [total[number * ROWS : (number + 1) * ROWS, :] for number in range(len(heads))]
    results = []
    for number, request in enumerate(requests):
        mine = slice(number * KVH, (number + 1) * KVH)
        first = request[4]
        level = by_lane(tops[mine], first) + jnp.log2(jnp.maximum(by_lane(totals[mine], first), 1.0))
        results.append(([m / t for m, t in zip(mixed[mine], totals[mine])], level))
    return results


def relayout_kernel(owners, place_ref, queries_ref, *outs):
    group = lax.div(place_ref[0], owners)
    for d, out in enumerate(outs):
        values = queries_ref[group ^ d].astype(F32)
        for head in range(KVH):
            first = head * GQ
            parts = [values[:, (first + g) * HD : (first + g + 1) * HD] for g in range(GQ)]
            out[head * ROWS : (head + 1) * ROWS, :] = jnp.concatenate(parts, axis=0).astype(BF16)


def relayout(place, owners, queries):
    groups = queries.shape[0]
    return pl.pallas_call(
        functools.partial(relayout_kernel, owners),
        out_shape=[jax.ShapeDtypeStruct((BODY, HD), BF16)] * groups,
        in_specs=[IN_SMEM, IN_VMEM],
        out_specs=[IN_VMEM] * groups,
        compiler_params=params(),
        cost_estimate=cost(0, 4 * queries.size),
    )(place, queries)


def new_kernel(owners, place_ref, *refs):
    group = lax.div(place_ref[0], owners)
    queries, (new_ref, out_ref, level_ref) = refs[:-3], refs[-3:]
    step = lax.broadcasted_iota(jnp.int32, (ROWS, STEPS), 0) % STEPS
    usable = lax.broadcasted_iota(jnp.int32, (ROWS, STEPS), 1) <= step
    for four in range(0, len(queries), 4):
        requests = []
        for d in range(four, four + 4):
            new = new_ref[group ^ d]
            heads = [new[:, head * HD : (head + 1) * HD] for head in range(2 * KVH)]
            rows = [queries[d][head * ROWS : (head + 1) * ROWS, :] for head in range(KVH)]
            requests.append((rows, heads[:KVH], heads[KVH:], usable, 0))
        for d, (mixed, level) in zip(range(four, four + 4), attend(requests)):
            for head, values in enumerate(mixed):
                out_ref[d, head * ROWS : (head + 1) * ROWS, :] = values
            level_ref[d] = level


def new_tokens(place, owners, queries, new_kv):
    groups = len(queries)
    return pl.pallas_call(
        functools.partial(new_kernel, owners),
        out_shape=[
            jax.ShapeDtypeStruct((groups, BODY, HD), F32),
            jax.ShapeDtypeStruct((groups, HALF, LANES), F32),
        ],
        in_specs=[IN_SMEM] + [IN_VMEM] * (groups + 1),
        out_specs=[IN_VMEM, IN_VMEM],
        compiler_params=params(),
        cost_estimate=cost(groups * KVH * 4 * ROWS * HD * HD, groups * BODY * HD * 6),
    )(place, *queries, new_kv)


def page_lists(page_owner, page_index, lengths):
    shape = page_owner.shape + (LANES,)
    named = page_owner[:, :, None] == lax.broadcasted_iota(jnp.int32, shape, 2)
    counts = jnp.clip(lengths[:, None, None] - lax.broadcasted_iota(jnp.int32, shape, 1) * PAGE, 0, PAGE)
    return (
        jnp.sum(jnp.where(named, counts, 0), axis=1),
        jnp.sum(jnp.where(named, page_index, 0), axis=1),
    )


def payload_kernel(after, counts_ref, pages_ref, *refs):
    visits, out = refs[: len(refs) - 1 - after], refs[-1]
    for number, visit in enumerate(visits):
        out[number * BODY : (number + 1) * BODY, :] = visit[...]
    tables = [counts_ref[...].astype(F32), pages_ref[...].astype(F32)]
    short = out.shape[0] - len(visits) * BODY - 2 * tables[0].shape[0]
    if short:
        tables.append(jnp.zeros((short, LANES), F32))
    out[len(visits) * BODY :, :] = jnp.concatenate(tables, axis=0).astype(BF16)


def payload(lists, visits, after=()):
    rows = len(visits) * BODY + list_rows(lists[0].shape[0])
    return pl.pallas_call(
        functools.partial(payload_kernel, len(after)),
        out_shape=jax.ShapeDtypeStruct((rows, HD), BF16),
        in_specs=[IN_VMEM] * (2 + len(visits) + len(after)),
        out_specs=IN_VMEM,
        compiler_params=params(),
        cost_estimate=cost(0, 4 * rows * HD),
    )(*lists, *visits, *after)


def touch_kernel(after_ref, cache_ref, out_ref):
    out_ref[...] = cache_ref[0, :HALF, :HD]


def touch(kv_cache, after):
    return pl.pallas_call(
        touch_kernel,
        out_shape=jax.ShapeDtypeStruct((HALF, HD), BF16),
        in_specs=[IN_VMEM, IN_VMEM],
        out_specs=IN_VMEM,
        compiler_params=params(),
        cost_estimate=cost(0, 2 * HALF * HD),
    )(after, kv_cache)


def item_kernel(slots, visitors, owners, place_ref, cache_ref, *refs):
    sides, each = len(slots), len(slots[0])
    entries = sides * each
    query_refs, (out_ref, rows_ref, level_ref, code_ref, order_ref) = refs[:sides], refs[sides:]
    group, owner = lax.div(place_ref[0], owners), lax.rem(place_ref[0], owners)
    lists = list_rows(visitors)
    rows = lax.broadcasted_iota(jnp.int32, (lists, LANES), 0)
    lanes = lane_ids()
    codes = []
    for side, query_ref in enumerate(query_refs):
        table = query_ref[each * BODY :, :].astype(F32)
        table = jnp.where(lane_ids(lists) == owner, table, 0.0)
        for pair in range(each // 2):
            factor = jnp.zeros((lists, LANES), F32)
            for second in range(2):
                row = group ^ slots[side][2 * pair + second]
                factor = jnp.where(rows == row, float(4096**second), factor)
                factor = jnp.where(rows == row + visitors, float(256 * 4096**second), factor)
            codes.append(jnp.sum(table * factor).astype(jnp.int32))
        rows_ref[side * each * BODY : (side + 1) * each * BODY, :] = query_ref[: each * BODY, :]

    for entry in range(entries):
        out = entry // 2 * PAIR + entry % 2 * BODY
        out_ref[out : out + BODY, :] = jnp.zeros((BODY, HD), BF16)
        first = entry % 2 * SECOND
        level_ref[entry] = jnp.where((lanes >= first) & (lanes < first + COLS), EMPTY, 0.0)
    found = jnp.int32(0)
    for entry in range(entries):
        code = (codes[entry // 2] >> (12 * (entry % 2))) & 4095
        code_ref[entry] = code
        order_ref[found] = entry
        found = found + jnp.where((code & 255) > 0, 1, 0)
    tokens = lax.broadcasted_iota(jnp.int32, (ROWS, PAGE), 1)

    def work(numbers):
        requests, places = [], []
        for number in numbers:
            entry = order_ref[number]
            code = code_ref[entry]
            page, odd = code >> 8, entry & 1
            start = entry * BODY
            queries = [rows_ref[pl.ds(pl.multiple_of(start + h * ROWS, HALF), ROWS), :] for h in range(KVH)]
            keys = [cache_ref[page, :, h * HD : (h + 1) * HD] for h in range(KVH)]
            values = [cache_ref[page, :, (KVH + h) * HD : (KVH + h + 1) * HD] for h in range(KVH)]
            requests.append((queries, keys, values, tokens < (code & 255), odd * SECOND))
            places.append((entry, (entry >> 1) * PAIR + odd * BODY))
        for (mixed, level), (entry, out) in zip(attend(requests), places):
            for head, part in enumerate(mixed):
                out_ref[pl.ds(pl.multiple_of(out + head * ROWS, HALF), ROWS), :] = part.astype(BF16)
            level_ref[entry] = level

    @pl.loop(0, found >> 1)
    def _(two):
        work([2 * two, 2 * two + 1])

    @pl.when((found & 1) == 1)
    def _():
        work([found - 1])

    for pair in range(entries // 2):
        start = pair * PAIR + 2 * BODY
        out_ref[start : start + HALF, :] = pack_stats(level_ref[2 * pair] + level_ref[2 * pair + 1])


def items(place, owners, kv_cache, payloads, slots, visitors):
    count = sum(len(row) for row in slots)
    return pl.pallas_call(
        functools.partial(item_kernel, slots, visitors, owners),
        out_shape=jax.ShapeDtypeStruct((count // 2 * PAIR, HD), BF16),
        in_specs=[IN_SMEM] + [IN_VMEM] * (1 + len(slots)),
        out_specs=IN_VMEM,
        scratch_shapes=[
            pltpu.VMEM((count * BODY, HD), BF16),
            pltpu.VMEM((count, HALF, LANES), F32),
            pltpu.SMEM((count,), jnp.int32),
            pltpu.SMEM((count + 1,), jnp.int32),
        ],
        compiler_params=params(),
        cost_estimate=cost(count * KVH * 4 * ROWS * HD * PAGE, count * PAGE * kv_cache.shape[2] * 2),
    )(place, kv_cache, *payloads)


def blend(levels):
    peak = functools.reduce(jnp.maximum, levels)
    shares = [jnp.exp2(level - peak) for level in levels]
    total = functools.reduce(jnp.add, shares)
    return [share / total for share in shares], peak + jnp.log2(total)


def mix(shares, refs, start, first_lane):
    values = []
    for index in range(COLS):
        row, lane = start + tile_start(index), first_lane + index
        tiles = [ref[row : row + HALF, :].astype(F32) for ref in refs]
        total = tiles[0]
        for share, tile in zip(shares[1:], tiles[1:]):
            total = total + share[:, lane : lane + 1] * (tile - tiles[0])
        values.append(total)
    return values


def merge_kernel(first, arrived_ref, own_ref, out_ref):
    for pair in range(out_ref.shape[0] // PAIR):
        part = slice(pair * PAIR, (pair + 1) * PAIR)
        arrived, own, out = arrived_ref.at[part], own_ref.at[first + pair * PAIR : first + (pair + 1) * PAIR], out_ref.at[part]
        shares, level = blend([unpack_stats(ref[2 * BODY : PAIR, :]) for ref in (arrived, own)])
        values = [mix(shares, (arrived, own), second * BODY, second * SECOND) for second in range(2)]
        for second in range(2):
            for index in range(COLS):
                row = second * BODY + tile_start(index)
                out[row : row + HALF, :] = values[second][index].astype(BF16)
        out[2 * BODY : PAIR, :] = pack_stats(level)


def merge(arrived, own):
    own, first = own
    return pl.pallas_call(
        functools.partial(merge_kernel, first),
        out_shape=jax.ShapeDtypeStruct(arrived.shape, BF16),
        in_specs=[IN_VMEM, IN_VMEM],
        out_specs=IN_VMEM,
        compiler_params=params(),
        cost_estimate=cost(0, 6 * arrived.size),
    )(arrived, own)


def split_kernel(firsts, *refs):
    arrays, outs = refs[: len(firsts)], refs[len(firsts) :]
    for pair in range(len(outs) // 2):
        start = pair * PAIR
        sources = [ref.at[first + start : first + start + PAIR] for ref, first in zip(arrays, firsts)]
        shares, level = blend([unpack_stats(ref[2 * BODY : PAIR, :]) for ref in sources])
        values = [mix(shares, sources, second * BODY, second * SECOND) for second in range(2)]
        for second in range(2):
            out = outs[2 * pair + second]
            for index in range(COLS):
                row = tile_start(index)
                out[row : row + HALF, :] = values[second][index].astype(BF16)
            here = pltpu.roll(level, LANES - SECOND, 1) if second else level
            out[BODY:LONE, :] = pack_stats(here)


def split(sources, requests):
    return pl.pallas_call(
        functools.partial(split_kernel, [first for _, first in sources]),
        out_shape=[jax.ShapeDtypeStruct((LONE, HD), BF16)] * requests,
        in_specs=[IN_VMEM] * len(sources),
        out_specs=[IN_VMEM] * requests,
        compiler_params=params(),
        cost_estimate=cost(0, 6 * requests * LONE * HD),
    )(*[array for array, _ in sources])


def final_kernel(first, early, owners, place_ref, *refs):
    earlier, parts = refs[:early], refs[early:-4]
    new_ref, level_ref, out_ref, rows_ref = refs[-4:]
    group = lax.div(place_ref[0], owners)
    count = len(parts) // 2
    for number in range(count):
        d = first + number
        both = (parts[2 * number], parts[2 * number + 1])
        shares, _ = blend([unpack_stats(part[BODY:LONE, :]) for part in both] + [level_ref[d]])
        for index, tile in enumerate(mix(shares, both + (new_ref.at[d],), 0, 0)):
            row = tile_start(index)
            rows_ref[number, row : row + HALF, :] = tile
    for number in range(count):
        row = group ^ (first + number) if early else number
        for head in range(KVH * GQ):
            tile = rows_ref[number, head * STEPS : (head + 1) * STEPS, :]
            out_ref[row, :, head * HD : (head + 1) * HD] = tile.astype(BF16)
    for ref in earlier:
        for number in range(ref.shape[0]):
            out_ref[group ^ (count + number)] = ref[number]


def final(place, owners, parts, first, new_out, new_level, earlier=()):
    count = len(parts) // 2
    requests = count + sum(e.shape[0] for e in earlier)
    return pl.pallas_call(
        functools.partial(final_kernel, first, len(earlier), owners),
        out_shape=jax.ShapeDtypeStruct((requests, STEPS, KVH * GQ * HD), BF16),
        in_specs=[IN_SMEM] + [IN_VMEM] * (len(earlier) + len(parts) + 2),
        out_specs=IN_VMEM,
        scratch_shapes=[pltpu.VMEM((count, BODY, HD), F32)],
        compiler_params=params(),
        cost_estimate=cost(0, count * BODY * HD * 10),
    )(place, *earlier, *parts, new_out, new_level)


def ring_order(owners):
    return list(range(0, owners, 2)) + list(range(owners - 1, 0, -2))


def per_device(queries, new_kv, kv_cache, page_owner, page_index, lengths):
    groups = lax.axis_size("grp")
    owners = lax.axis_size("cache")
    requests = queries.shape[0]
    assert requests == groups and requests % 4 == 0 and owners <= LANES
    reach = owners // 2
    order = ring_order(owners)
    forward = [(order[i], order[(i + 1) % owners]) for i in range(owners)]
    backward = [(b, a) for a, b in forward]
    place = jnp.reshape(lax.axis_index(("grp", "cache")), (1,)).astype(jnp.int32)

    def swap(array, d):
        return lax.ppermute(array, "grp", [(g, g ^ d) for g in range(groups)]) if d else array

    rows = relayout(place, owners, queries)
    visits = [rows[0]] + [None] * (groups - 1)
    for d in range(groups - 1, 0, -1):
        visits[d] = swap(rows[d], d)
    lists = page_lists(page_owner, page_index, lengths)

    cut = requests // 2
    slots = [list(range(cut)), list(range(cut, requests))]
    owned = functools.partial(items, place, owners, kv_cache, visitors=requests)

    def up(array):
        return lax.ppermute(array, "cache", forward)

    def down(array):
        return lax.ppermute(array, "cache", backward)

    def after(array, *others):
        return lax.optimization_barrier((array, others))[0]

    blocks = [payload(lists, visits[:cut])]
    blocks.append(payload(lists, visits[cut:], [touch(kv_cache, blocks[0])]))
    below, above = [up(block) for block in blocks], [down(block) for block in blocks]
    size = cut // 2 * PAIR
    both = owned(blocks, slots)
    parts = {(0, 0): (both, 0), (1, 0): (both, size)}
    new_out, new_level = new_tokens(place, owners, [after(rows[0], both), *rows[1:]], new_kv)
    done = [[both], [both, new_level]]
    for step in range(1, reach):
        for half in range(2):
            if step > 1:
                below[half], above[half] = up(below[half]), down(above[half])
            below[half], above[half] = after(below[half], *done[half]), after(above[half], *done[half])
            both = owned([below[half], above[half]], [slots[half]] * 2)
            parts[half, -step], parts[half, step] = (both, 0), (both, size)
            done[half] = [both]
    far = owned([up(below[0])], slots[:1]), owned([down(above[1])], slots[1:])

    def straight(array, ring, d):
        pairs = [(g * owners + a, (g ^ d) * owners + b) for g in range(groups) for a, b in ring]
        return lax.ppermute(array, ("grp", "cache"), pairs)

    home = [None] * requests
    for half in range(2):
        move, ring, sign = ((up, forward, 1), (down, backward, -1))[half]
        chain = far[half]
        for step in range(reach - 1, 1, -1):
            chain = merge(move(chain), parts[half, sign * step])
        long = split([(move(chain), 0), parts[half, sign]], cut)
        move, sign = ((down, -1), (up, 1))[half]
        own, first = parts[half, sign * (reach - 1)]
        chain = move(own[first : first + size])
        for step in range(reach - 2, 0, -1):
            chain = move(merge(chain, parts[half, sign * step]))
        short = split([parts[half, 0], (chain, 0)], cut)
        for number, d in enumerate(slots[half]):
            home[d] = [swap(short[number], d), straight(long[number], ring, d)]
    early = final(place, owners, sum(home[cut:], []), cut, new_out, new_level)
    return final(place, owners, sum(home[:cut], []), 0, new_out, new_level, [early])


def solution(mesh):
    in_specs = (
        P(("grp", "cache"), None, None),
        P(("grp", "cache"), None, None),
        P(("grp", "cache"), None, None),
        P(("grp", "cache"), None),
        P(("grp", "cache"), None, None),
        P(("grp", "cache")),
    )
    out_specs = P(("grp", "cache"), None, None)
    return jax.shard_map(
        per_device, mesh=mesh, in_specs=in_specs, out_specs=out_specs, check_vma=False
    )
```
